256 devices in a mesh: dp: 32 (over z, y), seq: 8 (over x, core).
Axes of the slice: x: 4, y: 4, z: 8, core: 2. Of those that a mesh axis runs over, the one named last changes fastest.
Arguments:
- qkv_time: bfloat16 [3, 32, 8, 128, 1536], P(None, 'dp', 'seq'), may hold values from -6 to 6
- shard_sizes: int32 [32, 8], P('dp'), may hold values from 1 to 32, 128 in all within a row
- bias_time: float32 [12, 15], replicated, may hold values from -4 to 4
- w_out: bfloat16 [1536, 1536], P(('dp', 'seq')), may hold values from -0.15625 to 0.15625
- cot_out: bfloat16 [32, 8, 8, 32, 1536], P('dp', 'seq'), may hold values from -17 to 17
Outputs:
- grad_qkv_time: bfloat16 [3, 32, 8, 128, 1536], P(None, 'dp', 'seq')
- grad_bias_time: float32 [12, 15], replicated
- grad_w_out: float32 [1536, 1536], P(('dp', 'seq'))
The draws below stay inside these ranges and needn't reach their ends.
Inputs may be any that keep to these rules, and one draw needn't show every extreme that they name: `shard_sizes`: each clip's 8 sizes sum to 128 and the largest is exactly 32; seq device j holds the positions that follow the first j shards.
All inputs are finite; a program needn't handle non-finite values.
Results may differ from the reference program's by a relative error of at most 0.0058.
Values may be sent and summed in bfloat16 or wider, within the bound.
No kernel may reach another device: no remote copies, remote signals or barrier semaphores. Data moves between devices by JAX's collectives and lax.ppermute only.
A program may use at most 128 MiB of HBM per device.

```python
import math
import jax
import jax.numpy as jnp
import numpy as np
from jax import lax

H = 12
HEAD = 128
DW = 1536
SPATIAL = 128
HD = 1536
FRAMES = 8
CLIPS = 32
CAP = 32
N_SEQ = 8


def rising(count):
    return jnp.arange(count, dtype=jnp.float32) / (count - 1)


def draw_qkv_time(key, part):
    key = jax.random.fold_in(key, 7)
    full_shape = (3, CLIPS, FRAMES, SPATIAL, H * HEAD)
    return jnp.clip(jax.random.normal(key, full_shape, jnp.float32), -6.0, 6.0).astype(jnp.bfloat16)


def draw_cot_out(key, part):
    key = jax.random.fold_in(key, 33)
    full_shape = (CLIPS, N_SEQ, FRAMES, CAP, DW)
    ladder = rising(CLIPS * N_SEQ).reshape(CLIPS, N_SEQ, 1, 1, 1)
    noise_part = jnp.clip(jax.random.normal(key, full_shape, jnp.float32), -4.0, 4.0)
    return ((1.0 + 2.0 * ladder) * noise_part).astype(jnp.bfloat16)


def levels(key, dims, cuts, smallest, top_value):
    factor_of = 1.0
    for dim, blocks in cuts:
        steps = jax.random.uniform(jax.random.fold_in(jax.random.fold_in(key, 6), dim), (blocks,), jnp.float32, smallest / len(cuts), top_value / len(cuts))
        factor_of = factor_of * jnp.repeat(jnp.exp(steps), dims[dim] // blocks).reshape((-1,) + (1,) * (len(dims) - 1 - dim))
    return factor_of


def profile(amount, total, most, slope):
    loads = [(1 << 20) // math.isqrt(rank ** slope) + 1 for rank in range(2, amount + 1)]
    spare, given = total - most - (amount - 1), [1] * (amount - 1)
    while spare > 0:
        free = [i for i in range(amount - 1) if given[i] < most]
        mass, left = sum([loads[i] for i in free]), spare
        for i in free:
            extra = min(most - given[i], max(1, left * loads[i] // mass), spare)
            given[i] = given[i] + extra
            spare = spare - extra
    return np.array([most] + given)


def ragged_sizes(key, amount, total, bound, skew):
    if amount == 2:
        one = jax.random.randint(key, (), max(1, total - bound), min(bound, total - 1) + 1)
        return jnp.stack([one, total - one])
    tallies = jnp.asarray(profile(amount, total, bound, skew), jnp.int32)
    pairs = (amount - 1) // 2
    source_of, sink = tallies[1:1 + 2 * pairs:2], tallies[2:2 + 2 * pairs:2]
    slack = jnp.minimum(source_of - 1, bound - sink)
    moved = jax.random.randint(jax.random.fold_in(key, 1), (pairs,), 0, 1 << 20) % (slack + 1)
    tallies = tallies.at[1:1 + 2 * pairs:2].set(source_of - moved).at[2:2 + 2 * pairs:2].set(sink + moved)
    return tallies[jax.random.permutation(jax.random.fold_in(key, 2), amount)]


def centred(own_key, dims, scale, limit, pieces=(), held_as=jnp.bfloat16):
    level = levels(own_key, dims, pieces, -0.22, 0.18) if pieces else 1.0
    entries = jax.random.normal(own_key, dims, jnp.float32) * scale * level
    return jnp.minimum(jnp.maximum(entries, -limit), limit).astype(held_as)


def setup_inputs(seed: int = 0) -> dict:
    key_list = jax.random.split(jax.random.key(seed), 6)
    qkv_time = draw_qkv_time(jax.random.fold_in(key_list[5], 71), 0)
    shard_sizes = jax.vmap(lambda own: ragged_sizes(own, N_SEQ, SPATIAL, CAP, 2))(jax.random.split(key_list[1], CLIPS)).reshape((CLIPS, N_SEQ)).astype(jnp.int32)
    bias_time = centred(key_list[2], (H, 2 * FRAMES - 1), 1.0, 4.0, (), jnp.float32)
    w_out = centred(key_list[3], (HD, DW), HD ** -0.5, 0.15625, ((0, 256),))
    cot_out = draw_cot_out(jax.random.fold_in(key_list[5], 71), 0)
    return dict(qkv_time=qkv_time, shard_sizes=shard_sizes, bias_time=bias_time, w_out=w_out, cot_out=cot_out)


def offset_table(count):
    index_row = jnp.arange(count, dtype=jnp.int32)
    shifted = index_row[None, :] - index_row[:, None] + count - 1
    labels = jnp.arange(2 * count - 1, dtype=jnp.int32)
    return (shifted[None, :, :] == labels[:, None, None]).astype(jnp.float32)

def rounded(values):
    return lax.optimization_barrier(values.astype(jnp.bfloat16)).astype(jnp.float32)

def normalize(scores):
    row_top = lax.optimization_barrier(jnp.max(scores, axis=-1, keepdims=True))
    weights = jnp.exp(scores - row_top)
    return weights / lax.optimization_barrier(jnp.sum(weights, axis=-1, keepdims=True))

def time_forward(queries, keys_in, values, pair_bias):
    frame_n, length, width = queries.shape
    heads_n = pair_bias.shape[0]
    head_len = width // heads_n
    factor = 1.0 / math.sqrt(head_len)
    q_heads = queries.reshape(frame_n, length, heads_n, head_len).astype(jnp.float32)
    k_heads = keys_in.reshape(frame_n, length, heads_n, head_len).astype(jnp.float32)
    v_heads = values.reshape(frame_n, length, heads_n, head_len).astype(jnp.float32)
    scores = jnp.einsum('fshd,gshd->shfg', q_heads, k_heads) * factor + pair_bias[None]
    probs_full = normalize(scores)
    probs_low = rounded(probs_full)
    mixed = jnp.einsum('shfg,gshd->fshd', probs_low, v_heads).reshape(frame_n, length, width).astype(jnp.bfloat16)
    return (probs_full, probs_low, mixed)

def time_backward(queries, keys_in, values, d_mixed, probs_full, probs_low):
    frame_n, length, width = queries.shape
    heads_n = probs_full.shape[1]
    head_len = width // heads_n
    factor = 1.0 / math.sqrt(head_len)
    q_heads = queries.reshape(frame_n, length, heads_n, head_len).astype(jnp.float32)
    k_heads = keys_in.reshape(frame_n, length, heads_n, head_len).astype(jnp.float32)
    v_heads = values.reshape(frame_n, length, heads_n, head_len).astype(jnp.float32)
    d_heads = d_mixed.reshape(frame_n, length, heads_n, head_len).astype(jnp.float32)
    grad_v = jnp.einsum('shfg,fshd->gshd', probs_low, d_heads)
    grad_p = jnp.einsum('fshd,gshd->shfg', d_heads, v_heads)
    grad_s = probs_full * (grad_p - lax.optimization_barrier(jnp.sum(probs_full * grad_p, axis=-1, keepdims=True)))
    grad_low = rounded(grad_s)
    grad_q = jnp.einsum('shfg,gshd->fshd', grad_low, k_heads) * factor
    grad_k = jnp.einsum('shfg,fshd->gshd', grad_low, q_heads) * factor
    grads = jnp.stack([grad_q, grad_k, grad_v]).reshape(3, frame_n, length, width).astype(jnp.bfloat16)
    return (grads, lax.optimization_barrier(jnp.sum(grad_s, axis=0)))

def position_slots(counts):
    starts = (jnp.cumsum(counts) - counts).astype(jnp.int32)
    position = jnp.arange(SPATIAL, dtype=jnp.int32)
    inside = (position[:, None] >= starts[None, :]) & (position[:, None] < (starts + counts)[None, :])
    owners = lax.optimization_barrier(jnp.sum(jnp.where(inside, jnp.arange(N_SEQ, dtype=jnp.int32)[None, :], 0), axis=1))
    first_pos = lax.optimization_barrier(jnp.sum(jnp.where(inside, starts[None, :], 0), axis=1))
    return (owners * CAP + position - first_pos).astype(jnp.int32)

def reference(qkv_time, shard_sizes, bias_time, w_out, cot_out):
    time_table = offset_table(FRAMES)
    pair_bias = jnp.einsum('ho,ofg->hfg', bias_time, time_table, precision=lax.Precision.HIGHEST)

    def one_clip(carry, clip_id):
        grad_w, pair_total = carry
        slot_index = position_slots(shard_sizes[clip_id])
        clip_qkv = qkv_time[:, clip_id]
        cot_rows = jnp.transpose(cot_out[clip_id], (1, 0, 2, 3)).reshape(FRAMES, N_SEQ * CAP, DW)
        upstream = jnp.take(cot_rows, slot_index, axis=1)
        probs_full, probs_low, mixed = time_forward(clip_qkv[0], clip_qkv[1], clip_qkv[2], pair_bias)
        mixed_rows = mixed.reshape(FRAMES * SPATIAL, HD)
        up_rows = upstream.reshape(FRAMES * SPATIAL, DW)
        d_mixed = jnp.dot(up_rows, w_out.T, preferred_element_type=jnp.float32).astype(jnp.bfloat16)
        d_mixed = d_mixed.reshape(FRAMES, SPATIAL, HD)
        grad_w = grad_w + jnp.dot(mixed_rows.T, up_rows, preferred_element_type=jnp.float32)
        grads, pair_sums = time_backward(clip_qkv[0], clip_qkv[1], clip_qkv[2], d_mixed, probs_full, probs_low)
        return ((grad_w, pair_total + pair_sums), grads)
    start_carry = (jnp.zeros((HD, DW), jnp.float32), jnp.zeros((H, FRAMES, FRAMES), jnp.float32))
    (grad_w_out, pair_total), time_grads = lax.scan(one_clip, start_carry, jnp.arange(CLIPS, dtype=jnp.int32))
    grad_qkv_time = jnp.transpose(time_grads, (1, 0, 2, 3, 4))
    grad_bias_time = jnp.einsum('hfg,ofg->ho', pair_total, time_table, precision=lax.Precision.HIGHEST)
    return (grad_qkv_time, grad_bias_time, grad_w_out)
```

```python
import math

import jax
import jax.numpy as jnp
from jax import lax
from jax.experimental import pallas as pl
from jax.experimental.pallas import tpu as pltpu
from jax.sharding import Mesh, PartitionSpec as P

Z, Y, X, C = 8, 4, 4, 2
SEQ = ("x", "core")
F = 8
POS = 128
HALF = 64
NB = 4
HL = 3
HD = 128
COLS = HL * HD
DW = 1536
CAP = 32
FACTOR = 1.0 / math.sqrt(HD)
NT = (((1,), (1,)), ((), ()))
TN = (((0,), (0,)), ((), ()))


def dot(a, b, dims):
    return lax.dot_general(a, b, dims, preferred_element_type=jnp.float32)


def fwd_kernel(qkv_ref, bias_ref, probs_ref, mixed_ref):
    for h in range(HL):
        cols = slice(h * HD, (h + 1) * HD)
        for b in range(NB):
            rows = slice(b * 16, (b + 1) * 16)
            q = qkv_ref[:, 0, rows, cols].reshape(POS, HD)
            k = qkv_ref[:, 1, rows, cols].reshape(POS, HD)
            v = qkv_ref[:, 2, rows, cols].reshape(POS, HD)
            s = dot(q, k, NT) * FACTOR + bias_ref[h]
            e = jnp.exp(s - jnp.max(s, axis=-1, keepdims=True))
            p = e / jnp.sum(e, axis=-1, keepdims=True)
            probs_ref[h, b] = p
            m = dot(p.astype(jnp.bfloat16), v, (((1,), (0,)), ((), ())))
            mixed_ref[:, rows, cols] = m.astype(jnp.bfloat16).reshape(F, 16, HD)


def bwd_kernel(qkv_ref, probs_ref, up_ref, w_ref, grads_ref, pair_ref, dm_ref):
    up = up_ref[...].reshape(F * HALF, DW)
    dm = dot(up, w_ref[...], NT)
    dm_ref[...] = dm.astype(jnp.bfloat16).reshape(F, HALF, COLS)
    for h in range(HL):
        cols = slice(h * HD, (h + 1) * HD)
        total = jnp.zeros((F, POS), jnp.float32)
        for b in range(NB):
            rows = slice(b * 16, (b + 1) * 16)
            q = qkv_ref[:, 0, rows, cols].reshape(POS, HD)
            k = qkv_ref[:, 1, rows, cols].reshape(POS, HD)
            v = qkv_ref[:, 2, rows, cols].reshape(POS, HD)
            d = dm_ref[:, rows, cols].reshape(POS, HD)
            p = probs_ref[h, b]
            g = dot(d, v, NT)
            ds = p * (g - jnp.sum(p * g, axis=-1, keepdims=True))
            total = total + jnp.sum(ds.reshape(F, 16, POS), axis=1)
            low = ds.astype(jnp.bfloat16)
            gq = dot(low, k, (((1,), (0,)), ((), ()))) * FACTOR
            gk = dot(low, q, TN) * FACTOR
            gv = dot(p.astype(jnp.bfloat16), d, TN)
            for i, val in enumerate((gq, gk, gv)):
                grads_ref[:, i, rows, cols] = val.astype(jnp.bfloat16).reshape(F, 16, HD)
        pair_ref[h] = total


def hop(x, axis, k, n):
    return lax.ppermute(x, axis, [(i, i ^ k) for i in range(n)])


def per_device(qkv_time, shard_sizes, bias_time, w_out, cot_out):
    bf, f32 = jnp.bfloat16, jnp.float32
    xi = lax.axis_index("x")
    core = lax.axis_index("core")

    cot = lax.all_to_all(cot_out[0, 0], SEQ, 0, 0, tiled=True).reshape(F * CAP, DW)

    packed = qkv_time[:, 0, 0].reshape(3, C, HALF, X, COLS).transpose(3, 1, 0, 2, 4)
    qkv = lax.all_to_all(packed.reshape(F, 3, HALF, COLS), SEQ, 0, 0, tiled=True)

    there = [
        ((2 * c + z0) * X + x, (z0 * X + x) * X + c)
        for c in range(X)
        for z0 in range(2)
        for x in range(X)
    ]
    w8 = jnp.pad(w_out, ((0, 2), (0, 0)))
    w8 = lax.ppermute(w8, ("z", "x"), there)
    wz = lax.all_to_all(jnp.broadcast_to(w8, (Z, 8, DW)), "z", 0, 0, tiled=True)
    wy = lax.all_to_all(jnp.broadcast_to(wz.reshape(64, DW), (Y, 64, DW)), "y", 0, 0, tiled=True)
    wo = hop(wy, "core", 1, C)
    held = jnp.concatenate([wy, wo]).reshape(2 * Y * 64, DW)
    r = lax.broadcasted_iota(jnp.int32, (COLS, 512), 0)
    t = lax.broadcasted_iota(jnp.int32, (COLS, 512), 1)
    i, sub = r % 6, r // 6
    rz0, ry, rx, rc = sub // 32, (sub // 8) % 4, (sub // 2) % 4, sub % 2
    spot = (((rc ^ core) * 4 + ry) * 8 + rz0 * 4 + rx) * 8 + i
    w_c = dot((spot == t).astype(bf), held, (((1,), (0,)), ((), ()))).astype(bf)

    counts = shard_sizes[0]
    starts = jnp.cumsum(counts) - counts
    slot = lax.broadcasted_iota(jnp.int32, (POS, F, CAP), 2)
    pos = lax.broadcasted_iota(jnp.int32, (POS, F, CAP), 0)
    pick = (slot < counts[None, :, None]) & (starts[None, :, None] + slot == pos)
    up = dot(pick.reshape(POS, F * CAP).astype(bf), cot, (((1,), (0,)), ((), ()))).astype(bf)
    up = jnp.broadcast_to(up.reshape(1, C, HALF, DW), (X, C, HALF, DW)).reshape(F, HALF, DW)
    up = lax.all_to_all(up, SEQ, 0, 0, tiled=True)

    local_bias = lax.dynamic_slice(bias_time, (xi * HL, 0), (HL, 15))
    pair = jnp.stack([local_bias[:, 7 - f : 15 - f] for f in range(F)], axis=1)
    same = jnp.eye(16, dtype=jnp.bool_)[None, None, :, None, :]
    bias_m = jnp.where(same, pair[:, :, None, :, None], f32(-1e30)).reshape(HL, POS, POS)
    probs, mixed = pl.pallas_call(
        fwd_kernel,
        out_shape=(
            jax.ShapeDtypeStruct((HL, NB, POS, POS), f32),
            jax.ShapeDtypeStruct((F, HALF, COLS), bf),
        ),
        compiler_params=pltpu.CompilerParams(vmem_limit_bytes=32 << 20),
        cost_estimate=pl.CostEstimate(flops=200_000_000, bytes_accessed=4_000_000, transcendentals=200_000),
        name="attn_fwd",
    )(qkv, bias_m)

    mixed_rows = mixed.reshape(F * HALF, COLS)
    q2 = lax.broadcasted_iota(jnp.int32, (COLS, COLS), 1)
    r2 = lax.broadcasted_iota(jnp.int32, (COLS, COLS), 0)
    i2, sub2 = q2 % 6, q2 // 6
    qc, qy, qz0, qx = sub2 // 32, (sub2 // 8) % 4, (sub2 // 4) % 2, sub2 % 4
    src = ((((qz0 * 4 + qy) * 4 + qx) * 2) + qc) * 6 + i2
    mixed_p = dot(mixed_rows, (src == r2).astype(bf), (((1,), (0,)), ((), ()))).astype(bf)
    up_rows = up.reshape(F * HALF, DW)
    gw = dot(mixed_p, up_rows, TN)
    half = COLS // 2
    mine = lax.dynamic_slice(gw, (core * half, 0), (half, DW))
    other = lax.dynamic_slice(gw, ((1 - core) * half, 0), (half, DW))
    gw = mine + hop(other, "core", 1, C)
    gw = gw.reshape(Y, 48, DW).astype(bf)
    gw = jnp.sum(lax.all_to_all(gw, "y", 0, 0, tiled=True).astype(f32), axis=0)
    gw = jnp.pad(gw.reshape(Z, 6, DW), ((0, 0), (0, 2), (0, 0)))
    gw = jnp.sum(lax.all_to_all(gw, "z", 0, 0, tiled=True), axis=0)
    grad_w_out = lax.ppermute(gw, ("z", "x"), [(b, a) for a, b in there])[:6]

    grads, pairs = pl.pallas_call(
        bwd_kernel,
        out_shape=(
            jax.ShapeDtypeStruct((F, 3, HALF, COLS), bf),
            jax.ShapeDtypeStruct((HL, F, POS), f32),
        ),
        scratch_shapes=[pltpu.VMEM((F, HALF, COLS), bf)],
        compiler_params=pltpu.CompilerParams(vmem_limit_bytes=32 << 20),
        cost_estimate=pl.CostEstimate(flops=900_000_000, bytes_accessed=6_000_000, transcendentals=0),
        name="attn_bwd",
    )(qkv, probs, up, w_c)
    back = lax.all_to_all(grads, SEQ, 0, 0, tiled=True).reshape(X, C, 3, HALF, COLS)
    grad_qkv = back.transpose(2, 1, 3, 0, 4).reshape(3, 1, 1, POS, DW)

    pairs = pairs.reshape(HL, F, F, 16).sum(axis=-1)
    offs = jnp.stack([jnp.pad(pairs[:, f], ((0, 0), (7 - f, f))) for f in range(F)]).sum(axis=0)
    offs = lax.dynamic_update_slice(jnp.zeros((16, 128), f32), jnp.pad(offs, ((0, 0), (0, 113))), (xi * HL, 0))
    for axis, n in (("core", C), ("x", X), ("y", Y), ("z", Z)):
        k = 1
        while k < n:
            offs = offs + hop(offs, axis, k, n)
            k *= 2
    return grad_qkv, offs[:12, :15], grad_w_out


def solution(mesh):
    grid = Mesh(mesh.devices.reshape(Z, Y, X, C), ("z", "y", "x", "core"))
    dp, every = ("z", "y"), ("z", "y", "x", "core")
    return jax.shard_map(
        per_device,
        mesh=grid,
        in_specs=(
            P(None, dp, SEQ, None, None),
            P(dp, None),
            P(),
            P(every, None),
            P(dp, SEQ, None, None, None),
        ),
        out_specs=(P(None, dp, SEQ, None, None), P(), P(every, None)),
        check_vma=False,
    )
```

```python
import functools
import math

import jax
import jax.numpy as jnp
from jax import lax
from jax.experimental import pallas as pl
from jax.experimental.pallas import tpu as pltpu
from jax.sharding import Mesh, PartitionSpec as P

Z, Y, X, C = 8, 4, 4, 2
SEQ = ("x", "core")
F = 8
POS = 128
HALF = 64
NB = 4
HL = 3
HD = 128
COLS = HL * HD
DW = 1536
CAP = 32
FACTOR = 1.0 / math.sqrt(HD)
NN = (((1,), (0,)), ((), ()))
NT = (((1,), (1,)), ((), ()))
TN = (((0,), (0,)), ((), ()))
bf, f32 = jnp.bfloat16, jnp.float32
CORE, YI, ZI, RANK = 0, 1, 2, 3


def dot(a, b, dims, **kw):
    return lax.dot_general(a, b, dims, preferred_element_type=f32, **kw)


def iota(shape, dim):
    return lax.broadcasted_iota(jnp.int32, shape, dim)


def call(body, name, outs, *ins, smem=0, scratch=(), flops=0):
    total = sum(math.prod(s) * jnp.dtype(d).itemsize for s, d in outs)
    total += sum(a.size * a.dtype.itemsize for a in ins)
    specs = [pl.BlockSpec(memory_space=pltpu.SMEM)] * smem
    specs += [pl.BlockSpec(memory_space=pltpu.VMEM)] * (len(ins) - smem)
    return pl.pallas_call(
        body,
        out_shape=tuple(jax.ShapeDtypeStruct(s, d) for s, d in outs),
        in_specs=specs,
        out_specs=tuple(pl.BlockSpec(memory_space=pltpu.VMEM) for _ in outs),
        scratch_shapes=list(scratch),
        compiler_params=pltpu.CompilerParams(vmem_limit_bytes=32 << 20),
        cost_estimate=pl.CostEstimate(flops=flops, bytes_accessed=total, transcendentals=0),
        name=name,
    )(*ins)


def compact_kernel(place, sizes, cot_ref, same_ref, other_ref):
    shape = (POS, F * CAP)
    row, col = iota(shape, 0), iota(shape, 1)
    pos = row ^ (place[CORE] * HALF)
    start = jnp.int32(0)
    picked = jnp.full(shape, -1, jnp.int32)
    for j in range(F):
        slot = col - j * CAP
        inside = (slot >= 0) & (slot < sizes[0, j])
        picked = jnp.where(inside, slot + start, picked)
        start = start + sizes[0, j]
    hot = (picked == pos).astype(f32).astype(bf)
    up = dot(hot, cot_ref[...].reshape(F * CAP, DW), NN).astype(bf)
    same_ref[...] = up[:HALF]
    other_ref[...] = up[HALF:]


def block(ref, i, b, h):
    return ref[:, i, b * 16 : (b + 1) * 16, h * HD : (h + 1) * HD].reshape(POS, HD)


def fwd_kernel(qkv_ref, bias_ref, order_ref, probs_ref, mixed_ref, raw_ref):
    for h in range(HL):
        for b in range(NB):
            q, k, v = (block(qkv_ref, i, b, h) for i in range(3))
            s = dot(q, k, NT) * FACTOR + bias_ref[h]
            e = jnp.exp(s - jnp.max(s, axis=-1, keepdims=True))
            p = e / jnp.sum(e, axis=-1, keepdims=True)
            probs_ref[h, b] = p
            m = dot(p.astype(bf), v, NN).astype(bf).reshape(F, 16, HD)
            raw_ref[:, b * 16 : (b + 1) * 16, h * HD : (h + 1) * HD] = m
    mixed_ref[...] = dot(raw_ref[...].reshape(F * HALF, COLS), order_ref[...], NN).astype(bf)


def gw_kernel(place, *refs):
    pieces, mixed_ref, up_ref, mine_ref, other_ref = refs[:F], *refs[F:]
    for k in range(F):
        up_ref[place[RANK] ^ k] = pieces[k][...]
    up = up_ref[...].reshape(F * HALF, DW)
    gw = dot(mixed_ref[...], up, TN)
    mine_ref[...] = gw[: COLS // 2]
    other_ref[...] = gw[COLS // 2 :].astype(bf)


def score_kernel(qkv_ref, probs_ref, up_ref, w_ref, dm_ref, ds_ref, sums_ref):
    dm = dot(up_ref[...].reshape(F * HALF, DW), w_ref[...], NT)
    dm_ref[...] = dm.astype(bf).reshape(F, HALF, COLS)
    for h in range(HL):
        cols = slice(h * HD, (h + 1) * HD)
        total = jnp.zeros((F, POS), f32)
        for b in range(NB):
            d = dm_ref[:, b * 16 : (b + 1) * 16, cols].reshape(POS, HD)
            p = probs_ref[h, b]
            g = dot(d, block(qkv_ref, 2, b, h), NT)
            ds = p * (g - jnp.sum(p * g, axis=-1, keepdims=True))
            total = total + jnp.sum(ds.reshape(F, 16, POS), axis=1)
            ds_ref[h, b] = ds.astype(bf)
        sums_ref[:, cols] = total


def grad_kernel(qkv_ref, probs_ref, dm_ref, ds_ref, grads_ref):
    for h in range(HL):
        cols = slice(h * HD, (h + 1) * HD)
        for b in range(NB):
            rows = slice(b * 16, (b + 1) * 16)
            d = dm_ref[:, rows, cols].reshape(POS, HD)
            low = ds_ref[h, b]
            gq = dot(low, block(qkv_ref, 1, b, h), NN) * FACTOR
            gk = dot(low, block(qkv_ref, 0, b, h), TN) * FACTOR
            gv = dot(probs_ref[h, b].astype(bf), d, TN)
            for i, val in enumerate((gq, gk, gv)):
                grads_ref[:, i, rows, cols] = val.astype(bf).reshape(F, 16, HD)


def tiles(x):
    return jnp.concatenate([x[:, a * 128 : (a + 1) * 128] for a in range(HL)], axis=0)


def join_kernel(mine_ref, other_ref, sums_ref, sums2_ref, own_ref, b_ref, m1, m2, m3):
    gw = mine_ref[...] + other_ref[...].astype(f32)
    b = tiles(sums_ref[...] + sums2_ref[...])
    own_ref[...] = gw[:48]
    high = b.astype(bf).astype(f32)
    low = (b - high).astype(bf).astype(f32)
    b_ref[...] = high + low
    ride = jnp.concatenate([high, low], axis=0).astype(bf)
    for k, m in enumerate((m1, m2, m3), 1):
        m[:, :DW] = gw[48 * k : 48 * (k + 1)].astype(bf)
        m[:, DW:] = ride


def ysum_kernel(own_ref, b_ref, m1, m2, m3, keep_ref, send_ref):
    gw = [own_ref[...]] + [m[:, :DW].astype(f32) for m in (m1, m2, m3)]
    rides = [m[:, DW:].astype(f32) for m in (m1, m2, m3)]
    b = [b_ref[...]] + [x[:24] + x[24:] for x in rides]
    gw, b = ((x[0] + x[1]) + (x[2] + x[3]) for x in (gw, b))
    flat = jnp.concatenate([b[2 * a : 2 * a + 2] for a in range(12)], axis=1)
    for ref, part in ((keep_ref, gw[:24]), (send_ref, gw[24:])):
        ref[:24] = part
        ref[24:26] = flat
        ref[26:] = jnp.zeros((6, DW), f32)


def zsum_kernel(keep_ref, recv_ref, first_ref, second_ref):
    n = first_ref.shape[0]
    total = keep_ref[...] + recv_ref[...]
    rows = {16: 12, 8: 6}[n]
    for ref, part in ((first_ref, total[:rows]), (second_ref, total[rows : 2 * rows])):
        ref[:rows] = part
        ref[rows : rows + 2] = total[2 * rows : 2 * rows + 2]
        if n - rows > 2:
            ref[rows + 2 :] = jnp.zeros((n - rows - 2, DW), f32)


def last_kernel(a_ref, b_ref, gw_ref, off_ref):
    total = a_ref[...] + b_ref[...]
    gw_ref[...] = total[:6]
    flat = total[6:8]
    rows = [flat[:, 128 * a : 128 * (a + 1)] for a in range(12)]
    sums = jnp.concatenate(rows, axis=0)
    out = jnp.zeros((16, 128), f32)
    head = iota((16, 24), 0) % HL
    t = iota((16, 24), 1)
    g = iota((128, 128), 0) // 16
    o = iota((128, 128), 1)
    hi = lax.Precision.HIGHEST
    for f in range(F):
        pick = (t == head * F + f).astype(f32)
        row = dot(pick, sums, NN, precision=hi)
        out = out + dot(row, (g - f + 7 == o).astype(f32), NN, precision=hi)
    off_ref[...] = out


def bias_kernel(place, *refs):
    parts, out_ref = refs[:4], refs[4]
    row = iota((16, 128), 0) // HL
    out = jnp.zeros((16, 128), f32)
    for k in range(4):
        out = out + jnp.where(row == ((place[ZI] // 2) ^ k), parts[k][...], 0.0)
    out_ref[...] = out[:12, :15]


def hop(x, axis, k, n):
    return lax.ppermute(x, axis, [(i, i ^ k) for i in range(n)])


def per_device(qkv_time, shard_sizes, bias_time, w_out, cot_out):
    xi, yi, zi = (lax.axis_index(a) for a in ("x", "y", "z"))
    core = lax.axis_index("core")
    place = jnp.stack([core, yi, zi, xi * C + core]).astype(jnp.int32)

    there = [
        ((2 * c + z0) * X + x, (z0 * X + x) * X + c)
        for c in range(X)
        for z0 in range(2)
        for x in range(X)
    ]
    held = lax.ppermute(jnp.pad(w_out, ((0, 2), (0, 0))), ("z", "x"), there)
    for axis, n in (("z", Z), ("y", Y), ("core", C)):
        k = 1
        while k < n:
            held = jnp.concatenate([held, hop(held, axis, k, n)])
            k *= 2

    cot = lax.all_to_all(cot_out[0, 0], SEQ, 0, 0, tiled=True)
    packed = qkv_time[:, 0, 0].reshape(3, C, HALF, X, COLS).transpose(3, 1, 0, 2, 4)
    qkv = lax.all_to_all(packed.reshape(F, 3, HALF, COLS), SEQ, 0, 0, tiled=True)

    same, other = call(
        compact_kernel, "compact", [((HALF, DW), bf)] * 2, place, shard_sizes, cot, smem=2, flops=100_000_000
    )
    pieces = [same] + [hop(other if k & 1 else same, SEQ, k, F) for k in range(1, F)]

    r, t = iota((COLS, 512), 0), iota((COLS, 512), 1)
    i, sub = r % 6, r // 6
    rj, ry, rc = (sub // 32) * 4 + (sub // 2) % 4, (sub // 8) % 4, sub % 2
    spot = (((rc ^ core) * 4 + (ry ^ yi)) * 8 + (rj ^ zi)) * 8 + i
    w_c = dot((spot == t).astype(bf), held, NN).astype(bf)

    local_bias = lax.dynamic_slice(bias_time, (xi * HL, 0), (HL, 15))
    pair = jnp.stack([local_bias[:, 7 - f : 15 - f] for f in range(F)], axis=1)
    alike = jnp.eye(16, dtype=jnp.bool_)[None, None, :, None, :]
    bias_m = jnp.where(alike, pair[:, :, None, :, None], f32(-1e30)).reshape(HL, POS, POS)
    t2, r2 = iota((COLS, COLS), 1), iota((COLS, COLS), 0)
    j = (((t2 // 24) % 2) + ((t2 // 12) % 2) * 2 + ((t2 // 6) % 2) * 4) ^ zi
    oy, oc = ((t2 // 48) % 4) ^ yi, (t2 // 192) ^ core
    src = (((j // 4) * 4 + oy) * 8 + (j % 4) * 2 + oc) * 6 + t2 % 6
    order = (src == r2).astype(bf)
    probs, mixed = call(
        fwd_kernel,
        "attn_fwd",
        [((HL, NB, POS, POS), f32), ((F * HALF, COLS), bf)],
        qkv,
        bias_m,
        order,
        scratch=[pltpu.VMEM((F, HALF, COLS), bf)],
        flops=250_000_000,
    )

    up, mine, theirs = call(
        gw_kernel,
        "grad_w",
        [((F, HALF, DW), bf), ((COLS // 2, DW), f32), ((COLS // 2, DW), bf)],
        place,
        *pieces,
        mixed,
        smem=1,
        flops=604_000_000,
    )
    theirs = hop(theirs, "core", 1, C)

    dm, ds, sums = call(
        score_kernel,
        "scores_bwd",
        [((F, HALF, COLS), bf), ((HL, NB, POS, POS), bf), ((F, COLS), f32)],
        qkv,
        probs,
        up,
        w_c,
        flops=700_000_000,
    )
    sums2 = hop(sums, "core", 1, C)
    (grads,) = call(
        grad_kernel, "grads", [((F, 3, HALF, COLS), bf)], qkv, probs, dm, ds, flops=150_000_000
    )

    wide = ((48, DW + 128), bf)
    own, b, *msgs = call(
        join_kernel, "join", [((48, DW), f32), ((24, 128), f32), wide, wide, wide], mine, theirs, sums, sums2
    )
    msgs = [hop(m, "y", k, Y) for k, m in enumerate(msgs, 1)]
    keep, send = call(ysum_kernel, "ysum", [((32, DW), f32)] * 2, own, b, *msgs)
    keep, send = call(zsum_kernel, "zsum1", [((16, DW), f32)] * 2, keep, hop(send, "z", 1, Z))
    first, second = call(zsum_kernel, "zsum2", [((8, DW), f32)] * 2, keep, hop(send, "z", 2, Z))
    home = [(a, b) for b, a in there]
    cross = [((((a // X) ^ 4) * X + a % X), b) for a, b in home]
    first = lax.ppermute(first, ("z", "x"), home)
    second = lax.ppermute(second, ("z", "x"), cross)
    grad_w_out, off = call(last_kernel, "last", [((6, DW), f32), ((16, 128), f32)], first, second)
    offs = [off] + [hop(off, "z", 2 * k, Z) for k in range(1, 4)]
    (grad_bias,) = call(bias_kernel, "bias", [((12, 15), f32)], place, *offs, smem=1)

    back = lax.all_to_all(grads, SEQ, 0, 0, tiled=True).reshape(X, C, 3, HALF, COLS)
    grad_qkv = back.transpose(2, 1, 3, 0, 4).reshape(3, 1, 1, POS, DW)
    return grad_qkv, grad_bias, grad_w_out


def solution(mesh):
    grid = Mesh(mesh.devices.reshape(Z, Y, X, C), ("z", "y", "x", "core"))
    dp, every = ("z", "y"), ("z", "y", "x", "core")
    return jax.shard_map(
        per_device,
        mesh=grid,
        in_specs=(
            P(None, dp, SEQ, None, None),
            P(dp, None),
            P(),
            P(every, None),
            P(dp, SEQ, None, None, None),
        ),
        out_specs=(P(None, dp, SEQ, None, None), P(), P(every, None)),
        check_vma=False,
    )
```

```python
import functools
import math

import jax
import jax.numpy as jnp
from jax import lax
from jax.experimental import pallas as pl
from jax.experimental.pallas import tpu as pltpu
from jax.sharding import Mesh, PartitionSpec as P

Z, Y, X, C = 8, 4, 4, 2
SEQ = ("x", "core")
F = 8
POS = 128
HALF = 64
NB = 4
HL = 3
HD = 128
COLS = HL * HD
DW = 1536
CAP = 32
FACTOR = 1.0 / math.sqrt(HD)
NN = (((1,), (0,)), ((), ()))
NT = (((1,), (1,)), ((), ()))
TN = (((0,), (0,)), ((), ()))
bf, f32 = jnp.bfloat16, jnp.float32
CORE, YI, ZI, RANK = 0, 1, 2, 3


def dot(a, b, dims, **kw):
    return lax.dot_general(a, b, dims, preferred_element_type=f32, **kw)


def iota(shape, dim):
    return lax.broadcasted_iota(jnp.int32, shape, dim)


def call(body, name, outs, *ins, smem=0, hbm=0, scratch=(), flops=0):
    total = sum(math.prod(s) * jnp.dtype(d).itemsize for s, d in outs)
    total += sum(a.size * a.dtype.itemsize for a in ins)
    specs = [pl.BlockSpec(memory_space=pltpu.SMEM)] * smem
    specs += [pl.BlockSpec(memory_space=pl.ANY)] * hbm
    specs += [pl.BlockSpec(memory_space=pltpu.VMEM)] * (len(ins) - smem - hbm)
    return pl.pallas_call(
        body,
        out_shape=tuple(jax.ShapeDtypeStruct(s, d) for s, d in outs),
        in_specs=specs,
        out_specs=tuple(pl.BlockSpec(memory_space=pltpu.VMEM) for _ in outs),
        scratch_shapes=list(scratch),
        compiler_params=pltpu.CompilerParams(vmem_limit_bytes=32 << 20),
        cost_estimate=pl.CostEstimate(flops=flops, bytes_accessed=total, transcendentals=0),
        name=name,
    )(*ins)


def compact_kernel(place, sizes, cot_ref, same_ref, other_ref):
    shape = (POS, F * CAP)
    row, col = iota(shape, 0), iota(shape, 1)
    pos = row ^ (place[CORE] * HALF)
    start = jnp.int32(0)
    picked = jnp.full(shape, -1, jnp.int32)
    for j in range(F):
        slot = col - j * CAP
        inside = (slot >= 0) & (slot < sizes[0, j])
        picked = jnp.where(inside, slot + start, picked)
        start = start + sizes[0, j]
    hot = (picked == pos).astype(f32).astype(bf)
    up = dot(hot, cot_ref[...].reshape(F * CAP, DW), NN).astype(bf)
    same_ref[...] = up[:HALF]
    other_ref[...] = up[HALF:]


def block(ref, i, b, h):
    return ref[:, i, b * 16 : (b + 1) * 16, h * HD : (h + 1) * HD].reshape(POS, HD)


def fwd_kernel(qkv_ref, bias_ref, order_ref, probs_ref, mixed_ref, raw_ref):
    for h in range(HL):
        for b in range(NB):
            q, k, v = (block(qkv_ref, i, b, h) for i in range(3))
            s = dot(q, k, NT) * FACTOR + bias_ref[h]
            e = jnp.exp(s - jnp.max(s, axis=-1, keepdims=True))
            p = e / jnp.sum(e, axis=-1, keepdims=True)
            probs_ref[h, b] = p
            m = dot(p.astype(bf), v, NN).astype(bf).reshape(F, 16, HD)
            raw_ref[:, b * 16 : (b + 1) * 16, h * HD : (h + 1) * HD] = m
    mixed_ref[...] = dot(raw_ref[...].reshape(F * HALF, COLS), order_ref[...], NN).astype(bf)


def gw_kernel(place, *refs):
    pieces, (mixed_ref, up_ref, mine_ref, other_ref, sems) = refs[:F], refs[F:]
    copies = [
        pltpu.make_async_copy(pieces[k], up_ref.at[place[RANK] ^ k], sems.at[k]) for k in range(F)
    ]
    for c in copies:
        c.start()
    for c in copies:
        c.wait()
    up = up_ref[...].reshape(F * HALF, DW)
    gw = dot(mixed_ref[...], up, TN)
    mine_ref[...] = gw[: COLS // 2]
    other_ref[...] = gw[COLS // 2 :].astype(bf)


def score_kernel(qkv_ref, probs_ref, up_ref, w_ref, spot_ref, dm_ref, ds_ref, sums_ref):
    dm = dot(up_ref[...].reshape(F * HALF, DW), w_ref[...], NT).astype(bf)
    dm = dot(dm, spot_ref[...], NN)
    dm_ref[...] = dm.astype(bf).reshape(F, HALF, COLS)
    for h in range(HL):
        cols = slice(h * HD, (h + 1) * HD)
        total = jnp.zeros((F, POS), f32)
        for b in range(NB):
            d = dm_ref[:, b * 16 : (b + 1) * 16, cols].reshape(POS, HD)
            p = probs_ref[h, b]
            g = dot(d, block(qkv_ref, 2, b, h), NT)
            ds = p * (g - jnp.sum(p * g, axis=-1, keepdims=True))
            total = total + jnp.sum(ds.reshape(F, 16, POS), axis=1)
            ds_ref[h, b] = ds.astype(bf)
        sums_ref[:, cols] = total


def grad_kernel(qkv_ref, probs_ref, dm_ref, ds_ref, grads_ref):
    for h in range(HL):
        cols = slice(h * HD, (h + 1) * HD)
        for b in range(NB):
            rows = slice(b * 16, (b + 1) * 16)
            d = dm_ref[:, rows, cols].reshape(POS, HD)
            low = ds_ref[h, b]
            gq = dot(low, block(qkv_ref, 1, b, h), NN) * FACTOR
            gk = dot(low, block(qkv_ref, 0, b, h), TN) * FACTOR
            gv = dot(probs_ref[h, b].astype(bf), d, TN)
            for i, val in enumerate((gq, gk, gv)):
                grads_ref[:, i, rows, cols] = val.astype(bf).reshape(F, 16, HD)


def tiles(x):
    return jnp.concatenate([x[:, a * 128 : (a + 1) * 128] for a in range(HL)], axis=0)


def split(b):
    high = b.astype(bf).astype(f32)
    low = (b - high).astype(bf).astype(f32)
    return high, low


def join_kernel(mine_ref, other_ref, s0, s1, s2, s3, own_ref, b_ref, m1, m2, m3):
    gw = mine_ref[...] + other_ref[...].astype(f32)
    high, low = split(tiles((s0[...] + s1[...]) + (s2[...] + s3[...])))
    own_ref[...] = gw[:48]
    b_ref[...] = high + low
    ride = jnp.concatenate([high, low], axis=0).astype(bf)
    for k, m in enumerate((m1, m2, m3), 1):
        m[:, :DW] = gw[48 * k : 48 * (k + 1)].astype(bf)
        m[:, DW:] = ride


def ysum_kernel(own_ref, b_ref, m1, m2, m3, own_out, b_out, n1, n2, n3):
    gw = [own_ref[...]] + [m[:, :DW].astype(f32) for m in (m1, m2, m3)]
    rides = [m[:, DW:].astype(f32) for m in (m1, m2, m3)]
    b = [b_ref[...]] + [x[:24] + x[24:] for x in rides]
    gw, b = ((x[0] + x[1]) + (x[2] + x[3]) for x in (gw, b))
    high, low = split(jnp.concatenate([b[2 * a : 2 * a + 2] for a in range(12)], axis=1))
    own_out[...] = gw[:12]
    b_out[...] = high + low
    for k, n in enumerate((n1, n2, n3), 1):
        n[...] = jnp.concatenate([gw[12 * k : 12 * (k + 1)], high, low], axis=0).astype(bf)


def zsum_kernel(own_ref, b_ref, n1, n2, n3, first_ref, second_ref, off_ref):
    parts = [n[...].astype(f32) for n in (n1, n2, n3)]
    gw = [own_ref[...]] + [x[:12] for x in parts]
    b = [b_ref[...]] + [x[12:14] + x[14:16] for x in parts]
    gw, flat = ((x[0] + x[1]) + (x[2] + x[3]) for x in (gw, b))
    pad = jnp.zeros((2, DW), f32)
    first_ref[...] = jnp.concatenate([gw[:6], pad], axis=0)
    second_ref[...] = jnp.concatenate([gw[6:], pad], axis=0)
    sums = jnp.concatenate([flat[:, 128 * a : 128 * (a + 1)] for a in range(12)], axis=0)
    out = jnp.zeros((16, 128), f32)
    head, t = iota((16, 24), 0) % HL, iota((16, 24), 1)
    g, o = iota((128, 128), 0) // 16, iota((128, 128), 1)
    hi = lax.Precision.HIGHEST
    for f in range(F):
        row = dot((t == head * F + f).astype(f32), sums, NN, precision=hi)
        out = out + dot(row, (g - f + 7 == o).astype(f32), NN, precision=hi)
    off_ref[...] = out


def last_kernel(place, a_ref, b_ref, o0, o1, o2, o3, gw_ref, bias_ref):
    gw_ref[...] = (a_ref[...] + b_ref[...])[:6]
    row = iota((16, 128), 0) // HL
    out = jnp.zeros((16, 128), f32)
    for k, o in enumerate((o0, o1, o2, o3)):
        out = out + jnp.where(row == ((place[RANK] // C) ^ k), o[...], 0.0)
    bias_ref[...] = out[:12, :15]


def hop(x, axis, k, n):
    return lax.ppermute(x, axis, [(i, i ^ k) for i in range(n)])


def per_device(qkv_time, shard_sizes, bias_time, w_out, cot_out):
    xi, yi, zi = (lax.axis_index(a) for a in ("x", "y", "z"))
    core = lax.axis_index("core")
    place = jnp.stack([core, yi, zi, xi * C + core]).astype(jnp.int32)

    there = [
        ((2 * c + z0) * X + x, (z0 * X + x) * X + c)
        for c in range(X)
        for z0 in range(2)
        for x in range(X)
    ]
    near = [(a, b ^ X) for a, b in there]
    rows8 = jnp.pad(w_out, ((0, 2), (0, 0)))
    held = jnp.concatenate([lax.ppermute(rows8, ("z", "x"), p) for p in (there, near)])
    held = jnp.concatenate([held, hop(held, "z", 2, Z)])

    cot = lax.all_to_all(cot_out[0, 0], SEQ, 0, 0, tiled=True)
    packed = qkv_time[:, 0, 0].reshape(3, C, HALF, X, COLS).transpose(3, 1, 0, 2, 4)
    qkv = lax.all_to_all(packed.reshape(F, 3, HALF, COLS), SEQ, 0, 0, tiled=True)

    same, other = call(
        compact_kernel, "compact", [((HALF, DW), bf)] * 2, place, shard_sizes, cot, smem=2, flops=100_000_000
    )
    held, same = lax.optimization_barrier((held, same))
    held = jnp.concatenate([held, hop(held, "z", 4, Z)])
    held = lax.all_gather(held, ("y", "core"), axis=0, tiled=True)
    pieces = [same] + [hop(other if k & 1 else same, SEQ, k, F) for k in range(1, F)]

    t, r = iota((512, COLS), 0), iota((512, COLS), 1)
    i, sub = r % 6, r // 6
    rj, ry, rc = (sub // 32) * 4 + (sub // 2) % 4, (sub // 8) % 4, sub % 2
    spot = ((((ry * C + rc) * Z + (rj ^ zi)) * 8 + i) == t).astype(bf)

    local_bias = lax.dynamic_slice(bias_time, (xi * HL, 0), (HL, 15))
    pair = jnp.stack([local_bias[:, 7 - f : 15 - f] for f in range(F)], axis=1)
    alike = jnp.eye(16, dtype=jnp.bool_)[None, None, :, None, :]
    bias_m = jnp.where(alike, pair[:, :, None, :, None], f32(-1e30)).reshape(HL, POS, POS)
    t2, r2 = iota((COLS, COLS), 1), iota((COLS, COLS), 0)
    j = ((t2 // 12) % 4 + ((t2 // 6) % 2) * 4) ^ zi
    oy, oc = ((t2 // 48) % 4) ^ yi, (t2 // 192) ^ core
    src = (((j // 4) * 4 + oy) * 8 + (j % 4) * 2 + oc) * 6 + t2 % 6
    order = (src == r2).astype(bf)
    probs, mixed = call(
        fwd_kernel,
        "attn_fwd",
        [((HL, NB, POS, POS), f32), ((F * HALF, COLS), bf)],
        qkv,
        bias_m,
        order,
        scratch=[pltpu.VMEM((F, HALF, COLS), bf)],
        flops=250_000_000,
    )

    up, mine, theirs = call(
        gw_kernel,
        "grad_w",
        [((F, HALF, DW), bf), ((COLS // 2, DW), f32), ((COLS // 2, DW), bf)],
        place,
        *pieces,
        mixed,
        smem=1,
        hbm=F,
        scratch=[pltpu.SemaphoreType.DMA((F,))],
        flops=604_000_000,
    )
    theirs = hop(theirs, "core", 1, C)

    dm, ds, sums = call(
        score_kernel,
        "scores_bwd",
        [((F, HALF, COLS), bf), ((HL, NB, POS, POS), bf), ((F, COLS), f32)],
        qkv,
        probs,
        up,
        held,
        spot,
        flops=900_000_000,
    )
    both = lax.ppermute(sums, ("z", "core"), [(i, i ^ 9) for i in range(Z * C)])
    sums = [sums, hop(sums, "core", 1, C), hop(sums, "z", 4, Z), both]
    (grads,) = call(
        grad_kernel, "grads", [((F, 3, HALF, COLS), bf)], qkv, probs, dm, ds, flops=150_000_000
    )

    wide = ((48, DW + 128), bf)
    own, b, *msgs = call(
        join_kernel, "join", [((48, DW), f32), ((24, 128), f32), wide, wide, wide], mine, theirs, *sums
    )
    msgs = [hop(m, "y", k, Y) for k, m in enumerate(msgs, 1)]
    part = ((16, DW), bf)
    own, b, *msgs = call(
        ysum_kernel, "ysum", [((12, DW), f32), ((2, DW), f32), part, part, part], own, b, *msgs
    )
    msgs = [hop(m, "z", k, Z) for k, m in enumerate(msgs, 1)]
    first, second, off = call(
        zsum_kernel, "zsum", [((8, DW), f32), ((8, DW), f32), ((16, 128), f32)], own, b, *msgs
    )
    home = [(a, b) for b, a in there]
    cross = [((((a // X) ^ 4) * X + a % X), b) for a, b in home]
    first = lax.ppermute(first, ("z", "x"), home)
    second = lax.ppermute(second, ("z", "x"), cross)
    offs = [off] + [hop(off, "x", k, X) for k in range(1, X)]

    back = lax.all_to_all(grads, SEQ, 0, 0, tiled=True).reshape(X, C, 3, HALF, COLS)
    grad_qkv = back.transpose(2, 1, 3, 0, 4).reshape(3, 1, 1, POS, DW)
    first, grad_qkv = lax.optimization_barrier((first, grad_qkv))
    grad_w_out, grad_bias = call(
        last_kernel, "last", [((6, DW), f32), ((12, 15), f32)], place, first, second, *offs, smem=1
    )
    return grad_qkv, grad_bias, grad_w_out


def solution(mesh):
    grid = Mesh(mesh.devices.reshape(Z, Y, X, C), ("z", "y", "x", "core"))
    dp, every = ("z", "y"), ("z", "y", "x", "core")
    return jax.shard_map(
        per_device,
        mesh=grid,
        in_specs=(
            P(None, dp, SEQ, None, None),
            P(dp, None),
            P(),
            P(every, None),
            P(dp, SEQ, None, None, None),
        ),
        out_specs=(P(None, dp, SEQ, None, None), P(), P(every, None)),
        check_vma=False,
    )
```

```python
import math

import jax
import jax.numpy as jnp
from jax import lax
from jax.experimental import pallas as pl
from jax.experimental.pallas import tpu as pltpu
from jax.sharding import Mesh, PartitionSpec as P

Z, Y, X, C = 8, 4, 4, 2
SEQ = ("x", "core")
F = 8
POS = 128
HALF = 64
NB = 4
HL = 3
HD = 128
COLS = HL * HD
DW = 1536
CAP = 32
FACTOR = 1.0 / math.sqrt(HD)
NN = (((1,), (0,)), ((), ()))
NT = (((1,), (1,)), ((), ()))
TN = (((0,), (0,)), ((), ()))
bf, f32 = jnp.bfloat16, jnp.float32


def dot(a, b, dims, **kw):
    return lax.dot_general(a, b, dims, preferred_element_type=f32, **kw)


def iota(shape, dim):
    return lax.broadcasted_iota(jnp.int32, shape, dim)


def call(body, name, outs, *ins, smem=0, scratch=(), flops=0, space=pltpu.VMEM, vmem=16):
    total = sum(math.prod(s) * jnp.dtype(d).itemsize for s, d in outs)
    total += sum(a.size * a.dtype.itemsize for a in ins)
    specs = [pl.BlockSpec(memory_space=pltpu.SMEM)] * smem
    specs += [pl.BlockSpec(memory_space=space)] * (len(ins) - smem)
    return pl.pallas_call(
        body,
        out_shape=tuple(jax.ShapeDtypeStruct(s, d) for s, d in outs),
        in_specs=specs,
        out_specs=tuple(pl.BlockSpec(memory_space=space) for _ in outs),
        scratch_shapes=list(scratch),
        compiler_params=pltpu.CompilerParams(vmem_limit_bytes=vmem << 20),
        cost_estimate=pl.CostEstimate(flops=flops, bytes_accessed=total, transcendentals=0),
        name=name,
    )(*ins)


def pack_kernel(qkv_ref, cot_ref, out_ref, sems):
    copies = []
    for d in range(F):
        rows, cols = pl.ds((d % C) * HALF, HALF), pl.ds((d // C) * COLS, COLS)
        copies.append((qkv_ref.at[:, rows, cols], out_ref.at[d, pl.ds(0, 3)]))
    for j in range(X):
        dst = out_ref.at[:, 3 + j // 2, pl.ds((j % 2) * CAP, CAP)]
        copies.append((cot_ref.at[:, :, pl.ds(j * COLS, COLS)], dst))
    copies = [pltpu.make_async_copy(src, dst, sems.at[n]) for n, (src, dst) in enumerate(copies)]
    for c in copies:
        c.start()
    for c in copies:
        c.wait()


def compact_kernel(sizes, recv_ref, out_ref):
    shape = (POS, F * CAP)
    pos, col = iota(shape, 0), iota(shape, 1)
    start = jnp.int32(0)
    picked = jnp.full(shape, -1, jnp.int32)
    for j in range(F):
        slot = col - j * CAP
        inside = (slot >= 0) & (slot < sizes[0, j])
        picked = jnp.where(inside, slot + start, picked)
        start = start + sizes[0, j]
    hot = (picked == pos).astype(f32).astype(bf)
    for j in range(X):
        slots = recv_ref[:, 3 + j // 2, (j % 2) * CAP : (j % 2 + 1) * CAP, :]
        up = dot(hot, slots.reshape(F * CAP, COLS), NN).astype(bf)
        for d in range(F):
            r = (d % C) * HALF
            out_ref[d, :, j * COLS : (j + 1) * COLS] = up[r : r + HALF]


def block(ref, i, b, h):
    return ref[:, i, b * 16 : (b + 1) * 16, h * HD : (h + 1) * HD].reshape(POS, HD)


def fwd_kernel(qkv_ref, bias_ref, order_ref, probs_ref, mixed_ref, raw_ref):
    for h in range(HL):
        for b in range(NB):
            q, k, v = (block(qkv_ref, i, b, h) for i in range(3))
            s = dot(q, k, NT) * FACTOR + bias_ref[h]
            e = jnp.exp(s - jnp.max(s, axis=-1, keepdims=True))
            p = e / jnp.sum(e, axis=-1, keepdims=True)
            probs_ref[h, b] = p
            m = dot(p.astype(bf), v, NN).astype(bf).reshape(F, 16, HD)
            raw_ref[:, b * 16 : (b + 1) * 16, h * HD : (h + 1) * HD] = m
    mixed_ref[...] = dot(raw_ref[...].reshape(F * HALF, COLS), order_ref[...], NN).astype(bf)


def gw_kernel(up_ref, mixed_ref, mine_ref, other_ref):
    gw = dot(mixed_ref[...], up_ref[...].reshape(F * HALF, DW), TN)
    mine_ref[...] = gw[: COLS // 2]
    other_ref[...] = gw[COLS // 2 :].astype(bf)


def score_kernel(qkv_ref, probs_ref, up_ref, w0_ref, w1_ref, spot_ref, dm_ref, ds_ref, sums_ref):
    up = up_ref[...].reshape(F * HALF, DW)
    dm = jnp.concatenate([dot(up, w[...], NT).astype(bf) for w in (w0_ref, w1_ref)], axis=1)
    dm = dot(dm, spot_ref[...], NN)
    dm_ref[...] = dm.astype(bf).reshape(F, HALF, COLS)
    for h in range(HL):
        cols = slice(h * HD, (h + 1) * HD)
        total = jnp.zeros((F, POS), f32)
        for b in range(NB):
            d = dm_ref[:, b * 16 : (b + 1) * 16, cols].reshape(POS, HD)
            p = probs_ref[h, b]
            g = dot(d, block(qkv_ref, 2, b, h), NT)
            ds = p * (g - jnp.sum(p * g, axis=-1, keepdims=True))
            total = total + jnp.sum(ds.reshape(F, 16, POS), axis=1)
            ds_ref[h, b] = ds.astype(bf)
        sums_ref[:, cols] = total


def grad_kernel(qkv_ref, probs_ref, dm_ref, ds_ref, grads_ref):
    for h in range(HL):
        cols = slice(h * HD, (h + 1) * HD)
        for b in range(NB):
            rows = slice(b * 16, (b + 1) * 16)
            d = dm_ref[:, rows, cols].reshape(POS, HD)
            low = ds_ref[h, b]
            gq = dot(low, block(qkv_ref, 1, b, h), NN) * FACTOR
            gk = dot(low, block(qkv_ref, 0, b, h), TN) * FACTOR
            gv = dot(probs_ref[h, b].astype(bf), d, TN)
            for i, val in enumerate((gq, gk, gv)):
                grads_ref[:, i, rows, cols] = val.astype(bf).reshape(F, 16, HD)


def tiles(x):
    return jnp.concatenate([x[:, a * 128 : (a + 1) * 128] for a in range(HL)], axis=0)


def split(b):
    high = b.astype(bf).astype(f32)
    low = (b - high).astype(bf).astype(f32)
    return high, low


def join_kernel(mine_ref, other_ref, s0, s1, own_ref, b_ref, m1, m2, m3):
    gw = mine_ref[...] + other_ref[...].astype(f32)
    high, low = split(tiles(s0[...] + s1[...]))
    own_ref[...] = gw[:48]
    b_ref[...] = high + low
    ride = jnp.concatenate([high, low], axis=0).astype(bf)
    for k, m in enumerate((m1, m2, m3), 1):
        m[:, :DW] = gw[48 * k : 48 * (k + 1)].astype(bf)
        m[:, DW:] = ride


def ysum_kernel(own_ref, b_ref, m1, m2, m3, own_out, b_out, n1, n2, n3):
    gw = [own_ref[...]] + [m[:, :DW].astype(f32) for m in (m1, m2, m3)]
    rides = [m[:, DW:].astype(f32) for m in (m1, m2, m3)]
    b = [b_ref[...]] + [x[:24] + x[24:] for x in rides]
    gw, b = ((x[0] + x[1]) + (x[2] + x[3]) for x in (gw, b))
    high, low = split(jnp.concatenate([b[2 * a : 2 * a + 2] for a in range(12)], axis=1))
    own_out[...] = gw[:12]
    b_out[...] = high + low
    for k, n in enumerate((n1, n2, n3), 1):
        n[...] = jnp.concatenate([gw[12 * k : 12 * (k + 1)], high, low], axis=0).astype(bf)


def zsum_kernel(own_ref, b_ref, n1, n2, n3, keep_ref, send_ref):
    parts = [n[...].astype(f32) for n in (n1, n2, n3)]
    gw = [own_ref[...]] + [x[:12] for x in parts]
    b = [b_ref[...]] + [x[12:14] + x[14:16] for x in parts]
    gw, b = ((x[0] + x[1]) + (x[2] + x[3]) for x in (gw, b))
    keep_ref[...] = jnp.concatenate([gw[:6], b], axis=0)
    send_ref[...] = jnp.concatenate([gw[6:], b], axis=0)


def total_kernel(keep_ref, recv_ref, sum_ref, off_ref):
    total = keep_ref[...] + recv_ref[...]
    sum_ref[...] = total
    flat = total[6:]
    sums = jnp.concatenate([flat[:, 128 * a : 128 * (a + 1)] for a in range(12)], axis=0)
    out = jnp.zeros((16, 128), f32)
    head, t = iota((16, 24), 0) % HL, iota((16, 24), 1)
    g, o = iota((128, 128), 0) // 16, iota((128, 128), 1)
    hi = lax.Precision.HIGHEST
    for f in range(F):
        row = dot((t == head * F + f).astype(f32), sums, NN, precision=hi)
        out = out + dot(row, (g - f + 7 == o).astype(f32), NN, precision=hi)
    off_ref[...] = out


def last_kernel(place, home_ref, o0, o1, o2, o3, gw_ref, bias_ref):
    gw_ref[...] = home_ref[:6]
    row = iota((16, 128), 0) // HL
    out = jnp.zeros((16, 128), f32)
    for k, o in enumerate((o0, o1, o2, o3)):
        out = out + jnp.where(row == ((place[0]) ^ k), o[...], 0.0)
    bias_ref[...] = out[:12, :15]


def hop(x, axis, k, n):
    return lax.ppermute(x, axis, [(i, i ^ k) for i in range(n)])


def per_device(qkv_time, shard_sizes, bias_time, w_out, cot_out):
    xi, yi, zi = (lax.axis_index(a) for a in ("x", "y", "z"))
    core = lax.axis_index("core")

    block5 = ((F, 5, HALF, COLS), bf)
    (packed,) = call(
        pack_kernel,
        "pack",
        [block5],
        qkv_time[:, 0, 0],
        cot_out[0, 0],
        scratch=[pltpu.SemaphoreType.DMA((F + X,))],
        space=pltpu.HBM,
        vmem=56,
    )
    recv = lax.all_to_all(packed, SEQ, 0, 0, tiled=True)

    there = [
        ((2 * c + z0) * X + x, (z0 * X + x) * X + c)
        for c in range(X)
        for z0 in range(2)
        for x in range(X)
    ]
    near = [(a, b ^ X) for a, b in there]
    rows8 = jnp.pad(w_out, ((0, 2), (0, 0)))
    rows8, _ = lax.optimization_barrier((rows8, packed))
    held = jnp.concatenate([lax.ppermute(rows8, ("z", "x"), p) for p in (there, near)])
    held = jnp.concatenate([held, hop(held, "z", 2, Z)])
    held = jnp.concatenate([held, hop(held, "z", 4, Z)])

    (up,) = call(
        compact_kernel, "compact", [((F, HALF, DW), bf)], shard_sizes, recv, smem=1, flops=100_000_000
    )
    held, up = lax.optimization_barrier((held, up))
    up = lax.all_to_all(up, SEQ, 0, 0, tiled=True)
    held = jnp.concatenate([held] + [hop(held, "y", k, Y) for k in range(1, Y)])
    recv, held = lax.optimization_barrier((recv, held))
    held2 = hop(held, "core", 1, C)

    t, r = iota((512, COLS), 0), iota((512, COLS), 1)
    i, sub = r % 6, r // 6
    rj, ry, rc = (sub // 32) * 4 + (sub // 2) % 4, (sub // 8) % 4, sub % 2
    spot = (((((rc ^ core) * Y + (ry ^ yi)) * Z + (rj ^ zi)) * 8 + i) == t).astype(bf)

    local_bias = lax.dynamic_slice(bias_time, (xi * HL, 0), (HL, 15))
    pair = jnp.stack([local_bias[:, 7 - f : 15 - f] for f in range(F)], axis=1)
    alike = jnp.eye(16, dtype=jnp.bool_)[None, None, :, None, :]
    bias_m = jnp.where(alike, pair[:, :, None, :, None], f32(-1e30)).reshape(HL, POS, POS)
    t2, r2 = iota((COLS, COLS), 1), iota((COLS, COLS), 0)
    j = ((t2 // 12) % 4 + ((t2 // 6) % 2) * 4) ^ zi
    oy, oc = ((t2 // 48) % 4) ^ yi, (t2 // 192) ^ core
    src = (((j // 4) * 4 + oy) * 8 + (j % 4) * 2 + oc) * 6 + t2 % 6
    order = (src == r2).astype(bf)
    probs, mixed = call(
        fwd_kernel,
        "attn_fwd",
        [((HL, NB, POS, POS), f32), ((F * HALF, COLS), bf)],
        recv,
        bias_m,
        order,
        scratch=[pltpu.VMEM((F, HALF, COLS), bf)],
        flops=250_000_000,
    )

    mine, theirs = call(
        gw_kernel,
        "grad_w",
        [((COLS // 2, DW), f32), ((COLS // 2, DW), bf)],
        up,
        mixed,
        flops=604_000_000,
    )
    theirs = hop(theirs, "core", 1, C)
    up, theirs = lax.optimization_barrier((up, theirs))

    dm, ds, sums = call(
        score_kernel,
        "scores_bwd",
        [((F, HALF, COLS), bf), ((HL, NB, POS, POS), bf), ((F, COLS), f32)],
        recv,
        probs,
        up,
        held,
        held2,
        spot,
        flops=900_000_000,
    )
    sums2 = hop(sums, "core", 1, C)

    wide = ((48, DW + 128), bf)
    own, b, *msgs = call(
        join_kernel, "join", [((48, DW), f32), ((24, 128), f32), wide, wide, wide], mine, theirs, sums, sums2
    )
    msgs = [hop(m, "y", k, Y) for k, m in enumerate(msgs, 1)]
    dm, msgs[1], msgs[2] = lax.optimization_barrier((dm, msgs[1], msgs[2]))
    (grads,) = call(
        grad_kernel, "grads", [((F, 3, HALF, COLS), bf)], recv, probs, dm, ds, flops=150_000_000
    )
    part = ((16, DW), bf)
    own, b, *msgs = call(
        ysum_kernel, "ysum", [((12, DW), f32), ((2, DW), f32), part, part, part], own, b, *msgs
    )
    msgs = [hop(m, "z", k, Z) for k, m in enumerate(msgs, 1)]
    keep, send = call(zsum_kernel, "zsum", [((8, DW), f32)] * 2, own, b, *msgs)
    total, off = call(
        total_kernel, "total", [((8, DW), f32), ((16, 128), f32)], keep, hop(send, "z", 4, Z)
    )
    home = lax.ppermute(total, ("z", "x"), [(b, a) for a, b in there])
    offs = [off] + [hop(off, "x", k, X) for k in range(1, X)]

    back = lax.all_to_all(grads, SEQ, 0, 0, tiled=True).reshape(X, C, 3, HALF, COLS)
    grad_qkv = back.transpose(2, 1, 3, 0, 4).reshape(3, 1, 1, POS, DW)
    home, grad_qkv = lax.optimization_barrier((home, grad_qkv))
    grad_w_out, grad_bias = call(
        last_kernel, "last", [((6, DW), f32), ((12, 15), f32)], xi.reshape(1), home, *offs, smem=1
    )
    return grad_qkv, grad_bias, grad_w_out


def solution(mesh):
    grid = Mesh(mesh.devices.reshape(Z, Y, X, C), ("z", "y", "x", "core"))
    dp, every = ("z", "y"), ("z", "y", "x", "core")
    return jax.shard_map(
        per_device,
        mesh=grid,
        in_specs=(
            P(None, dp, SEQ, None, None),
            P(dp, None),
            P(),
            P(every, None),
            P(dp, SEQ, None, None, None),
        ),
        out_specs=(P(None, dp, SEQ, None, None), P(), P(every, None)),
        check_vma=False,
    )
```

```python
import math

import jax
import jax.numpy as jnp
import numpy as np
from jax import lax
from jax.experimental import pallas as pl
from jax.experimental.pallas import tpu as pltpu
from jax.sharding import Mesh, PartitionSpec as P

Z, Y, X, C = 8, 4, 4, 2
SEQ = ("x", "core")
F = 8
POS = 128
HALF = 64
NB = 4
HL = 3
HD = 128
COLS = HL * HD
DW = 1536
CAP = 32
FACTOR = 1.0 / math.sqrt(HD)
NN = (((1,), (0,)), ((), ()))
NT = (((1,), (1,)), ((), ()))
TN = (((0,), (0,)), ((), ()))
bf, f32 = jnp.bfloat16, jnp.float32
CORE, YI, ZI, XI, RANK = range(5)

ROW = np.arange(COLS)
ROWS_OF = np.zeros((8, COLS), np.int32)
ROWS_OF[0] = ROW // 6 % 2
ROWS_OF[1] = ROW // 48 % 4
ROWS_OF[2] = ROW // 192 * 4 + ROW // 12 % 4
ROWS_OF[3] = ROW % 6
LEAVE = np.zeros((8, COLS), np.int32)
LEAVE[0] = ROW // 192
LEAVE[1] = (((ROW % 48 // 24) * 4 + ROW // 48 % 4) * 8 + ROW % 24 // 6 * 2) * 6 + ROW % 6


def dot(a, b, dims, **kw):
    return lax.dot_general(a, b, dims, preferred_element_type=f32, **kw)


def iota(shape, dim):
    return lax.broadcasted_iota(jnp.int32, shape, dim)


def call(body, name, outs, *ins, smem=0, scratch=(), flops=0, space=pltpu.VMEM, vmem=16):
    total = sum(math.prod(s) * jnp.dtype(d).itemsize for s, d in outs)
    total += sum(a.size * a.dtype.itemsize for a in ins)
    specs = [pl.BlockSpec(memory_space=pltpu.SMEM)] * smem
    specs += [pl.BlockSpec(memory_space=space)] * (len(ins) - smem)
    return pl.pallas_call(
        body,
        out_shape=tuple(jax.ShapeDtypeStruct(s, d) for s, d in outs),
        in_specs=specs,
        out_specs=tuple(pl.BlockSpec(memory_space=space) for _ in outs),
        scratch_shapes=list(scratch),
        compiler_params=pltpu.CompilerParams(vmem_limit_bytes=vmem << 20),
        cost_estimate=pl.CostEstimate(flops=flops, bytes_accessed=total, transcendentals=0),
        name=name,
    )(*ins)


def pack_kernel(qkv_ref, cot_ref, out_ref):
    for d in range(F):
        r, c = d % C * HALF, d // C * COLS
        out_ref[d, :3] = qkv_ref[:, r : r + HALF, c : c + COLS]
    for j in range(X):
        r = j % 2 * CAP
        out_ref[:, 3 + j // 2, r : r + CAP, :] = cot_ref[:, :, j * COLS : (j + 1) * COLS]


def compact_kernel(sizes, recv_ref, out_ref):
    shape = (POS, F * CAP)
    pos, col = iota(shape, 0), iota(shape, 1)
    start = jnp.int32(0)
    picked = jnp.full(shape, -1, jnp.int32)
    for j in range(F):
        slot = col - j * CAP
        inside = (slot >= 0) & (slot < sizes[0, j])
        picked = jnp.where(inside, slot + start, picked)
        start = start + sizes[0, j]
    hot = (picked == pos).astype(f32).astype(bf)
    for j in range(X):
        slots = recv_ref[:, 3 + j // 2, (j % 2) * CAP : (j % 2 + 1) * CAP, :]
        up = dot(hot, slots.reshape(F * CAP, COLS), NN).astype(bf)
        for d in range(F):
            r = (d % C) * HALF
            out_ref[d, :, j * COLS : (j + 1) * COLS] = up[r : r + HALF]


def block(ref, i, b, h):
    return ref[:, i, b * 16 : (b + 1) * 16, h * HD : (h + 1) * HD].reshape(POS, HD)


def fwd_kernel(place, bias, leave_ref, qkv_ref, probs_ref, mixed_ref, raw_ref):
    row, col = iota((POS, POS), 0), iota((POS, POS), 1)
    alike = (row & 15) == (col & 15)
    offset = (col >> 4) - (row >> 4) + 7
    for h in range(HL):
        pair = jnp.full((POS, POS), -1e30, f32)
        for o in range(15):
            pair = jnp.where(alike & (offset == o), bias[place[XI] * HL + h, o], pair)
        for b in range(NB):
            q, k, v = (block(qkv_ref, i, b, h) for i in range(3))
            s = dot(q, k, NT) * FACTOR + pair
            e = jnp.exp(s - jnp.max(s, axis=-1, keepdims=True))
            p = e / jnp.sum(e, axis=-1, keepdims=True)
            probs_ref[h, b] = p
            m = dot(p.astype(bf), v, NN).astype(bf).reshape(F, 16, HD)
            raw_ref[:, b * 16 : (b + 1) * 16, h * HD : (h + 1) * HD] = m
    source = leave_ref[1:2] + (leave_ref[0:1] ^ place[CORE]) * 6
    order = (iota((COLS, COLS), 0) == source).astype(f32).astype(bf)
    mixed_ref[...] = dot(raw_ref[...].reshape(F * HALF, COLS), order, NN).astype(bf)


def gw_kernel(up_ref, mixed_ref, mine_ref, other_ref):
    gw = dot(mixed_ref[...], up_ref[...].reshape(F * HALF, DW), TN)
    mine_ref[...] = gw[: COLS // 2]
    other_ref[...] = gw[COLS // 2 :].astype(bf)


def score_kernel(place, rows_ref, qkv_ref, probs_ref, up_ref, w0_ref, w1_ref, dm_ref, ds_ref, sums_ref):
    up = up_ref[...].reshape(F * HALF, DW)
    dm = jnp.concatenate([dot(up, w[...], NT).astype(bf) for w in (w0_ref, w1_ref)], axis=1)
    c, y, j = (rows_ref[n : n + 1] ^ place[n] for n in (CORE, YI, ZI))
    spot = ((c * Y + y) * Z + j) * 8 + rows_ref[3:4]
    spot = (iota((512, COLS), 0) == spot).astype(f32).astype(bf)
    dm = dot(dm, spot, NN)
    dm_ref[...] = dm.astype(bf).reshape(F, HALF, COLS)
    for h in range(HL):
        cols = slice(h * HD, (h + 1) * HD)
        total = jnp.zeros((F, POS), f32)
        for b in range(NB):
            d = dm_ref[:, b * 16 : (b + 1) * 16, cols].reshape(POS, HD)
            p = probs_ref[h, b]
            g = dot(d, block(qkv_ref, 2, b, h), NT)
            ds = p * (g - jnp.sum(p * g, axis=-1, keepdims=True))
            total = total + jnp.sum(ds.reshape(F, 16, POS), axis=1)
            ds_ref[h, b] = ds.astype(bf)
        sums_ref[:, cols] = total


def grad_kernel(place, qkv_ref, probs_ref, dm_ref, ds_ref, *refs):
    pieces, nat_ref = refs[:F], refs[F]
    for h in range(HL):
        cols = slice(h * HD, (h + 1) * HD)
        for b in range(NB):
            rows = slice(b * 16, (b + 1) * 16)
            d = dm_ref[:, rows, cols].reshape(POS, HD)
            low = ds_ref[h, b]
            gq = dot(low, block(qkv_ref, 1, b, h), NN) * FACTOR
            gk = dot(low, block(qkv_ref, 0, b, h), TN) * FACTOR
            gv = dot(probs_ref[h, b].astype(bf), d, TN)
            for i, val in enumerate((gq, gk, gv)):
                nat_ref[:, i, rows, cols] = val.astype(bf).reshape(F, 16, HD)
    for k in range(F):
        pieces[k][...] = nat_ref[place[RANK] ^ k]


def unpack_kernel(place, *refs):
    pieces, out_ref, nat_ref = refs[:F], refs[F], refs[F + 1]
    for k in range(F):
        nat_ref[place[RANK] ^ k] = pieces[k][...]
    for d in range(F):
        r, c = d % C * HALF, d // C * COLS
        out_ref[:, r : r + HALF, c : c + COLS] = nat_ref[d]


def split(b):
    high = b.astype(bf).astype(f32)
    low = (b - high).astype(bf).astype(f32)
    return high, low


def join_kernel(mine_ref, other_ref, s0, s1, out_ref):
    gw = mine_ref[...] + other_ref[...].astype(f32)
    hot = ((iota((COLS, 128), 0) >> 4) == iota((COLS, 128), 1)).astype(f32)
    b = dot(s0[...] + s1[...], hot, NN, precision=lax.Precision.HIGHEST)
    high, low = split(b)
    ride = jnp.concatenate([high, low, jnp.zeros((32, 128), f32)], axis=0).astype(bf)
    for y in range(Y):
        out_ref[y, :, :DW] = gw[48 * y : 48 * (y + 1)].astype(bf)
        out_ref[y, :, DW:] = ride


def ysum_kernel(in_ref, out_ref):
    gw = jnp.sum(in_ref[:, :, :DW].astype(f32), axis=0)
    ride = jnp.sum(in_ref[:, :, DW:].astype(f32), axis=0)
    high, low = split(ride[:8] + ride[8:16])
    pad = jnp.zeros((1, DW - F * 128), f32)
    flat = [jnp.concatenate([x[f : f + 1] for f in range(F)] + [pad], axis=1) for x in (high, low)]
    for j in range(Z):
        out_ref[j] = jnp.concatenate([gw[6 * j : 6 * j + 6]] + flat, axis=0).astype(bf)


def total_kernel(in_ref, sum_ref, off_ref):
    total = jnp.sum(in_ref[...].astype(f32), axis=0)
    sum_ref[...] = total
    flat = total[6:7] + total[7:8]
    head, lane = iota((16, 128), 0) % HL, iota((16, 128), 1)
    g, o = iota((128, 128), 0) & 7, iota((128, 128), 1)
    out = jnp.zeros((16, 128), f32)
    for f in range(F):
        row = jnp.where((lane >> 3) == head, flat[:, 128 * f : 128 * (f + 1)], 0.0)
        out = out + dot(row, (g - f + 7 == o).astype(f32), NN, precision=lax.Precision.HIGHEST)
    off_ref[...] = out


def last_kernel(place, home_ref, o0, o1, o2, o3, gw_ref, bias_ref):
    gw_ref[...] = home_ref[:6]
    row = iota((16, 128), 0) // HL
    out = jnp.zeros((16, 128), f32)
    for k, o in enumerate((o0, o1, o2, o3)):
        out = out + jnp.where(row == (place[XI] ^ k), o[...], 0.0)
    bias_ref[...] = out[:12, :15]


def hop(x, axis, k, n):
    return lax.ppermute(x, axis, [(i, i ^ k) for i in range(n)])


def per_device(qkv_time, shard_sizes, bias_time, w_out, cot_out):
    xi, yi, zi, core = (lax.axis_index(a) for a in ("x", "y", "z", "core"))
    place = jnp.stack([core, yi, zi, xi, xi * C + core]).astype(jnp.int32)

    block5 = ((F, 5, HALF, COLS), bf)
    (packed,) = call(
        pack_kernel,
        "pack",
        [block5],
        qkv_time[:, 0, 0],
        cot_out[0, 0],
    )
    recv = lax.all_to_all(packed, SEQ, 0, 0, tiled=True)

    there = [
        ((2 * c + z0) * X + x, (z0 * X + x) * X + c)
        for c in range(X)
        for z0 in range(2)
        for x in range(X)
    ]
    near = [(a, b ^ X) for a, b in there]
    rows8 = jnp.pad(w_out, ((0, 2), (0, 0)))
    rows8, _ = lax.optimization_barrier((rows8, packed))
    held = jnp.concatenate([lax.ppermute(rows8, ("z", "x"), p) for p in (there, near)])
    held = jnp.concatenate([held, hop(held, "z", 2, Z)])
    held = jnp.concatenate([held, hop(held, "z", 4, Z)])

    (up,) = call(
        compact_kernel, "compact", [((F, HALF, DW), bf)], shard_sizes, recv, smem=1, flops=100_000_000
    )
    held, up = lax.optimization_barrier((held, up))
    up = lax.all_to_all(up, SEQ, 0, 0, tiled=True)
    held = jnp.concatenate([held] + [hop(held, "y", k, Y) for k in range(1, Y)])
    recv, held = lax.optimization_barrier((recv, held))
    held2 = hop(held, "core", 1, C)

    probs, mixed = call(
        fwd_kernel,
        "attn_fwd",
        [((HL, NB, POS, POS), f32), ((F * HALF, COLS), bf)],
        place,
        bias_time,
        LEAVE,
        recv,
        smem=2,
        scratch=[pltpu.VMEM((F, HALF, COLS), bf)],
        flops=250_000_000,
    )

    mine, theirs = call(
        gw_kernel,
        "grad_w",
        [((COLS // 2, DW), f32), ((COLS // 2, DW), bf)],
        up,
        mixed,
        flops=604_000_000,
    )
    theirs = hop(theirs, "core", 1, C)
    up, theirs = lax.optimization_barrier((up, theirs))

    dm, ds, sums = call(
        score_kernel,
        "scores_bwd",
        [((F, HALF, COLS), bf), ((HL, NB, POS, POS), bf), ((F, COLS), f32)],
        place,
        ROWS_OF,
        recv,
        probs,
        up,
        held,
        held2,
        smem=1,
        flops=900_000_000,
    )
    sums2 = hop(sums, "core", 1, C)

    pieces = call(
        grad_kernel,
        "grads",
        [((3, HALF, COLS), bf)] * F,
        place,
        recv,
        probs,
        dm,
        ds,
        smem=1,
        scratch=[pltpu.VMEM((F, 3, HALF, COLS), bf)],
        flops=150_000_000,
    )

    (msgs,) = call(join_kernel, "join", [((Y, 48, DW + 128), bf)], mine, theirs, sums, sums2)
    msgs, *pieces = lax.optimization_barrier((msgs, *pieces))
    msgs = lax.all_to_all(msgs, "y", 0, 0, tiled=True)
    pieces = pieces[:1] + [hop(p, SEQ, k, F) for k, p in enumerate(pieces[1:], 1)]
    msgs, *pieces[2:6] = lax.optimization_barrier((msgs, *pieces[2:6]))
    (msgs,) = call(ysum_kernel, "ysum", [((Z, 8, DW), bf)], msgs)
    msgs = lax.all_to_all(msgs, "z", 0, 0, tiled=True)
    total, off = call(total_kernel, "total", [((8, DW), f32), ((16, 128), f32)], msgs)
    home = lax.ppermute(total, ("z", "x"), [(b, a) for a, b in there])
    offs = [off] + [hop(off, "x", k, X) for k in range(1, X)]

    (grad_qkv,) = call(
        unpack_kernel,
        "unpack",
        [((3, POS, DW), bf)],
        place,
        *pieces,
        smem=1,
        scratch=[pltpu.VMEM((F, 3, HALF, COLS), bf)],
    )
    grad_qkv = grad_qkv.reshape(3, 1, 1, POS, DW)
    home, grad_qkv = lax.optimization_barrier((home, grad_qkv))
    grad_w_out, grad_bias = call(
        last_kernel, "last", [((6, DW), f32), ((12, 15), f32)], place, home, *offs, smem=1
    )
    return grad_qkv, grad_bias, grad_w_out


def solution(mesh):
    grid = Mesh(mesh.devices.reshape(Z, Y, X, C), ("z", "y", "x", "core"))
    dp, every = ("z", "y"), ("z", "y", "x", "core")
    return jax.shard_map(
        per_device,
        mesh=grid,
        in_specs=(
            P(None, dp, SEQ, None, None),
            P(dp, None),
            P(),
            P(every, None),
            P(dp, SEQ, None, None, None),
        ),
        out_specs=(P(None, dp, SEQ, None, None), P(), P(every, None)),
        check_vma=False,
    )
```

```python
import math

import jax
import jax.numpy as jnp
import numpy as np
from jax import lax
from jax.experimental import pallas as pl
from jax.experimental.pallas import tpu as pltpu
from jax.sharding import Mesh, PartitionSpec as P

Z, Y, X, C = 8, 4, 4, 2
SEQ = ("x", "core")
F = 8
POS = 128
HALF = 64
NB = 4
HL = 3
HD = 128
COLS = HL * HD
DW = 1536
CAP = 32
FACTOR = 1.0 / math.sqrt(HD)
NN = (((1,), (0,)), ((), ()))
NT = (((1,), (1,)), ((), ()))
TN = (((0,), (0,)), ((), ()))
bf, f32 = jnp.bfloat16, jnp.float32
CORE, YI, ZI, XI, RANK = range(5)

ROW = np.arange(COLS)
ROWS_OF = np.zeros((8, COLS), np.int32)
ROWS_OF[0] = ROW // 6 % 2
ROWS_OF[1] = ROW // 48 % 4
ROWS_OF[2] = ROW // 192 * 4 + ROW // 12 % 4
ROWS_OF[3] = ROW % 6
LEAVE = np.zeros((8, COLS), np.int32)
LEAVE[0] = ROW // 192
SUB = ROW % 192 // 6
LEAVE[1] = ((SUB // 16 * 4 + SUB % 4) * 8 + SUB // 4 % 4 * 2) * 6 + ROW % 6


def dot(a, b, dims, **kw):
    return lax.dot_general(a, b, dims, preferred_element_type=f32, **kw)


def iota(shape, dim):
    return lax.broadcasted_iota(jnp.int32, shape, dim)


def call(body, name, outs, *ins, smem=0, scratch=(), flops=0, space=pltpu.VMEM, vmem=16):
    total = sum(math.prod(s) * jnp.dtype(d).itemsize for s, d in outs)
    total += sum(a.size * a.dtype.itemsize for a in ins)
    specs = [pl.BlockSpec(memory_space=pltpu.SMEM)] * smem
    specs += [pl.BlockSpec(memory_space=space)] * (len(ins) - smem)
    return pl.pallas_call(
        body,
        out_shape=tuple(jax.ShapeDtypeStruct(s, d) for s, d in outs),
        in_specs=specs,
        out_specs=tuple(pl.BlockSpec(memory_space=space) for _ in outs),
        scratch_shapes=list(scratch),
        compiler_params=pltpu.CompilerParams(vmem_limit_bytes=vmem << 20),
        cost_estimate=pl.CostEstimate(flops=flops, bytes_accessed=total, transcendentals=0),
        name=name,
    )(*ins)


def pack_kernel(qkv_ref, cot_ref, out_ref):
    for d in range(F):
        r, c = d % C * HALF, d // C * COLS
        out_ref[d, :3] = qkv_ref[:, r : r + HALF, c : c + COLS]
    for j in range(X):
        r = j % 2 * CAP
        out_ref[:, 3 + j // 2, r : r + CAP, :] = cot_ref[:, :, j * COLS : (j + 1) * COLS]


def compact_kernel(sizes, recv_ref, out_ref):
    shape = (POS, F * CAP)
    pos, col = iota(shape, 0), iota(shape, 1)
    start = jnp.int32(0)
    picked = jnp.full(shape, -1, jnp.int32)
    for j in range(F):
        slot = col - j * CAP
        inside = (slot >= 0) & (slot < sizes[0, j])
        picked = jnp.where(inside, slot + start, picked)
        start = start + sizes[0, j]
    hot = (picked == pos).astype(f32).astype(bf)
    for j in range(X):
        slots = recv_ref[:, 3 + j // 2, (j % 2) * CAP : (j % 2 + 1) * CAP, :]
        up = dot(hot, slots.reshape(F * CAP, COLS), NN).astype(bf)
        for d in range(F):
            r = (d % C) * HALF
            out_ref[d, :, j * COLS : (j + 1) * COLS] = up[r : r + HALF]


def block(ref, i, b, h):
    return ref[:, i, b * 16 : (b + 1) * 16, h * HD : (h + 1) * HD].reshape(POS, HD)


def fwd_kernel(place, bias, leave_ref, qkv_ref, probs_ref, mixed_ref, raw_ref):
    row, col = iota((POS, POS), 0), iota((POS, POS), 1)
    alike = (row & 15) == (col & 15)
    offset = (col >> 4) - (row >> 4) + 7
    for h in range(HL):
        pair = jnp.full((POS, POS), -1e30, f32)
        for o in range(15):
            pair = jnp.where(alike & (offset == o), bias[place[XI] * HL + h, o], pair)
        for b in range(NB):
            q, k, v = (block(qkv_ref, i, b, h) for i in range(3))
            s = dot(q, k, NT) * FACTOR + pair
            e = jnp.exp(s - jnp.max(s, axis=-1, keepdims=True))
            p = e / jnp.sum(e, axis=-1, keepdims=True)
            probs_ref[h, b] = p
            m = dot(p.astype(bf), v, NN).astype(bf).reshape(F, 16, HD)
            raw_ref[:, b * 16 : (b + 1) * 16, h * HD : (h + 1) * HD] = m
    source = leave_ref[1:2] + (leave_ref[0:1] ^ place[CORE]) * 6
    order = (iota((COLS, COLS), 0) == source).astype(f32).astype(bf)
    mixed_ref[...] = dot(raw_ref[...].reshape(F * HALF, COLS), order, NN).astype(bf)


def score_kernel(place, rows_ref, recv_ref, probs_ref, mixed_ref, up_ref, w0_ref, w1_ref, *outs):
    mine_ref, other_ref, dm_ref, ds_ref, sums_ref = outs
    up = up_ref[...].reshape(F * HALF, DW)
    gw = dot(mixed_ref[...], up, TN)
    mine_ref[...] = gw[: COLS // 2]
    other_ref[...] = gw[COLS // 2 :].astype(bf)
    dm = jnp.concatenate([dot(up, w[...], NT).astype(bf) for w in (w0_ref, w1_ref)], axis=1)
    c, y, j = (rows_ref[n : n + 1] ^ place[n] for n in (CORE, YI, ZI))
    spot = ((c * Y + y) * Z + j) * 8 + rows_ref[3:4]
    spot = (iota((512, COLS), 0) == spot).astype(f32).astype(bf)
    dm = dot(dm, spot, NN)
    dm_ref[...] = dm.astype(bf).reshape(F, HALF, COLS)
    for h in range(HL):
        cols = slice(h * HD, (h + 1) * HD)
        total = jnp.zeros((F, POS), f32)
        for b in range(NB):
            d = dm_ref[:, b * 16 : (b + 1) * 16, cols].reshape(POS, HD)
            p = probs_ref[h, b]
            g = dot(d, block(recv_ref, 2, b, h), NT)
            ds = p * (g - jnp.sum(p * g, axis=-1, keepdims=True))
            total = total + jnp.sum(ds.reshape(F, 16, POS), axis=1)
            ds_ref[h, b] = ds.astype(bf)
        sums_ref[:, cols] = total


def grad_kernel(place, qkv_ref, probs_ref, dm_ref, ds_ref, *refs):
    pieces, nat_ref = refs[:F], refs[F]
    for h in range(HL):
        cols = slice(h * HD, (h + 1) * HD)
        for b in range(NB):
            rows = slice(b * 16, (b + 1) * 16)
            d = dm_ref[:, rows, cols].reshape(POS, HD)
            low = ds_ref[h, b]
            gq = dot(low, block(qkv_ref, 1, b, h), NN) * FACTOR
            gk = dot(low, block(qkv_ref, 0, b, h), TN) * FACTOR
            gv = dot(probs_ref[h, b].astype(bf), d, TN)
            for i, val in enumerate((gq, gk, gv)):
                nat_ref[:, i, rows, cols] = val.astype(bf).reshape(F, 16, HD)
    for k in range(F):
        pieces[k][...] = nat_ref[place[RANK] ^ k]


def unpack_kernel(place, *refs):
    pieces, out_ref, nat_ref = refs[:F], refs[F], refs[F + 1]
    for k in range(F):
        nat_ref[place[RANK] ^ k] = pieces[k][...]
    for d in range(F):
        r, c = d % C * HALF, d // C * COLS
        out_ref[:, r : r + HALF, c : c + COLS] = nat_ref[d]


def split(b):
    high = b.astype(bf).astype(f32)
    low = (b - high).astype(bf).astype(f32)
    return high, low


def join_kernel(mine_ref, other_ref, s0, s1, out_ref):
    gw = mine_ref[...] + other_ref[...].astype(f32)
    hot = ((iota((COLS, 128), 0) >> 4) == iota((COLS, 128), 1)).astype(f32)
    b = dot(s0[...] + s1[...], hot, NN, precision=lax.Precision.HIGHEST)
    pad = jnp.zeros((1, DW - F * 128), f32)
    flat = [jnp.concatenate([x[f : f + 1] for f in range(F)] + [pad], axis=1) for x in split(b)]
    for d in range(Z * Y):
        out_ref[d] = jnp.concatenate([gw[6 * d : 6 * d + 6]] + flat, axis=0).astype(bf)


def total_kernel(in_ref, sum_ref, off_ref):
    total = jnp.sum(in_ref[...].astype(f32), axis=0)
    sum_ref[...] = total
    flat = total[6:7] + total[7:8]
    head, lane = iota((16, 128), 0) % HL, iota((16, 128), 1)
    g, o = iota((128, 128), 0) & 7, iota((128, 128), 1)
    out = jnp.zeros((16, 128), f32)
    for f in range(F):
        row = jnp.where((lane >> 3) == head, flat[:, 128 * f : 128 * (f + 1)], 0.0)
        out = out + dot(row, (g - f + 7 == o).astype(f32), NN, precision=lax.Precision.HIGHEST)
    off_ref[...] = out


def last_kernel(home_ref, off_ref, gw_ref, bias_ref):
    gw_ref[...] = home_ref[:6]
    row = iota((16, 128), 0) // HL
    out = jnp.zeros((16, 128), f32)
    for c in range(X):
        out = out + jnp.where(row == c, off_ref[c], 0.0)
    bias_ref[...] = out[:12, :15]


def hop(x, axis, k, n):
    return lax.ppermute(x, axis, [(i, i ^ k) for i in range(n)])


def per_device(qkv_time, shard_sizes, bias_time, w_out, cot_out):
    xi, yi, zi, core = (lax.axis_index(a) for a in ("x", "y", "z", "core"))
    place = jnp.stack([core, yi, zi, xi, xi * C + core]).astype(jnp.int32)

    block5 = ((F, 5, HALF, COLS), bf)
    (packed,) = call(
        pack_kernel,
        "pack",
        [block5],
        qkv_time[:, 0, 0],
        cot_out[0, 0],
    )
    there = [
        ((2 * c + z0) * X + x, (z0 * X + x) * X + c)
        for c in range(X)
        for z0 in range(2)
        for x in range(X)
    ]
    near = [(a, b ^ X) for a, b in there]
    rows8 = jnp.pad(w_out, ((0, 2), (0, 0)))
    held = [lax.ppermute(rows8, ("z", "x"), p) for p in (there, near)]
    packed, *held = lax.optimization_barrier((packed, *held))
    recv = lax.all_to_all(packed, SEQ, 0, 0, tiled=True)
    held = jnp.concatenate(held)
    held = jnp.concatenate([held, hop(held, "z", 2, Z)])
    held = jnp.concatenate([held, hop(held, "z", 4, Z)])

    (up,) = call(
        compact_kernel, "compact", [((F, HALF, DW), bf)], shard_sizes, recv, smem=1, flops=100_000_000
    )
    held, up = lax.optimization_barrier((held, up))
    up = lax.all_to_all(up, SEQ, 0, 0, tiled=True)
    held = jnp.concatenate([held] + [hop(held, "y", k, Y) for k in range(1, Y)])
    recv, held = lax.optimization_barrier((recv, held))
    held2 = hop(held, "core", 1, C)

    probs, mixed = call(
        fwd_kernel,
        "attn_fwd",
        [((HL, NB, POS, POS), f32), ((F * HALF, COLS), bf)],
        place,
        bias_time,
        LEAVE,
        recv,
        smem=2,
        scratch=[pltpu.VMEM((F, HALF, COLS), bf)],
        flops=250_000_000,
    )

    mine, theirs, dm, ds, sums = call(
        score_kernel,
        "scores_bwd",
        [
            ((COLS // 2, DW), f32),
            ((COLS // 2, DW), bf),
            ((F, HALF, COLS), bf),
            ((HL, NB, POS, POS), bf),
            ((F, COLS), f32),
        ],
        place,
        ROWS_OF,
        recv,
        probs,
        mixed,
        up,
        held,
        held2,
        smem=1,
        flops=1_500_000_000,
    )
    theirs = hop(theirs, "core", 1, C)
    sums2 = hop(sums, "core", 1, C)

    pieces = call(
        grad_kernel,
        "grads",
        [((3, HALF, COLS), bf)] * F,
        place,
        recv,
        probs,
        dm,
        ds,
        smem=1,
        scratch=[pltpu.VMEM((F, 3, HALF, COLS), bf)],
        flops=150_000_000,
    )

    (msgs,) = call(join_kernel, "join", [((Z * Y, 8, DW), bf)], mine, theirs, sums, sums2)
    msgs, *pieces = lax.optimization_barrier((msgs, *pieces))
    msgs = lax.all_to_all(msgs, ("z", "y"), 0, 0, tiled=True)
    pieces = pieces[:1] + [hop(p, SEQ, k, F) for k, p in enumerate(pieces[1:], 1)]
    msgs, *pieces = lax.optimization_barrier((msgs, *pieces))
    total, off = call(total_kernel, "total", [((8, DW), f32), ((16, 128), f32)], msgs)
    home = lax.ppermute(total, ("z", "x"), [(b, a) for a, b in there])
    off = lax.all_to_all(jnp.broadcast_to(off, (X, 16, 128)), "x", 0, 0, tiled=True)
    (grad_qkv,) = call(
        unpack_kernel,
        "unpack",
        [((3, POS, DW), bf)],
        place,
        *pieces,
        smem=1,
        scratch=[pltpu.VMEM((F, 3, HALF, COLS), bf)],
    )
    grad_qkv = grad_qkv.reshape(3, 1, 1, POS, DW)
    home, grad_qkv = lax.optimization_barrier((home, grad_qkv))
    grad_w_out, grad_bias = call(
        last_kernel, "last", [((6, DW), f32), ((12, 15), f32)], home, off
    )
    return grad_qkv, grad_bias, grad_w_out


def solution(mesh):
    grid = Mesh(mesh.devices.reshape(Z, Y, X, C), ("z", "y", "x", "core"))
    dp, every = ("z", "y"), ("z", "y", "x", "core")
    return jax.shard_map(
        per_device,
        mesh=grid,
        in_specs=(
            P(None, dp, SEQ, None, None),
            P(dp, None),
            P(),
            P(every, None),
            P(dp, SEQ, None, None, None),
        ),
        out_specs=(P(None, dp, SEQ, None, None), P(), P(every, None)),
        check_vma=False,
    )
```

```python
import math

import jax
import jax.numpy as jnp
import numpy as np
from jax import lax
from jax.experimental import pallas as pl
from jax.experimental.pallas import tpu as pltpu
from jax.sharding import Mesh, PartitionSpec as P

Z, Y, X, C = 8, 4, 4, 2
SEQ = ("x", "core")
F = 8
POS = 128
HALF = 64
NB = 4
HL = 3
HD = 128
COLS = HL * HD
DW = 1536
CAP = 32
FACTOR = 1.0 / math.sqrt(HD)
NN = (((1,), (0,)), ((), ()))
NT = (((1,), (1,)), ((), ()))
TN = (((0,), (0,)), ((), ()))
bf, f32 = jnp.bfloat16, jnp.float32
CORE, YI, ZI, XI, RANK = range(5)

ROW = np.arange(COLS)
ROWS_OF = np.zeros((8, COLS), np.int32)
ROWS_OF[0] = ROW // 6 % 2
ROWS_OF[1] = ROW // 48 % 4
ROWS_OF[2] = ROW // 192 * 4 + ROW // 12 % 4
ROWS_OF[3] = ROW % 6
LEAVE = np.zeros((8, COLS), np.int32)
LEAVE[0] = ROW // 192
SUB = ROW % 192 // 6
LEAVE[1] = ((SUB // 16 * 4 + SUB % 4) * 8 + SUB // 4 % 4 * 2) * 6 + ROW % 6


def dot(a, b, dims, **kw):
    return lax.dot_general(a, b, dims, preferred_element_type=f32, **kw)


def iota(shape, dim):
    return lax.broadcasted_iota(jnp.int32, shape, dim)


def call(body, name, outs, *ins, smem=0, scratch=(), flops=0, space=pltpu.VMEM, vmem=16):
    total = sum(math.prod(s) * jnp.dtype(d).itemsize for s, d in outs)
    total += sum(a.size * a.dtype.itemsize for a in ins)
    specs = [pl.BlockSpec(memory_space=pltpu.SMEM)] * smem
    specs += [pl.BlockSpec(memory_space=space)] * (len(ins) - smem)
    return pl.pallas_call(
        body,
        out_shape=tuple(jax.ShapeDtypeStruct(s, d) for s, d in outs),
        in_specs=specs,
        out_specs=tuple(pl.BlockSpec(memory_space=space) for _ in outs),
        scratch_shapes=list(scratch),
        compiler_params=pltpu.CompilerParams(vmem_limit_bytes=vmem << 20),
        cost_estimate=pl.CostEstimate(flops=flops, bytes_accessed=total, transcendentals=0),
        name=name,
    )(*ins)


def stack_kernel(*refs):
    out_ref, row = refs[-1], 0
    for ref in refs[:-1]:
        out_ref[row : row + HALF] = ref[...]
        row += HALF


def stack(parts):
    return call(stack_kernel, "stack", [((len(parts) * HALF, DW), bf)], *parts)[0]


def pack_kernel(qkv_ref, out_ref):
    for d in range(F):
        r, c = d % C * HALF, d // C * COLS
        out_ref[d] = qkv_ref[:, r : r + HALF, c : c + COLS]


def compact_kernel(place, sizes, cot_ref, same_ref, other_ref):
    shape = (POS, F * CAP)
    row, col = iota(shape, 0), iota(shape, 1)
    pos = row ^ (place[CORE] * HALF)
    start = jnp.int32(0)
    picked = jnp.full(shape, -1, jnp.int32)
    for j in range(F):
        slot = col - j * CAP
        inside = (slot >= 0) & (slot < sizes[0, j])
        picked = jnp.where(inside, slot + start, picked)
        start = start + sizes[0, j]
    hot = (picked == pos).astype(f32).astype(bf)
    up = dot(hot, cot_ref[...].reshape(F * CAP, DW), NN).astype(bf)
    same_ref[...] = up[:HALF]
    other_ref[...] = up[HALF:]


def block(ref, i, b, h):
    return ref[:, i, b * 16 : (b + 1) * 16, h * HD : (h + 1) * HD].reshape(POS, HD)


def fwd_kernel(place, bias, leave_ref, qkv_ref, probs_ref, mixed_ref, raw_ref):
    row, col = iota((POS, POS), 0), iota((POS, POS), 1)
    alike = (row & 15) == (col & 15)
    offset = (col >> 4) - (row >> 4) + 7
    for h in range(HL):
        pair = jnp.full((POS, POS), -1e30, f32)
        for o in range(15):
            pair = jnp.where(alike & (offset == o), bias[place[XI] * HL + h, o], pair)
        for b in range(NB):
            q, k, v = (block(qkv_ref, i, b, h) for i in range(3))
            s = dot(q, k, NT) * FACTOR + pair
            e = jnp.exp(s - jnp.max(s, axis=-1, keepdims=True))
            p = e / jnp.sum(e, axis=-1, keepdims=True)
            probs_ref[h, b] = p
            m = dot(p.astype(bf), v, NN).astype(bf).reshape(F, 16, HD)
            raw_ref[:, b * 16 : (b + 1) * 16, h * HD : (h + 1) * HD] = m
    source = leave_ref[1:2] + (leave_ref[0:1] ^ place[CORE]) * 6
    order = (iota((COLS, COLS), 0) == source).astype(f32).astype(bf)
    mixed_ref[...] = dot(raw_ref[...].reshape(F * HALF, COLS), order, NN).astype(bf)


def score_kernel(place, rows_ref, recv_ref, probs_ref, mixed_ref, u0, u1, u3, q1, q3, w0_ref, w1_ref, *outs):
    mine_ref, other_ref, dm_ref, ds_ref, sums_ref, up_ref = outs
    halves = [(0, u0[:HALF], u0[HALF:]), (1, u1[:HALF], u1[HALF:])]
    halves += [(2, q1[...], q3[...]), (3, u3[:HALF], u3[HALF:])]
    for k, same, other in halves:
        chip = (place[XI] ^ k) * C
        up_ref[chip + place[CORE]] = same
        up_ref[chip + 1 - place[CORE]] = other
    up = up_ref[...].reshape(F * HALF, DW)
    gw = dot(mixed_ref[...], up, TN)
    mine_ref[...] = gw[: COLS // 2]
    other_ref[...] = gw[COLS // 2 :].astype(bf)
    dm = jnp.concatenate([dot(up, w[...], NT).astype(bf) for w in (w0_ref, w1_ref)], axis=1)
    c, y, j = (rows_ref[n : n + 1] ^ place[n] for n in (CORE, YI, ZI))
    spot = ((c * Y + y) * Z + j) * 8 + rows_ref[3:4]
    spot = (iota((512, COLS), 0) == spot).astype(f32).astype(bf)
    dm = dot(dm, spot, NN)
    dm_ref[...] = dm.astype(bf).reshape(F, HALF, COLS)
    for h in range(HL):
        cols = slice(h * HD, (h + 1) * HD)
        total = jnp.zeros((F, POS), f32)
        for b in range(NB):
            d = dm_ref[:, b * 16 : (b + 1) * 16, cols].reshape(POS, HD)
            p = probs_ref[h, b]
            g = dot(d, block(recv_ref, 2, b, h), NT)
            ds = p * (g - jnp.sum(p * g, axis=-1, keepdims=True))
            total = total + jnp.sum(ds.reshape(F, 16, POS), axis=1)
            ds_ref[h, b] = ds.astype(bf)
        sums_ref[:, cols] = total


def grad_kernel(place, qkv_ref, probs_ref, dm_ref, ds_ref, *refs):
    pieces, nat_ref = refs[:F], refs[F]
    for h in range(HL):
        cols = slice(h * HD, (h + 1) * HD)
        for b in range(NB):
            rows = slice(b * 16, (b + 1) * 16)
            d = dm_ref[:, rows, cols].reshape(POS, HD)
            low = ds_ref[h, b]
            gq = dot(low, block(qkv_ref, 1, b, h), NN) * FACTOR
            gk = dot(low, block(qkv_ref, 0, b, h), TN) * FACTOR
            gv = dot(probs_ref[h, b].astype(bf), d, TN)
            for i, val in enumerate((gq, gk, gv)):
                nat_ref[:, i, rows, cols] = val.astype(bf).reshape(F, 16, HD)
    for k in range(F):
        pieces[k][...] = nat_ref[place[RANK] ^ k]


def unpack_kernel(place, *refs):
    pieces, out_ref, nat_ref = refs[:F], refs[F], refs[F + 1]
    for k in range(F):
        nat_ref[place[RANK] ^ k] = pieces[k][...]
    for d in range(F):
        r, c = d % C * HALF, d // C * COLS
        out_ref[:, r : r + HALF, c : c + COLS] = nat_ref[d]


def split(b):
    high = b.astype(bf).astype(f32)
    low = (b - high).astype(bf).astype(f32)
    return high, low


def join_kernel(mine_ref, other_ref, s0, s1, out_ref):
    gw = mine_ref[...] + other_ref[...].astype(f32)
    hot = ((iota((COLS, 128), 0) >> 4) == iota((COLS, 128), 1)).astype(f32)
    b = dot(s0[...] + s1[...], hot, NN, precision=lax.Precision.HIGHEST)
    ride = jnp.concatenate([x[:, :64] for x in split(b)], axis=1)
    for d in range(Z * Y):
        part = gw[6 * d : 6 * d + 6]
        ends = [
            jnp.concatenate([part[r + i : r + i + 1, 1152:] for i in range(3)], axis=1) for r in (0, 3)
        ]
        part = jnp.concatenate([part[:, :1152]] + ends, axis=0)
        out_ref[d] = jnp.concatenate([part, ride], axis=1).astype(bf)


def total_kernel(in_ref, sum_ref, off_ref):
    total = jnp.sum(in_ref[...].astype(f32), axis=0)
    sum_ref[:, :1152] = total[:, :1152]
    for r in range(6):
        sum_ref[r : r + 1, 1152:] = total[6 + r // 3 : 7 + r // 3, r % 3 * 384 : (r % 3 + 1) * 384]
    sum_ref[6:, 1152:] = jnp.zeros((2, 384), f32)
    sums = total[:, 1152:1216] + total[:, 1216:]
    head, lane = iota((16, 64), 0) % HL, iota((16, 64), 1)
    g, o = iota((64, 128), 0) & 7, iota((64, 128), 1)
    out = jnp.zeros((16, 128), f32)
    for f in range(F):
        row = jnp.where((lane >> 3) == head, sums[f : f + 1], 0.0)
        out = out + dot(row, (g - f + 7 == o).astype(f32), NN, precision=lax.Precision.HIGHEST)
    off_ref[...] = out


def last_kernel(place, home_ref, o0, o1, o2, o3, gw_ref, bias_ref):
    gw_ref[...] = home_ref[:6]
    row = iota((16, 128), 0) // HL
    out = jnp.zeros((16, 128), f32)
    for k, o in enumerate((o0, o1, o2, o3)):
        out = out + jnp.where(row == (place[XI] ^ k), o[...], 0.0)
    bias_ref[...] = out[:12, :15]


def hop(x, axis, k, n):
    return lax.ppermute(x, axis, [(i, i ^ k) for i in range(n)])


def per_device(qkv_time, shard_sizes, bias_time, w_out, cot_out):
    xi, yi, zi, core = (lax.axis_index(a) for a in ("x", "y", "z", "core"))
    place = jnp.stack([core, yi, zi, xi, xi * C + core]).astype(jnp.int32)

    there = [
        ((2 * c + z0) * X + x, (z0 * X + x) * X + c)
        for c in range(X)
        for z0 in range(2)
        for x in range(X)
    ]
    near = [(a, b ^ X) for a, b in there]
    rows8 = jnp.pad(w_out, ((0, 2), (0, 0)))
    held = [lax.ppermute(rows8, ("z", "x"), p) for p in (there, near)]
    cot, *held = lax.optimization_barrier((cot_out[0, 0], *held))

    cot = lax.all_to_all(cot, SEQ, 0, 0, tiled=True)
    (packed,) = call(pack_kernel, "pack", [((F, 3, HALF, COLS), bf)], qkv_time[:, 0, 0])
    held = jnp.concatenate(held)
    held = jnp.concatenate([held, hop(held, "z", 2, Z)])
    held = jnp.concatenate([held, hop(held, "z", 4, Z)])
    packed, held = lax.optimization_barrier((packed, held))
    recv = lax.all_to_all(packed, SEQ, 0, 0, tiled=True)

    same, other = call(
        compact_kernel,
        "compact",
        [((HALF, DW), bf)] * 2,
        place,
        shard_sizes,
        cot,
        smem=2,
        flops=100_000_000,
    )
    u0 = stack([same, hop(other, "core", 1, C)])
    held, u0 = lax.optimization_barrier((held, u0))
    u1, u3 = hop(u0, "x", 1, X), hop(u0, "x", 3, X)
    held = [held] + [hop(held, "y", k, Y) for k in range(1, Y)]

    far = u3[:HALF], u1[HALF:]
    held, far = lax.optimization_barrier((held, far))
    q1, q3 = hop(far[0], "x", 1, X), hop(far[1], "x", 3, X)
    held = stack(held)
    held2 = hop(held, "core", 1, C)

    probs, mixed = call(
        fwd_kernel,
        "attn_fwd",
        [((HL, NB, POS, POS), f32), ((F * HALF, COLS), bf)],
        place,
        bias_time,
        LEAVE,
        recv,
        smem=2,
        scratch=[pltpu.VMEM((F, HALF, COLS), bf)],
        flops=20_000_000_000,
    )

    mine, theirs, dm, ds, sums = call(
        score_kernel,
        "scores_bwd",
        [
            ((COLS // 2, DW), f32),
            ((COLS // 2, DW), bf),
            ((F, HALF, COLS), bf),
            ((HL, NB, POS, POS), bf),
            ((F, COLS), f32),
        ],
        place,
        ROWS_OF,
        recv,
        probs,
        mixed,
        u0,
        u1,
        u3,
        q1,
        q3,
        held,
        held2,
        smem=1,
        scratch=[pltpu.VMEM((F, HALF, DW), bf)],
        flops=1_500_000_000,
    )
    theirs = hop(theirs, "core", 1, C)
    sums2 = hop(sums, "core", 1, C)

    pieces = call(
        grad_kernel,
        "grads",
        [((3, HALF, COLS), bf)] * F,
        place,
        recv,
        probs,
        dm,
        ds,
        smem=1,
        scratch=[pltpu.VMEM((F, 3, HALF, COLS), bf)],
        flops=150_000_000,
    )

    (msgs,) = call(join_kernel, "join", [((Z * Y, 8, 1280), bf)], mine, theirs, sums, sums2)
    msgs, *pieces = lax.optimization_barrier((msgs, *pieces))
    msgs = lax.all_to_all(msgs, ("z", "y"), 0, 0, tiled=True)
    pieces = pieces[:1] + [hop(p, SEQ, k, F) for k, p in enumerate(pieces[1:], 1)]
    msgs, *pieces[1:6] = lax.optimization_barrier((msgs, *pieces[1:6]))
    total, off = call(total_kernel, "total", [((8, DW), f32), ((16, 128), f32)], msgs)
    home = lax.ppermute(total, ("z", "x"), [(b, a) for a, b in there])
    offs = [off] + [hop(off, "x", k, X) for k in range(1, X)]
    (grad_qkv,) = call(
        unpack_kernel,
        "unpack",
        [((3, POS, DW), bf)],
        place,
        *pieces,
        smem=1,
        scratch=[pltpu.VMEM((F, 3, HALF, COLS), bf)],
    )
    grad_qkv = grad_qkv.reshape(3, 1, 1, POS, DW)
    home, grad_qkv = lax.optimization_barrier((home, grad_qkv))
    grad_w_out, grad_bias = call(
        last_kernel, "last", [((6, DW), f32), ((12, 15), f32)], place, home, *offs, smem=1
    )
    return grad_qkv, grad_bias, grad_w_out


def solution(mesh):
    grid = Mesh(mesh.devices.reshape(Z, Y, X, C), ("z", "y", "x", "core"))
    dp, every = ("z", "y"), ("z", "y", "x", "core")
    return jax.shard_map(
        per_device,
        mesh=grid,
        in_specs=(
            P(None, dp, SEQ, None, None),
            P(dp, None),
            P(),
            P(every, None),
            P(dp, SEQ, None, None, None),
        ),
        out_specs=(P(None, dp, SEQ, None, None), P(), P(every, None)),
        check_vma=False,
    )
```

```python
import math

import jax
import jax.numpy as jnp
import numpy as np
from jax import lax
from jax.experimental import pallas as pl
from jax.experimental.pallas import tpu as pltpu
from jax.sharding import Mesh, PartitionSpec as P

Z, Y, X, C = 8, 4, 4, 2
SEQ = ("x", "core")
F = 8
POS = 128
HALF = 64
NB = 4
HL = 3
HD = 128
COLS = HL * HD
DW = 1536
CAP = 32
FACTOR = 1.0 / math.sqrt(HD)
NN = (((1,), (0,)), ((), ()))
NT = (((1,), (1,)), ((), ()))
TN = (((0,), (0,)), ((), ()))
bf, f32 = jnp.bfloat16, jnp.float32
CORE, YI, ZI, XI, RANK = range(5)

ROW = np.arange(COLS)
ROWS_OF = np.zeros((8, COLS), np.int32)
ROWS_OF[0] = ROW // 6 % 2
ROWS_OF[1] = ROW // 48 % 4
ROWS_OF[2] = ROW // 192 * 4 + ROW // 12 % 4
ROWS_OF[3] = ROW % 6
LEAVE = np.zeros((8, COLS), np.int32)
LEAVE[0] = ROW // 192
SUB = ROW % 192 // 6
LEAVE[1] = ((SUB // 16 * 4 + SUB % 4) * 8 + SUB // 4 % 4 * 2) * 6 + ROW % 6


def dot(a, b, dims, **kw):
    return lax.dot_general(a, b, dims, preferred_element_type=f32, **kw)


def iota(shape, dim):
    return lax.broadcasted_iota(jnp.int32, shape, dim)


def call(body, name, outs, *ins, smem=0, scratch=(), flops=0, space=pltpu.VMEM, vmem=16):
    total = sum(math.prod(s) * jnp.dtype(d).itemsize for s, d in outs)
    total += sum(a.size * a.dtype.itemsize for a in ins)
    specs = [pl.BlockSpec(memory_space=pltpu.SMEM)] * smem
    specs += [pl.BlockSpec(memory_space=space)] * (len(ins) - smem)
    return pl.pallas_call(
        body,
        out_shape=tuple(jax.ShapeDtypeStruct(s, d) for s, d in outs),
        in_specs=specs,
        out_specs=tuple(pl.BlockSpec(memory_space=space) for _ in outs),
        scratch_shapes=list(scratch),
        compiler_params=pltpu.CompilerParams(vmem_limit_bytes=vmem << 20),
        cost_estimate=pl.CostEstimate(flops=flops, bytes_accessed=total, transcendentals=0),
        name=name,
    )(*ins)


def stack_kernel(*refs):
    out_ref, row = refs[-1], 0
    for ref in refs[:-1]:
        out_ref[row : row + HALF] = ref[...]
        row += HALF


def stack(parts):
    return call(stack_kernel, "stack", [((len(parts) * HALF, DW), bf)], *parts)[0]


def pack_kernel(qkv_ref, out_ref):
    for d in range(F):
        r, c = d % C * HALF, d // C * COLS
        out_ref[d] = qkv_ref[:, r : r + HALF, c : c + COLS]


def compact_kernel(place, sizes, cot_ref, same_ref, other_ref):
    shape = (POS, F * CAP)
    row, col = iota(shape, 0), iota(shape, 1)
    pos = row ^ (place[CORE] * HALF)
    start = jnp.int32(0)
    picked = jnp.full(shape, -1, jnp.int32)
    for j in range(F):
        slot = col - j * CAP
        inside = (slot >= 0) & (slot < sizes[0, j])
        picked = jnp.where(inside, slot + start, picked)
        start = start + sizes[0, j]
    hot = (picked == pos).astype(f32).astype(bf)
    up = dot(hot, cot_ref[...].reshape(F * CAP, DW), NN).astype(bf)
    same_ref[...] = up[:HALF]
    other_ref[...] = up[HALF:]


def block(ref, i, b, h):
    return ref[:, i, b * 16 : (b + 1) * 16, h * HD : (h + 1) * HD].reshape(POS, HD)


def fwd_kernel(place, bias, leave_ref, qkv_ref, probs_ref, mixed_ref, raw_ref):
    row, col = iota((POS, POS), 0), iota((POS, POS), 1)
    alike = (row & 15) == (col & 15)
    offset = (col >> 4) - (row >> 4) + 7
    for h in range(HL):
        pair = jnp.full((POS, POS), -1e30, f32)
        for o in range(15):
            pair = jnp.where(alike & (offset == o), bias[place[XI] * HL + h, o], pair)
        for b in range(NB):
            q, k, v = (block(qkv_ref, i, b, h) for i in range(3))
            s = dot(q, k, NT) * FACTOR + pair
            e = jnp.exp(s - jnp.max(s, axis=-1, keepdims=True))
            p = e / jnp.sum(e, axis=-1, keepdims=True)
            probs_ref[h, b] = p
            m = dot(p.astype(bf), v, NN).astype(bf).reshape(F, 16, HD)
            raw_ref[:, b * 16 : (b + 1) * 16, h * HD : (h + 1) * HD] = m
    source = leave_ref[1:2] + (leave_ref[0:1] ^ place[CORE]) * 6
    order = (iota((COLS, COLS), 0) == source).astype(f32).astype(bf)
    mixed_ref[...] = dot(raw_ref[...].reshape(F * HALF, COLS), order, NN).astype(bf)


def gw_kernel(place, mixed_ref, u0, u1, u2, u3, mine_ref, other_ref, up_ref):
    for k, ref in enumerate((u0, u1, u2, u3)):
        chip = (place[XI] ^ k) * C
        up_ref[chip + place[CORE]] = ref[:HALF]
        up_ref[chip + 1 - place[CORE]] = ref[HALF:]
    gw = dot(mixed_ref[...], up_ref[...].reshape(F * HALF, DW), TN)
    mine_ref[...] = gw[: COLS // 2]
    other_ref[...] = gw[COLS // 2 :].astype(bf)


def score_kernel(place, rows_ref, recv_ref, probs_ref, up_ref, w0_ref, w1_ref, dm_ref, ds_ref, sums_ref):
    up = up_ref[...].reshape(F * HALF, DW)
    dm = jnp.concatenate([dot(up, w[...], NT).astype(bf) for w in (w0_ref, w1_ref)], axis=1)
    c, y, j = (rows_ref[n : n + 1] ^ place[n] for n in (CORE, YI, ZI))
    spot = ((c * Y + y) * Z + j) * 8 + rows_ref[3:4]
    spot = (iota((512, COLS), 0) == spot).astype(f32).astype(bf)
    dm = dot(dm, spot, NN)
    dm_ref[...] = dm.astype(bf).reshape(F, HALF, COLS)
    for h in range(HL):
        cols = slice(h * HD, (h + 1) * HD)
        total = jnp.zeros((F, POS), f32)
        for b in range(NB):
            d = dm_ref[:, b * 16 : (b + 1) * 16, cols].reshape(POS, HD)
            p = probs_ref[h, b]
            g = dot(d, block(recv_ref, 2, b, h), NT)
            ds = p * (g - jnp.sum(p * g, axis=-1, keepdims=True))
            total = total + jnp.sum(ds.reshape(F, 16, POS), axis=1)
            ds_ref[h, b] = ds.astype(bf)
        sums_ref[:, cols] = total


def grad_kernel(place, qkv_ref, probs_ref, dm_ref, ds_ref, *refs):
    pieces, nat_ref = refs[:F], refs[F]
    for h in range(HL):
        cols = slice(h * HD, (h + 1) * HD)
        for b in range(NB):
            rows = slice(b * 16, (b + 1) * 16)
            d = dm_ref[:, rows, cols].reshape(POS, HD)
            low = ds_ref[h, b]
            gq = dot(low, block(qkv_ref, 1, b, h), NN) * FACTOR
            gk = dot(low, block(qkv_ref, 0, b, h), TN) * FACTOR
            gv = dot(probs_ref[h, b].astype(bf), d, TN)
            for i, val in enumerate((gq, gk, gv)):
                nat_ref[:, i, rows, cols] = val.astype(bf).reshape(F, 16, HD)
    for k in range(F):
        pieces[k][...] = nat_ref[place[RANK] ^ k]


def unpack_kernel(place, *refs):
    pieces, out_ref, nat_ref = refs[:F], refs[F], refs[F + 1]
    for k in range(F):
        nat_ref[place[RANK] ^ k] = pieces[k][...]
    for d in range(F):
        r, c = d % C * HALF, d // C * COLS
        out_ref[:, r : r + HALF, c : c + COLS] = nat_ref[d]


def split(b):
    high = b.astype(bf).astype(f32)
    low = (b - high).astype(bf).astype(f32)
    return high, low


def join_kernel(mine_ref, other_ref, s0, s1, out_ref):
    gw = mine_ref[...] + other_ref[...].astype(f32)
    hot = ((iota((COLS, 128), 0) >> 4) == iota((COLS, 128), 1)).astype(f32)
    b = dot(s0[...] + s1[...], hot, NN, precision=lax.Precision.HIGHEST)
    ride = jnp.concatenate([x[:, :64] for x in split(b)], axis=1)
    for d in range(Z * Y):
        part = gw[6 * d : 6 * d + 6]
        ends = [
            jnp.concatenate([part[r + i : r + i + 1, 1152:] for i in range(3)], axis=1) for r in (0, 3)
        ]
        part = jnp.concatenate([part[:, :1152]] + ends, axis=0)
        out_ref[d] = jnp.concatenate([part, ride], axis=1).astype(bf)


def total_kernel(in_ref, sum_ref, off_ref):
    total = jnp.sum(in_ref[...].astype(f32), axis=0)
    sum_ref[:, :1152] = total[:, :1152]
    for r in range(6):
        sum_ref[r : r + 1, 1152:] = total[6 + r // 3 : 7 + r // 3, r % 3 * 384 : (r % 3 + 1) * 384]
    sum_ref[6:, 1152:] = jnp.zeros((2, 384), f32)
    sums = total[:, 1152:1216] + total[:, 1216:]
    head, lane = iota((16, 64), 0) % HL, iota((16, 64), 1)
    g, o = iota((64, 128), 0) & 7, iota((64, 128), 1)
    out = jnp.zeros((16, 128), f32)
    for f in range(F):
        row = jnp.where((lane >> 3) == head, sums[f : f + 1], 0.0)
        out = out + dot(row, (g - f + 7 == o).astype(f32), NN, precision=lax.Precision.HIGHEST)
    off_ref[...] = out


def last_kernel(place, home_ref, o0, o1, o2, o3, gw_ref, bias_ref):
    gw_ref[...] = home_ref[:6]
    row = iota((16, 128), 0) // HL
    out = jnp.zeros((16, 128), f32)
    for k, o in enumerate((o0, o1, o2, o3)):
        out = out + jnp.where(row == (place[XI] ^ k), o[...], 0.0)
    bias_ref[...] = out[:12, :15]


def hop(x, axis, k, n):
    return lax.ppermute(x, axis, [(i, i ^ k) for i in range(n)])


def per_device(qkv_time, shard_sizes, bias_time, w_out, cot_out):
    xi, yi, zi, core = (lax.axis_index(a) for a in ("x", "y", "z", "core"))
    place = jnp.stack([core, yi, zi, xi, xi * C + core]).astype(jnp.int32)

    there = [
        ((2 * c + z0) * X + x, (z0 * X + x) * X + c)
        for c in range(X)
        for z0 in range(2)
        for x in range(X)
    ]
    near = [(a, b ^ X) for a, b in there]
    cot = lax.all_to_all(cot_out[0, 0], SEQ, 0, 0, tiled=True)
    (packed,) = call(pack_kernel, "pack", [((F, 3, HALF, COLS), bf)], qkv_time[:, 0, 0])
    rows8, packed = lax.optimization_barrier((jnp.pad(w_out, ((0, 2), (0, 0))), packed))
    held = [lax.ppermute(rows8, ("z", "x"), p) for p in (there, near)]
    held = jnp.concatenate(held)
    held = jnp.concatenate([held, hop(held, "z", 2, Z)])
    packed, held = lax.optimization_barrier((packed, held))
    recv = lax.all_to_all(packed, SEQ, 0, 0, tiled=True)

    same, other = call(
        compact_kernel,
        "compact",
        [((HALF, DW), bf)] * 2,
        place,
        shard_sizes,
        cot,
        smem=2,
        flops=100_000_000,
    )
    held, same = lax.optimization_barrier((held, same))
    held = jnp.concatenate([held, hop(held, "z", 4, Z)])
    u0 = stack([same, hop(other, "core", 1, C)])
    held, u0 = lax.optimization_barrier((held, u0))
    ups = [u0] + [hop(u0, "x", k, X) for k in range(1, X)]
    held = [held] + [hop(held, "y", k, Y) for k in range(1, Y)]
    held, ups[1], ups[3] = lax.optimization_barrier((held, ups[1], ups[3]))
    held = stack(held)
    held2 = hop(held, "core", 1, C)

    probs, mixed = call(
        fwd_kernel,
        "attn_fwd",
        [((HL, NB, POS, POS), f32), ((F * HALF, COLS), bf)],
        place,
        bias_time,
        LEAVE,
        recv,
        smem=2,
        scratch=[pltpu.VMEM((F, HALF, COLS), bf)],
        flops=20_000_000_000,
    )

    mine, theirs, up = call(
        gw_kernel,
        "grad_w",
        [((COLS // 2, DW), f32), ((COLS // 2, DW), bf), ((F, HALF, DW), bf)],
        place,
        mixed,
        *ups,
        smem=1,
        flops=20_000_000_000,
    )
    dm, ds, sums = call(
        score_kernel,
        "scores_bwd",
        [((F, HALF, COLS), bf), ((HL, NB, POS, POS), bf), ((F, COLS), f32)],
        place,
        ROWS_OF,
        recv,
        probs,
        up,
        held,
        held2,
        smem=1,
        flops=900_000_000,
    )
    theirs = hop(theirs, "core", 1, C)
    sums2 = hop(sums, "core", 1, C)

    pieces = call(
        grad_kernel,
        "grads",
        [((3, HALF, COLS), bf)] * F,
        place,
        recv,
        probs,
        dm,
        ds,
        smem=1,
        scratch=[pltpu.VMEM((F, 3, HALF, COLS), bf)],
        flops=150_000_000,
    )

    (msgs,) = call(join_kernel, "join", [((Z * Y, 8, 1280), bf)], mine, theirs, sums, sums2)
    msgs, *pieces = lax.optimization_barrier((msgs, *pieces))
    msgs = lax.all_to_all(msgs, ("z", "y"), 0, 0, tiled=True)
    pieces = pieces[:1] + [hop(p, SEQ, k, F) for k, p in enumerate(pieces[1:], 1)]
    msgs, *pieces[1:6] = lax.optimization_barrier((msgs, *pieces[1:6]))
    total, off = call(total_kernel, "total", [((8, DW), f32), ((16, 128), f32)], msgs)
    home = lax.ppermute(total, ("z", "x"), [(b, a) for a, b in there])
    offs = [off] + [hop(off, "x", k, X) for k in range(1, X)]
    (grad_qkv,) = call(
        unpack_kernel,
        "unpack",
        [((3, POS, DW), bf)],
        place,
        *pieces,
        smem=1,
        scratch=[pltpu.VMEM((F, 3, HALF, COLS), bf)],
    )
    grad_qkv = grad_qkv.reshape(3, 1, 1, POS, DW)
    home, grad_qkv = lax.optimization_barrier((home, grad_qkv))
    grad_w_out, grad_bias = call(
        last_kernel, "last", [((6, DW), f32), ((12, 15), f32)], place, home, *offs, smem=1
    )
    return grad_qkv, grad_bias, grad_w_out


def solution(mesh):
    grid = Mesh(mesh.devices.reshape(Z, Y, X, C), ("z", "y", "x", "core"))
    dp, every = ("z", "y"), ("z", "y", "x", "core")
    return jax.shard_map(
        per_device,
        mesh=grid,
        in_specs=(
            P(None, dp, SEQ, None, None),
            P(dp, None),
            P(),
            P(every, None),
            P(dp, SEQ, None, None, None),
        ),
        out_specs=(P(None, dp, SEQ, None, None), P(), P(every, None)),
        check_vma=False,
    )
```

```python
import math

import jax
import jax.numpy as jnp
import numpy as np
from jax import lax
from jax.experimental import pallas as pl
from jax.experimental.pallas import tpu as pltpu
from jax.sharding import Mesh, PartitionSpec as P

Z, Y, X, C = 8, 4, 4, 2
SEQ = ("x", "core")
F = 8
POS = 128
HALF = 64
NB = 4
HL = 3
HD = 128
COLS = HL * HD
DW = 1536
CAP = 32
FACTOR = 1.0 / math.sqrt(HD)
NN = (((1,), (0,)), ((), ()))
NT = (((1,), (1,)), ((), ()))
TN = (((0,), (0,)), ((), ()))
bf, f32 = jnp.bfloat16, jnp.float32
CORE, YI, ZI, XI, RANK = range(5)

ROW = np.arange(COLS)
ROWS_OF = np.zeros((8, COLS), np.int32)
ROWS_OF[0] = ROW // 6 % 2
ROWS_OF[1] = ROW // 48 % 4
ROWS_OF[2] = ROW // 192 * 4 + ROW // 12 % 4
ROWS_OF[3] = ROW % 6
LEAVE = np.zeros((8, COLS), np.int32)
LEAVE[0] = ROW // 192
SUB = ROW % 192 // 6
LEAVE[1] = ((SUB // 16 * 4 + SUB % 4) * 8 + SUB // 4 % 4 * 2) * 6 + ROW % 6


def dot(a, b, dims, **kw):
    return lax.dot_general(a, b, dims, preferred_element_type=f32, **kw)


def iota(shape, dim):
    return lax.broadcasted_iota(jnp.int32, shape, dim)


def call(body, name, outs, *ins, smem=0, scratch=(), flops=0, space=pltpu.VMEM, vmem=16):
    total = sum(math.prod(s) * jnp.dtype(d).itemsize for s, d in outs)
    total += sum(a.size * a.dtype.itemsize for a in ins)
    specs = [pl.BlockSpec(memory_space=pltpu.SMEM)] * smem
    specs += [pl.BlockSpec(memory_space=space)] * (len(ins) - smem)
    return pl.pallas_call(
        body,
        out_shape=tuple(jax.ShapeDtypeStruct(s, d) for s, d in outs),
        in_specs=specs,
        out_specs=tuple(pl.BlockSpec(memory_space=space) for _ in outs),
        scratch_shapes=list(scratch),
        compiler_params=pltpu.CompilerParams(vmem_limit_bytes=vmem << 20),
        cost_estimate=pl.CostEstimate(flops=flops, bytes_accessed=total, transcendentals=0),
        name=name,
    )(*ins)


def stack_kernel(*refs):
    out_ref, row = refs[-1], 0
    for ref in refs[:-1]:
        rows = ref.shape[0]
        out_ref[row : row + rows] = ref[...]
        row += rows


def stack(parts):
    rows = sum(p.shape[0] for p in parts)
    return call(stack_kernel, "stack", [((rows, DW), bf)], *parts)[0]


def pack_kernel(qkv_ref, out_ref):
    for d in range(F):
        r, c = d % C * HALF, d // C * COLS
        out_ref[d] = qkv_ref[:, r : r + HALF, c : c + COLS]


def compact_kernel(place, sizes, cot_ref, same_ref, other_ref):
    shape = (POS, F * CAP)
    row, col = iota(shape, 0), iota(shape, 1)
    pos = row ^ (place[CORE] * HALF)
    start = jnp.int32(0)
    picked = jnp.full(shape, -1, jnp.int32)
    for j in range(F):
        slot = col - j * CAP
        inside = (slot >= 0) & (slot < sizes[0, j])
        picked = jnp.where(inside, slot + start, picked)
        start = start + sizes[0, j]
    hot = (picked == pos).astype(f32).astype(bf)
    up = dot(hot, cot_ref[...].reshape(F * CAP, DW), NN).astype(bf)
    same_ref[...] = up[:HALF]
    other_ref[...] = up[HALF:]


def block(ref, i, b, h):
    return ref[:, i, b * 16 : (b + 1) * 16, h * HD : (h + 1) * HD].reshape(POS, HD)


def fwd_kernel(place, bias, leave_ref, qkv_ref, probs_ref, mixed_ref, raw_ref):
    row, col = iota((POS, POS), 0), iota((POS, POS), 1)
    alike = (row & 15) == (col & 15)
    offset = (col >> 4) - (row >> 4) + 7
    for h in range(HL):
        pair = jnp.full((POS, POS), -1e30, f32)
        for o in range(15):
            pair = jnp.where(alike & (offset == o), bias[place[XI] * HL + h, o], pair)
        for b in range(NB):
            q, k, v = (block(qkv_ref, i, b, h) for i in range(3))
            s = dot(q, k, NT) * FACTOR + pair
            e = jnp.exp(s - jnp.max(s, axis=-1, keepdims=True))
            p = e / jnp.sum(e, axis=-1, keepdims=True)
            probs_ref[h, b] = p
            m = dot(p.astype(bf), v, NN).astype(bf).reshape(F, 16, HD)
            raw_ref[:, b * 16 : (b + 1) * 16, h * HD : (h + 1) * HD] = m
    source = leave_ref[1:2] + (leave_ref[0:1] ^ place[CORE]) * 6
    order = (iota((COLS, COLS), 0) == source).astype(f32).astype(bf)
    mixed_ref[...] = dot(raw_ref[...].reshape(F * HALF, COLS), order, NN).astype(bf)


def gw_kernel(place, mixed_ref, u0, u1, u2, u3, mine_ref, other_ref, up_ref):
    for k, ref in enumerate((u0, u1, u2, u3)):
        chip = (place[XI] ^ k) * C
        up_ref[chip + place[CORE]] = ref[:HALF]
        up_ref[chip + 1 - place[CORE]] = ref[HALF:]
    gw = dot(mixed_ref[...], up_ref[...].reshape(F * HALF, DW), TN)
    mine_ref[...] = gw[: COLS // 2]
    other_ref[...] = gw[COLS // 2 :].astype(bf)


def score_kernel(place, rows_ref, recv_ref, probs_ref, up_ref, w0_ref, w1_ref, dm_ref, ds_ref, sums_ref):
    up = up_ref[...].reshape(F * HALF, DW)
    dm = jnp.concatenate([dot(up, w[...], NT).astype(bf) for w in (w0_ref, w1_ref)], axis=1)
    c, y, j = (rows_ref[n : n + 1] ^ place[n] for n in (CORE, YI, ZI))
    spot = ((c * Y + y) * Z + j) * 8 + rows_ref[3:4]
    spot = (iota((512, COLS), 0) == spot).astype(f32).astype(bf)
    dm = dot(dm, spot, NN)
    dm_ref[...] = dm.astype(bf).reshape(F, HALF, COLS)
    for h in range(HL):
        cols = slice(h * HD, (h + 1) * HD)
        total = jnp.zeros((F, POS), f32)
        for b in range(NB):
            d = dm_ref[:, b * 16 : (b + 1) * 16, cols].reshape(POS, HD)
            p = probs_ref[h, b]
            g = dot(d, block(recv_ref, 2, b, h), NT)
            ds = p * (g - jnp.sum(p * g, axis=-1, keepdims=True))
            total = total + jnp.sum(ds.reshape(F, 16, POS), axis=1)
            ds_ref[h, b] = ds.astype(bf)
        sums_ref[:, cols] = total


def grad_kernel(place, qkv_ref, probs_ref, dm_ref, ds_ref, *refs):
    pieces, nat_ref = refs[:F], refs[F]
    for h in range(HL):
        cols = slice(h * HD, (h + 1) * HD)
        for b in range(NB):
            rows = slice(b * 16, (b + 1) * 16)
            d = dm_ref[:, rows, cols].reshape(POS, HD)
            low = ds_ref[h, b]
            gq = dot(low, block(qkv_ref, 1, b, h), NN) * FACTOR
            gk = dot(low, block(qkv_ref, 0, b, h), TN) * FACTOR
            gv = dot(probs_ref[h, b].astype(bf), d, TN)
            for i, val in enumerate((gq, gk, gv)):
                nat_ref[:, i, rows, cols] = val.astype(bf).reshape(F, 16, HD)
    for k in range(F):
        pieces[k][...] = nat_ref[place[RANK] ^ k]


def unpack_kernel(place, *refs):
    pieces, out_ref, nat_ref = refs[:F], refs[F], refs[F + 1]
    for k in range(F):
        nat_ref[place[RANK] ^ k] = pieces[k][...]
    for d in range(F):
        r, c = d % C * HALF, d // C * COLS
        out_ref[:, r : r + HALF, c : c + COLS] = nat_ref[d]


def split(b):
    high = b.astype(bf).astype(f32)
    low = (b - high).astype(bf).astype(f32)
    return high, low


def join_kernel(mine_ref, other_ref, s0, s1, out_ref):
    gw = mine_ref[...] + other_ref[...].astype(f32)
    hot = ((iota((COLS, 128), 0) >> 4) == iota((COLS, 128), 1)).astype(f32)
    b = dot(s0[...] + s1[...], hot, NN, precision=lax.Precision.HIGHEST)
    ride = jnp.concatenate([x[:, :64] for x in split(b)], axis=1)
    for d in range(Z * Y):
        part = gw[6 * d : 6 * d + 6]
        ends = [
            jnp.concatenate([part[r + i : r + i + 1, 1152:] for i in range(3)], axis=1) for r in (0, 3)
        ]
        part = jnp.concatenate([part[:, :1152]] + ends, axis=0)
        out_ref[d] = jnp.concatenate([part, ride], axis=1).astype(bf)


def total_kernel(in_ref, sum_ref, off_ref):
    total = jnp.sum(in_ref[...].astype(f32), axis=0)
    sum_ref[:, :1152] = total[:, :1152]
    for r in range(6):
        sum_ref[r : r + 1, 1152:] = total[6 + r // 3 : 7 + r // 3, r % 3 * 384 : (r % 3 + 1) * 384]
    sum_ref[6:, 1152:] = jnp.zeros((2, 384), f32)
    sums = total[:, 1152:1216] + total[:, 1216:]
    head, lane = iota((16, 64), 0) % HL, iota((16, 64), 1)
    g, o = iota((64, 128), 0) & 7, iota((64, 128), 1)
    out = jnp.zeros((16, 128), f32)
    for f in range(F):
        row = jnp.where((lane >> 3) == head, sums[f : f + 1], 0.0)
        out = out + dot(row, (g - f + 7 == o).astype(f32), NN, precision=lax.Precision.HIGHEST)
    off_ref[...] = out


def last_kernel(place, home_ref, o0, o1, o2, o3, gw_ref, bias_ref):
    gw_ref[...] = home_ref[:6]
    row = iota((16, 128), 0) // HL
    out = jnp.zeros((16, 128), f32)
    for k, o in enumerate((o0, o1, o2, o3)):
        out = out + jnp.where(row == (place[XI] ^ k), o[...], 0.0)
    bias_ref[...] = out[:12, :15]


def hop(x, axis, k, n):
    return lax.ppermute(x, axis, [(i, i ^ k) for i in range(n)])


def per_device(qkv_time, shard_sizes, bias_time, w_out, cot_out):
    xi, yi, zi, core = (lax.axis_index(a) for a in ("x", "y", "z", "core"))
    place = jnp.stack([core, yi, zi, xi, xi * C + core]).astype(jnp.int32)

    there = [
        ((2 * c + z0) * X + x, (z0 * X + x) * X + c)
        for c in range(X)
        for z0 in range(2)
        for x in range(X)
    ]
    near = [(a, b ^ X) for a, b in there]
    cot = lax.all_to_all(cot_out[0, 0], SEQ, 0, 0, tiled=True)
    (packed,) = call(pack_kernel, "pack", [((F, 3, HALF, COLS), bf)], qkv_time[:, 0, 0])
    rows8, packed = lax.optimization_barrier((jnp.pad(w_out, ((0, 2), (0, 0))), packed))
    held = [lax.ppermute(rows8, ("z", "x"), p) for p in (there, near)]
    packed, held = lax.optimization_barrier((packed, held))
    recv = lax.all_to_all(packed, SEQ, 0, 0, tiled=True)
    held = jnp.concatenate(held)
    held = jnp.concatenate([held, hop(held, "z", 2, Z)])

    same, other = call(
        compact_kernel,
        "compact",
        [((HALF, DW), bf)] * 2,
        place,
        shard_sizes,
        cot,
        smem=2,
        flops=100_000_000,
    )
    held, same = lax.optimization_barrier((held, same))
    held = jnp.concatenate([held, hop(held, "z", 4, Z)])
    u0 = stack([same, hop(other, "core", 1, C)])
    held, _ = lax.optimization_barrier((held, u0))
    ups = [u0] + [hop(u0, "x", k, X) for k in range(1, X)]
    held = stack([held, hop(held, "y", 1, Y)])
    held, ups[1] = lax.optimization_barrier((held, ups[1]))
    held = stack([held, hop(held, "y", 2, Y)])
    held2 = hop(held, "core", 1, C)

    probs, mixed = call(
        fwd_kernel,
        "attn_fwd",
        [((HL, NB, POS, POS), f32), ((F * HALF, COLS), bf)],
        place,
        bias_time,
        LEAVE,
        recv,
        smem=2,
        scratch=[pltpu.VMEM((F, HALF, COLS), bf)],
        flops=20_000_000_000,
    )

    mine, theirs, up = call(
        gw_kernel,
        "grad_w",
        [((COLS // 2, DW), f32), ((COLS // 2, DW), bf), ((F, HALF, DW), bf)],
        place,
        mixed,
        *ups,
        smem=1,
        flops=20_000_000_000,
    )
    dm, ds, sums = call(
        score_kernel,
        "scores_bwd",
        [((F, HALF, COLS), bf), ((HL, NB, POS, POS), bf), ((F, COLS), f32)],
        place,
        ROWS_OF,
        recv,
        probs,
        up,
        held,
        held2,
        smem=1,
        flops=900_000_000,
    )
    theirs = hop(theirs, "core", 1, C)
    sums2 = hop(sums, "core", 1, C)

    pieces = call(
        grad_kernel,
        "grads",
        [((3, HALF, COLS), bf)] * F,
        place,
        recv,
        probs,
        dm,
        ds,
        smem=1,
        scratch=[pltpu.VMEM((F, 3, HALF, COLS), bf)],
        flops=150_000_000,
    )

    (msgs,) = call(join_kernel, "join", [((Z * Y, 8, 1280), bf)], mine, theirs, sums, sums2)
    msgs, *pieces = lax.optimization_barrier((msgs, *pieces))
    msgs = lax.all_to_all(msgs, ("z", "y"), 0, 0, tiled=True)
    pieces = pieces[:1] + [hop(p, SEQ, k, F) for k, p in enumerate(pieces[1:], 1)]
    msgs, *pieces[1:6] = lax.optimization_barrier((msgs, *pieces[1:6]))
    total, off = call(total_kernel, "total", [((8, DW), f32), ((16, 128), f32)], msgs)
    home = lax.ppermute(total, ("z", "x"), [(b, a) for a, b in there])
    offs = [off] + [hop(off, "x", k, X) for k in range(1, X)]
    (grad_qkv,) = call(
        unpack_kernel,
        "unpack",
        [((3, POS, DW), bf)],
        place,
        *pieces,
        smem=1,
        scratch=[pltpu.VMEM((F, 3, HALF, COLS), bf)],
    )
    grad_qkv = grad_qkv.reshape(3, 1, 1, POS, DW)
    home, grad_qkv = lax.optimization_barrier((home, grad_qkv))
    grad_w_out, grad_bias = call(
        last_kernel, "last", [((6, DW), f32), ((12, 15), f32)], place, home, *offs, smem=1
    )
    return grad_qkv, grad_bias, grad_w_out


def solution(mesh):
    grid = Mesh(mesh.devices.reshape(Z, Y, X, C), ("z", "y", "x", "core"))
    dp, every = ("z", "y"), ("z", "y", "x", "core")
    return jax.shard_map(
        per_device,
        mesh=grid,
        in_specs=(
            P(None, dp, SEQ, None, None),
            P(dp, None),
            P(),
            P(every, None),
            P(dp, SEQ, None, None, None),
        ),
        out_specs=(P(None, dp, SEQ, None, None), P(), P(every, None)),
        check_vma=False,
    )
```

```python
import math

import jax
import jax.numpy as jnp
import numpy as np
from jax import lax
from jax.experimental import pallas as pl
from jax.experimental.pallas import tpu as pltpu
from jax.sharding import Mesh, PartitionSpec as P

Z, Y, X, C = 8, 4, 4, 2
SEQ = ("x", "core")
F = 8
POS = 128
HALF = 64
NB = 4
HL = 3
HD = 128
COLS = HL * HD
DW = 1536
CAP = 32
FACTOR = 1.0 / math.sqrt(HD)
NN = (((1,), (0,)), ((), ()))
NT = (((1,), (1,)), ((), ()))
TN = (((0,), (0,)), ((), ()))
bf, f32 = jnp.bfloat16, jnp.float32
CORE, YI, ZI, XI, RANK = range(5)

ROW = np.arange(COLS)
ROWS_OF = np.zeros((8, COLS), np.int32)
ROWS_OF[0] = ROW // 6 % 2
ROWS_OF[1] = ROW // 48 % 4
ROWS_OF[2] = ROW // 192 * 4 + ROW // 12 % 4
ROWS_OF[3] = ROW % 6
LEAVE = np.zeros((8, COLS), np.int32)
LEAVE[0] = ROW // 192
SUB = ROW % 192 // 6
LEAVE[1] = ((SUB // 16 * 4 + SUB % 4) * 8 + SUB // 4 % 4 * 2) * 6 + ROW % 6


def dot(a, b, dims, **kw):
    return lax.dot_general(a, b, dims, preferred_element_type=f32, **kw)


def iota(shape, dim):
    return lax.broadcasted_iota(jnp.int32, shape, dim)


def call(body, name, outs, *ins, smem=0, scratch=(), flops=0, space=pltpu.VMEM, vmem=16):
    total = sum(math.prod(s) * jnp.dtype(d).itemsize for s, d in outs)
    total += sum(a.size * a.dtype.itemsize for a in ins)
    specs = [pl.BlockSpec(memory_space=pltpu.SMEM)] * smem
    specs += [pl.BlockSpec(memory_space=space)] * (len(ins) - smem)
    return pl.pallas_call(
        body,
        out_shape=tuple(jax.ShapeDtypeStruct(s, d) for s, d in outs),
        in_specs=specs,
        out_specs=tuple(pl.BlockSpec(memory_space=space) for _ in outs),
        scratch_shapes=list(scratch),
        compiler_params=pltpu.CompilerParams(vmem_limit_bytes=vmem << 20),
        cost_estimate=pl.CostEstimate(flops=flops, bytes_accessed=total, transcendentals=0),
        name=name,
    )(*ins)


def stack_kernel(*refs):
    out_ref, row = refs[-1], 0
    for ref in refs[:-1]:
        rows = ref.shape[0]
        out_ref[row : row + rows] = ref[...]
        row += rows


def stack(parts):
    rows = sum(p.shape[0] for p in parts)
    return call(stack_kernel, "stack", [((rows, DW), bf)], *parts)[0]


def pack_kernel(place, qkv_ref, *refs):
    pieces, nat_ref = refs[:X], refs[X]
    for c in range(X):
        nat_ref[c] = qkv_ref[:, :, c * COLS : (c + 1) * COLS]
    for k in range(X):
        pieces[k][...] = nat_ref[place[XI] ^ k]


def half(core):
    return pl.ds(pl.multiple_of(core * HALF, HALF), HALF)


def cross_kernel(place, *refs):
    for k in range(X):
        refs[X][k] = refs[k][:, half(1 - place[CORE]), :]


def compact_kernel(place, sizes, cot_ref, same_ref, other_ref):
    shape = (POS, F * CAP)
    row, col = iota(shape, 0), iota(shape, 1)
    pos = row ^ (place[CORE] * HALF)
    start = jnp.int32(0)
    picked = jnp.full(shape, -1, jnp.int32)
    for j in range(F):
        slot = col - j * CAP
        inside = (slot >= 0) & (slot < sizes[0, j])
        picked = jnp.where(inside, slot + start, picked)
        start = start + sizes[0, j]
    hot = (picked == pos).astype(f32).astype(bf)
    up = dot(hot, cot_ref[...].reshape(F * CAP, DW), NN).astype(bf)
    same_ref[...] = up[:HALF]
    other_ref[...] = up[HALF:]


def block(ref, i, b, h):
    return ref[:, i, b * 16 : (b + 1) * 16, h * HD : (h + 1) * HD].reshape(POS, HD)


def fwd_kernel(place, bias, leave_ref, p0, p1, p2, p3, cross_ref, probs_ref, mixed_ref, qkv_ref, raw_ref):
    for k, ref in enumerate((p0, p1, p2, p3)):
        frame = (place[XI] ^ k) * C
        qkv_ref[frame + place[CORE]] = ref[:, half(place[CORE]), :]
        qkv_ref[frame + 1 - place[CORE]] = cross_ref[k]
    row, col = iota((POS, POS), 0), iota((POS, POS), 1)
    alike = (row & 15) == (col & 15)
    offset = (col >> 4) - (row >> 4) + 7
    for h in range(HL):
        pair = jnp.full((POS, POS), -1e30, f32)
        for o in range(15):
            pair = jnp.where(alike & (offset == o), bias[place[XI] * HL + h, o], pair)
        for b in range(NB):
            q, k, v = (block(qkv_ref, i, b, h) for i in range(3))
            s = dot(q, k, NT) * FACTOR + pair
            e = jnp.exp(s - jnp.max(s, axis=-1, keepdims=True))
            p = e / jnp.sum(e, axis=-1, keepdims=True)
            probs_ref[h, b] = p
            m = dot(p.astype(bf), v, NN).astype(bf).reshape(F, 16, HD)
            raw_ref[:, b * 16 : (b + 1) * 16, h * HD : (h + 1) * HD] = m
    source = leave_ref[1:2] + (leave_ref[0:1] ^ place[CORE]) * 6
    order = (iota((COLS, COLS), 0) == source).astype(f32).astype(bf)
    mixed_ref[...] = dot(raw_ref[...].reshape(F * HALF, COLS), order, NN).astype(bf)


def gw_kernel(place, mixed_ref, u0, u1, u2, u3, mine_ref, other_ref, up_ref):
    for k, ref in enumerate((u0, u1, u2, u3)):
        chip = (place[XI] ^ k) * C
        up_ref[chip + place[CORE]] = ref[:HALF]
        up_ref[chip + 1 - place[CORE]] = ref[HALF:]
    gw = dot(mixed_ref[...], up_ref[...].reshape(F * HALF, DW), TN)
    mine_ref[...] = gw[: COLS // 2]
    other_ref[...] = gw[COLS // 2 :].astype(bf)


def score_kernel(place, rows_ref, recv_ref, probs_ref, up_ref, w0_ref, w1_ref, dm_ref, ds_ref, sums_ref):
    up = up_ref[...].reshape(F * HALF, DW)
    dm = jnp.concatenate([dot(up, w[...], NT).astype(bf) for w in (w0_ref, w1_ref)], axis=1)
    c, y, j = (rows_ref[n : n + 1] ^ place[n] for n in (CORE, YI, ZI))
    spot = ((c * Y + y) * Z + j) * 8 + rows_ref[3:4]
    spot = (iota((512, COLS), 0) == spot).astype(f32).astype(bf)
    dm = dot(dm, spot, NN)
    dm_ref[...] = dm.astype(bf).reshape(F, HALF, COLS)
    for h in range(HL):
        cols = slice(h * HD, (h + 1) * HD)
        total = jnp.zeros((F, POS), f32)
        for b in range(NB):
            d = dm_ref[:, b * 16 : (b + 1) * 16, cols].reshape(POS, HD)
            p = probs_ref[h, b]
            g = dot(d, block(recv_ref, 2, b, h), NT)
            ds = p * (g - jnp.sum(p * g, axis=-1, keepdims=True))
            total = total + jnp.sum(ds.reshape(F, 16, POS), axis=1)
            ds_ref[h, b] = ds.astype(bf)
        sums_ref[:, cols] = total


def grad_kernel(place, qkv_ref, probs_ref, dm_ref, ds_ref, *refs):
    pieces, nat_ref = refs[:F], refs[F]
    for h in range(HL):
        cols = slice(h * HD, (h + 1) * HD)
        for b in range(NB):
            rows = slice(b * 16, (b + 1) * 16)
            d = dm_ref[:, rows, cols].reshape(POS, HD)
            low = ds_ref[h, b]
            gq = dot(low, block(qkv_ref, 1, b, h), NN) * FACTOR
            gk = dot(low, block(qkv_ref, 0, b, h), TN) * FACTOR
            gv = dot(probs_ref[h, b].astype(bf), d, TN)
            for i, val in enumerate((gq, gk, gv)):
                nat_ref[:, i, rows, cols] = val.astype(bf).reshape(F, 16, HD)
    for k in range(F):
        pieces[k][...] = nat_ref[place[RANK] ^ k]


def unpack_kernel(place, *refs):
    pieces, out_ref, nat_ref = refs[:F], refs[F], refs[F + 1]
    for k in range(F):
        nat_ref[place[RANK] ^ k] = pieces[k][...]
    for d in range(F):
        r, c = d % C * HALF, d // C * COLS
        out_ref[:, r : r + HALF, c : c + COLS] = nat_ref[d]


def split(b):
    high = b.astype(bf).astype(f32)
    low = (b - high).astype(bf).astype(f32)
    return high, low


def join_kernel(mine_ref, other_ref, s0, s1, out_ref):
    gw = mine_ref[...] + other_ref[...].astype(f32)
    hot = ((iota((COLS, 128), 0) >> 4) == iota((COLS, 128), 1)).astype(f32)
    b = dot(s0[...] + s1[...], hot, NN, precision=lax.Precision.HIGHEST)
    ride = jnp.concatenate([x[:, :64] for x in split(b)], axis=1)
    for d in range(Z * Y):
        part = gw[6 * d : 6 * d + 6]
        ends = [
            jnp.concatenate([part[r + i : r + i + 1, 1152:] for i in range(3)], axis=1) for r in (0, 3)
        ]
        part = jnp.concatenate([part[:, :1152]] + ends, axis=0)
        out_ref[d] = jnp.concatenate([part, ride], axis=1).astype(bf)


def total_kernel(in_ref, sum_ref, off_ref):
    total = jnp.sum(in_ref[...].astype(f32), axis=0)
    sum_ref[:, :1152] = total[:, :1152]
    for r in range(6):
        sum_ref[r : r + 1, 1152:] = total[6 + r // 3 : 7 + r // 3, r % 3 * 384 : (r % 3 + 1) * 384]
    sum_ref[6:, 1152:] = jnp.zeros((2, 384), f32)
    sums = total[:, 1152:1216] + total[:, 1216:]
    head, lane = iota((16, 64), 0) % HL, iota((16, 64), 1)
    g, o = iota((64, 128), 0) & 7, iota((64, 128), 1)
    out = jnp.zeros((16, 128), f32)
    for f in range(F):
        row = jnp.where((lane >> 3) == head, sums[f : f + 1], 0.0)
        out = out + dot(row, (g - f + 7 == o).astype(f32), NN, precision=lax.Precision.HIGHEST)
    off_ref[...] = out


def last_kernel(place, home_ref, o0, o1, o2, o3, gw_ref, bias_ref):
    gw_ref[...] = home_ref[:6]
    row = iota((16, 128), 0) // HL
    out = jnp.zeros((16, 128), f32)
    for k, o in enumerate((o0, o1, o2, o3)):
        out = out + jnp.where(row == (place[XI] ^ k), o[...], 0.0)
    bias_ref[...] = out[:12, :15]


def hop(x, axis, k, n):
    return lax.ppermute(x, axis, [(i, i ^ k) for i in range(n)])


def per_device(qkv_time, shard_sizes, bias_time, w_out, cot_out):
    xi, yi, zi, core = (lax.axis_index(a) for a in ("x", "y", "z", "core"))
    place = jnp.stack([core, yi, zi, xi, xi * C + core]).astype(jnp.int32)

    there = [
        ((2 * c + z0) * X + x, (z0 * X + x) * X + c)
        for c in range(X)
        for z0 in range(2)
        for x in range(X)
    ]
    near = [(a, b ^ X) for a, b in there]
    cot = lax.all_to_all(cot_out[0, 0], SEQ, 0, 0, tiled=True)
    packed = call(
        pack_kernel,
        "pack",
        [((3, POS, COLS), bf)] * X,
        place,
        qkv_time[:, 0, 0],
        smem=1,
        scratch=[pltpu.VMEM((X, 3, POS, COLS), bf)],
    )
    rows8 = jnp.pad(w_out, ((0, 2), (0, 0)))
    rows8, packed = lax.optimization_barrier((rows8, packed))
    held = [lax.ppermute(rows8, ("z", "x"), p) for p in (there, near)]
    packed, held = lax.optimization_barrier((packed, held))
    packed = [packed[0]] + [hop(packed[k], "x", k, X) for k in range(1, X)]
    held = jnp.concatenate(held)
    held = jnp.concatenate([held, hop(held, "z", 2, Z)])

    same, other = call(
        compact_kernel,
        "compact",
        [((HALF, DW), bf)] * 2,
        place,
        shard_sizes,
        cot,
        smem=2,
        flops=100_000_000,
    )
    held, same = lax.optimization_barrier((held, same))
    held = jnp.concatenate([held, hop(held, "z", 4, Z)])
    z4 = held
    u0 = stack([same, hop(other, "core", 1, C)])
    held, _ = lax.optimization_barrier((held, u0))
    ups = [u0] + [hop(u0, "x", k, X) for k in range(1, X)]
    held = stack([held, hop(held, "y", 1, Y)])
    held, ups[1] = lax.optimization_barrier((held, ups[1]))
    held = stack([held, hop(held, "y", 2, Y)])
    held2 = hop(held, "core", 1, C)

    packed, _, _ = lax.optimization_barrier((packed, u0, z4))
    (cross,) = call(cross_kernel, "cross", [((X, 3, HALF, COLS), bf)], place, *packed, smem=1)
    cross = hop(cross, "core", 1, C)
    probs, mixed, recv = call(
        fwd_kernel,
        "attn_fwd",
        [((HL, NB, POS, POS), f32), ((F * HALF, COLS), bf), ((F, 3, HALF, COLS), bf)],
        place,
        bias_time,
        LEAVE,
        *packed,
        cross,
        smem=2,
        scratch=[pltpu.VMEM((F, HALF, COLS), bf)],
        flops=20_000_000_000,
    )

    mine, theirs, up = call(
        gw_kernel,
        "grad_w",
        [((COLS // 2, DW), f32), ((COLS // 2, DW), bf), ((F, HALF, DW), bf)],
        place,
        mixed,
        *ups,
        smem=1,
        flops=20_000_000_000,
    )
    dm, ds, sums = call(
        score_kernel,
        "scores_bwd",
        [((F, HALF, COLS), bf), ((HL, NB, POS, POS), bf), ((F, COLS), f32)],
        place,
        ROWS_OF,
        recv,
        probs,
        up,
        held,
        held2,
        smem=1,
        flops=900_000_000,
    )
    theirs = hop(theirs, "core", 1, C)
    sums2 = hop(sums, "core", 1, C)

    pieces = call(
        grad_kernel,
        "grads",
        [((3, HALF, COLS), bf)] * F,
        place,
        recv,
        probs,
        dm,
        ds,
        smem=1,
        scratch=[pltpu.VMEM((F, 3, HALF, COLS), bf)],
        flops=150_000_000,
    )

    (msgs,) = call(join_kernel, "join", [((Z * Y, 8, 1280), bf)], mine, theirs, sums, sums2)
    msgs, *pieces = lax.optimization_barrier((msgs, *pieces))
    msgs = lax.all_to_all(msgs, ("z", "y"), 0, 0, tiled=True)
    pieces = pieces[:1] + [hop(p, SEQ, k, F) for k, p in enumerate(pieces[1:], 1)]
    msgs, *pieces[1:6] = lax.optimization_barrier((msgs, *pieces[1:6]))
    total, off = call(total_kernel, "total", [((8, DW), f32), ((16, 128), f32)], msgs)
    home = lax.ppermute(total, ("z", "x"), [(b, a) for a, b in there])
    offs = [off] + [hop(off, "x", k, X) for k in range(1, X)]
    (grad_qkv,) = call(
        unpack_kernel,
        "unpack",
        [((3, POS, DW), bf)],
        place,
        *pieces,
        smem=1,
        scratch=[pltpu.VMEM((F, 3, HALF, COLS), bf)],
    )
    grad_qkv = grad_qkv.reshape(3, 1, 1, POS, DW)
    home, grad_qkv = lax.optimization_barrier((home, grad_qkv))
    grad_w_out, grad_bias = call(
        last_kernel, "last", [((6, DW), f32), ((12, 15), f32)], place, home, *offs, smem=1
    )
    return grad_qkv, grad_bias, grad_w_out


def solution(mesh):
    grid = Mesh(mesh.devices.reshape(Z, Y, X, C), ("z", "y", "x", "core"))
    dp, every = ("z", "y"), ("z", "y", "x", "core")
    return jax.shard_map(
        per_device,
        mesh=grid,
        in_specs=(
            P(None, dp, SEQ, None, None),
            P(dp, None),
            P(),
            P(every, None),
            P(dp, SEQ, None, None, None),
        ),
        out_specs=(P(None, dp, SEQ, None, None), P(), P(every, None)),
        check_vma=False,
    )
```

```python
import math

import jax
import jax.numpy as jnp
import numpy as np
from jax import lax
from jax.experimental import pallas as pl
from jax.experimental.pallas import tpu as pltpu
from jax.sharding import Mesh, PartitionSpec as P

Z, Y, X, C = 8, 4, 4, 2
SEQ = ("x", "core")
F = 8
POS = 128
HALF = 64
NB = 4
HL = 3
HD = 128
COLS = HL * HD
DW = 1536
CAP = 32
FACTOR = 1.0 / math.sqrt(HD)
NN = (((1,), (0,)), ((), ()))
NT = (((1,), (1,)), ((), ()))
TN = (((0,), (0,)), ((), ()))
bf, f32 = jnp.bfloat16, jnp.float32
CORE, YI, ZI, XI, RANK = range(5)

ROW = np.arange(COLS)
ROWS_OF = np.zeros((8, COLS), np.int32)
ROWS_OF[0] = ROW // 6 % 2
ROWS_OF[1] = ROW // 48 % 4
ROWS_OF[2] = ROW // 192 * 4 + ROW // 12 % 4
ROWS_OF[3] = ROW % 6
LEAVE = np.zeros((8, COLS), np.int32)
LEAVE[0] = ROW // 192
SUB = ROW % 192 // 6
LEAVE[1] = ((SUB // 16 * 4 + SUB % 4) * 8 + SUB // 4 % 4 * 2) * 6 + ROW % 6


def dot(a, b, dims, **kw):
    return lax.dot_general(a, b, dims, preferred_element_type=f32, **kw)


def iota(shape, dim):
    return lax.broadcasted_iota(jnp.int32, shape, dim)


def call(body, name, outs, *ins, smem=0, scratch=(), flops=0, space=pltpu.VMEM, vmem=16):
    total = sum(math.prod(s) * jnp.dtype(d).itemsize for s, d in outs)
    total += sum(a.size * a.dtype.itemsize for a in ins)
    specs = [pl.BlockSpec(memory_space=pltpu.SMEM)] * smem
    specs += [pl.BlockSpec(memory_space=space)] * (len(ins) - smem)
    return pl.pallas_call(
        body,
        out_shape=tuple(jax.ShapeDtypeStruct(s, d) for s, d in outs),
        in_specs=specs,
        out_specs=tuple(pl.BlockSpec(memory_space=space) for _ in outs),
        scratch_shapes=list(scratch),
        compiler_params=pltpu.CompilerParams(vmem_limit_bytes=vmem << 20),
        cost_estimate=pl.CostEstimate(flops=flops, bytes_accessed=total, transcendentals=0),
        name=name,
    )(*ins)


def stack_kernel(*refs):
    out_ref, row = refs[-1], 0
    for ref in refs[:-1]:
        rows = ref.shape[0]
        out_ref[row : row + rows] = ref[...]
        row += rows


def stack(parts):
    rows = sum(p.shape[0] for p in parts)
    return call(stack_kernel, "stack", [((rows, DW), bf)], *parts)[0]


def pack_kernel(place, qkv_ref, *refs):
    pieces, nat_ref = refs[:X], refs[X]
    for c in range(X):
        nat_ref[c] = qkv_ref[:, :, c * COLS : (c + 1) * COLS]
    for k in range(X):
        pieces[k][...] = nat_ref[place[XI] ^ k]


def half(core):
    return pl.ds(pl.multiple_of(core * HALF, HALF), HALF)


def cross_kernel(place, *refs):
    for k in range(X):
        refs[X][k] = refs[k][:, half(1 - place[CORE]), :]


def compact_kernel(place, sizes, cot_ref, same_ref, other_ref):
    shape = (POS, F * CAP)
    row, col = iota(shape, 0), iota(shape, 1)
    pos = row ^ (place[CORE] * HALF)
    start = jnp.int32(0)
    picked = jnp.full(shape, -1, jnp.int32)
    for j in range(F):
        slot = col - j * CAP
        inside = (slot >= 0) & (slot < sizes[0, j])
        picked = jnp.where(inside, slot + start, picked)
        start = start + sizes[0, j]
    hot = (picked == pos).astype(f32).astype(bf)
    up = dot(hot, cot_ref[...].reshape(F * CAP, DW), NN).astype(bf)
    same_ref[...] = up[:HALF]
    other_ref[...] = up[HALF:]


def block(ref, i, b, h):
    return ref[:, i, b * 16 : (b + 1) * 16, h * HD : (h + 1) * HD].reshape(POS, HD)


def fwd_kernel(place, bias, leave_ref, p0, p1, p2, p3, cross_ref, probs_ref, mixed_ref, qkv_ref, raw_ref):
    for k, ref in enumerate((p0, p1, p2, p3)):
        frame = (place[XI] ^ k) * C
        qkv_ref[frame + place[CORE]] = ref[:, half(place[CORE]), :]
        qkv_ref[frame + 1 - place[CORE]] = cross_ref[k]
    row, col = iota((POS, POS), 0), iota((POS, POS), 1)
    alike = (row & 15) == (col & 15)
    offset = (col >> 4) - (row >> 4) + 7
    for h in range(HL):
        pair = jnp.full((POS, POS), -1e30, f32)
        for o in range(15):
            pair = jnp.where(alike & (offset == o), bias[place[XI] * HL + h, o], pair)
        for b in range(NB):
            q, k, v = (block(qkv_ref, i, b, h) for i in range(3))
            s = dot(q, k, NT) * FACTOR + pair
            e = jnp.exp(s - jnp.max(s, axis=-1, keepdims=True))
            p = e / jnp.sum(e, axis=-1, keepdims=True)
            probs_ref[h, b] = p
            m = dot(p.astype(bf), v, NN).astype(bf).reshape(F, 16, HD)
            raw_ref[:, b * 16 : (b + 1) * 16, h * HD : (h + 1) * HD] = m
    source = leave_ref[1:2] + (leave_ref[0:1] ^ place[CORE]) * 6
    order = (iota((COLS, COLS), 0) == source).astype(f32).astype(bf)
    mixed_ref[...] = dot(raw_ref[...].reshape(F * HALF, COLS), order, NN).astype(bf)


def gw_kernel(place, mixed_ref, u0, u1, u2, u3, mine_ref, other_ref, up_ref):
    for k, ref in enumerate((u0, u1, u2, u3)):
        chip = (place[XI] ^ k) * C
        up_ref[chip + place[CORE]] = ref[:HALF]
        up_ref[chip + 1 - place[CORE]] = ref[HALF:]
    gw = dot(mixed_ref[...], up_ref[...].reshape(F * HALF, DW), TN)
    mine_ref[...] = gw[: COLS // 2]
    other_ref[...] = gw[COLS // 2 :].astype(bf)


def score_kernel(place, rows_ref, recv_ref, probs_ref, up_ref, w0_ref, w1_ref, dm_ref, ds_ref, sums_ref):
    up = up_ref[...].reshape(F * HALF, DW)
    dm = jnp.concatenate([dot(up, w[...], NT).astype(bf) for w in (w0_ref, w1_ref)], axis=1)
    c, y, j = (rows_ref[n : n + 1] ^ place[n] for n in (CORE, YI, ZI))
    spot = ((c * Y + y) * Z + j) * 8 + rows_ref[3:4]
    spot = (iota((512, COLS), 0) == spot).astype(f32).astype(bf)
    dm = dot(dm, spot, NN)
    dm_ref[...] = dm.astype(bf).reshape(F, HALF, COLS)
    for h in range(HL):
        cols = slice(h * HD, (h + 1) * HD)
        total = jnp.zeros((F, POS), f32)
        for b in range(NB):
            d = dm_ref[:, b * 16 : (b + 1) * 16, cols].reshape(POS, HD)
            p = probs_ref[h, b]
            g = dot(d, block(recv_ref, 2, b, h), NT)
            ds = p * (g - jnp.sum(p * g, axis=-1, keepdims=True))
            total = total + jnp.sum(ds.reshape(F, 16, POS), axis=1)
            ds_ref[h, b] = ds.astype(bf)
        sums_ref[:, cols] = total


def grad_kernel(place, qkv_ref, probs_ref, dm_ref, ds_ref, *refs):
    pieces, nat_ref = refs[:F], refs[F]
    for h in range(HL):
        cols = slice(h * HD, (h + 1) * HD)
        for b in range(NB):
            rows = slice(b * 16, (b + 1) * 16)
            d = dm_ref[:, rows, cols].reshape(POS, HD)
            low = ds_ref[h, b]
            gq = dot(low, block(qkv_ref, 1, b, h), NN) * FACTOR
            gk = dot(low, block(qkv_ref, 0, b, h), TN) * FACTOR
            gv = dot(probs_ref[h, b].astype(bf), d, TN)
            for i, val in enumerate((gq, gk, gv)):
                nat_ref[:, i, rows, cols] = val.astype(bf).reshape(F, 16, HD)
    for k in range(F):
        pieces[k][...] = nat_ref[place[RANK] ^ k]


def unpack_kernel(place, *refs):
    pieces, out_ref, nat_ref = refs[:F], refs[F], refs[F + 1]
    for k in range(F):
        nat_ref[place[RANK] ^ k] = pieces[k][...]
    for d in range(F):
        r, c = d % C * HALF, d // C * COLS
        out_ref[:, r : r + HALF, c : c + COLS] = nat_ref[d]


def split(b):
    high = b.astype(bf).astype(f32)
    low = (b - high).astype(bf).astype(f32)
    return high, low


def join_kernel(mine_ref, other_ref, s0, s1, out_ref):
    gw = mine_ref[...] + other_ref[...].astype(f32)
    hot = ((iota((COLS, 128), 0) >> 4) == iota((COLS, 128), 1)).astype(f32)
    b = dot(s0[...] + s1[...], hot, NN, precision=lax.Precision.HIGHEST)
    ride = jnp.concatenate([x[:, :64] for x in split(b)], axis=1)
    for d in range(Z * Y):
        part = gw[6 * d : 6 * d + 6]
        ends = [
            jnp.concatenate([part[r + i : r + i + 1, 1152:] for i in range(3)], axis=1) for r in (0, 3)
        ]
        part = jnp.concatenate([part[:, :1152]] + ends, axis=0)
        out_ref[d] = jnp.concatenate([part, ride], axis=1).astype(bf)


def total_kernel(in_ref, sum_ref, off_ref):
    total = jnp.sum(in_ref[...].astype(f32), axis=0)
    sum_ref[:, :1152] = total[:, :1152]
    for r in range(6):
        sum_ref[r : r + 1, 1152:] = total[6 + r // 3 : 7 + r // 3, r % 3 * 384 : (r % 3 + 1) * 384]
    sum_ref[6:, 1152:] = jnp.zeros((2, 384), f32)
    sums = total[:, 1152:1216] + total[:, 1216:]
    head, lane = iota((16, 64), 0) % HL, iota((16, 64), 1)
    g, o = iota((64, 128), 0) & 7, iota((64, 128), 1)
    out = jnp.zeros((16, 128), f32)
    for f in range(F):
        row = jnp.where((lane >> 3) == head, sums[f : f + 1], 0.0)
        out = out + dot(row, (g - f + 7 == o).astype(f32), NN, precision=lax.Precision.HIGHEST)
    off_ref[...] = out


def last_kernel(place, home_ref, o0, o1, o2, o3, gw_ref, bias_ref):
    gw_ref[...] = home_ref[:6]
    row = iota((16, 128), 0) // HL
    out = jnp.zeros((16, 128), f32)
    for k, o in enumerate((o0, o1, o2, o3)):
        out = out + jnp.where(row == (place[XI] ^ k), o[...], 0.0)
    bias_ref[...] = out[:12, :15]


def hop(x, axis, k, n):
    return lax.ppermute(x, axis, [(i, i ^ k) for i in range(n)])


def per_device(qkv_time, shard_sizes, bias_time, w_out, cot_out):
    xi, yi, zi, core = (lax.axis_index(a) for a in ("x", "y", "z", "core"))
    place = jnp.stack([core, yi, zi, xi, xi * C + core]).astype(jnp.int32)

    there = [
        ((2 * c + z0) * X + x, (z0 * X + x) * X + c)
        for c in range(X)
        for z0 in range(2)
        for x in range(X)
    ]
    near = [(a, b ^ X) for a, b in there]
    cot = lax.all_to_all(cot_out[0, 0], SEQ, 0, 0, tiled=True)
    packed = call(
        pack_kernel,
        "pack",
        [((3, POS, COLS), bf)] * X,
        place,
        qkv_time[:, 0, 0],
        smem=1,
        scratch=[pltpu.VMEM((X, 3, POS, COLS), bf)],
    )
    rows8 = jnp.pad(w_out, ((0, 2), (0, 0)))
    rows8, packed = lax.optimization_barrier((rows8, packed))
    held = [lax.ppermute(rows8, ("z", "x"), p) for p in (there, near)]
    packed, held = lax.optimization_barrier((packed, held))
    packed = [packed[0]] + [hop(packed[k], "x", k, X) for k in range(1, X)]
    held = jnp.concatenate(held)
    held = jnp.concatenate([held, hop(held, "z", 2, Z)])

    same, other = call(
        compact_kernel,
        "compact",
        [((HALF, DW), bf)] * 2,
        place,
        shard_sizes,
        cot,
        smem=2,
        flops=100_000_000,
    )
    held, same = lax.optimization_barrier((held, same))
    held = jnp.concatenate([held, hop(held, "z", 4, Z)])
    u0 = stack([same, hop(other, "core", 1, C)])
    ups = [u0] + [hop(u0, "x", k, X) for k in range(1, X)]
    held = stack([held, hop(held, "y", 1, Y)])
    y1 = held
    held = stack([held, hop(held, "y", 2, Y)])
    held2 = hop(held, "core", 1, C)

    packed, _, _ = lax.optimization_barrier((packed, u0, y1))
    (cross,) = call(cross_kernel, "cross", [((X, 3, HALF, COLS), bf)], place, *packed, smem=1)
    cross = hop(cross, "core", 1, C)
    probs, mixed, recv = call(
        fwd_kernel,
        "attn_fwd",
        [((HL, NB, POS, POS), f32), ((F * HALF, COLS), bf), ((F, 3, HALF, COLS), bf)],
        place,
        bias_time,
        LEAVE,
        *packed,
        cross,
        smem=2,
        scratch=[pltpu.VMEM((F, HALF, COLS), bf)],
        flops=20_000_000_000,
    )

    mine, theirs, up = call(
        gw_kernel,
        "grad_w",
        [((COLS // 2, DW), f32), ((COLS // 2, DW), bf), ((F, HALF, DW), bf)],
        place,
        mixed,
        *ups,
        smem=1,
        flops=20_000_000_000,
    )
    dm, ds, sums = call(
        score_kernel,
        "scores_bwd",
        [((F, HALF, COLS), bf), ((HL, NB, POS, POS), bf), ((F, COLS), f32)],
        place,
        ROWS_OF,
        recv,
        probs,
        up,
        held,
        held2,
        smem=1,
        flops=900_000_000,
    )
    theirs = hop(theirs, "core", 1, C)
    sums2 = hop(sums, "core", 1, C)

    pieces = call(
        grad_kernel,
        "grads",
        [((3, HALF, COLS), bf)] * F,
        place,
        recv,
        probs,
        dm,
        ds,
        smem=1,
        scratch=[pltpu.VMEM((F, 3, HALF, COLS), bf)],
        flops=150_000_000,
    )

    (msgs,) = call(join_kernel, "join", [((Z * Y, 8, 1280), bf)], mine, theirs, sums, sums2)
    msgs, *pieces = lax.optimization_barrier((msgs, *pieces))
    msgs = lax.all_to_all(msgs, ("z", "y"), 0, 0, tiled=True)
    pieces = pieces[:1] + [hop(p, SEQ, k, F) for k, p in enumerate(pieces[1:], 1)]
    msgs, *pieces[1:6] = lax.optimization_barrier((msgs, *pieces[1:6]))
    total, off = call(total_kernel, "total", [((8, DW), f32), ((16, 128), f32)], msgs)
    home = lax.ppermute(total, ("z", "x"), [(b, a) for a, b in there])
    offs = [off] + [hop(off, "x", k, X) for k in range(1, X)]
    (grad_qkv,) = call(
        unpack_kernel,
        "unpack",
        [((3, POS, DW), bf)],
        place,
        *pieces,
        smem=1,
        scratch=[pltpu.VMEM((F, 3, HALF, COLS), bf)],
    )
    grad_qkv = grad_qkv.reshape(3, 1, 1, POS, DW)
    home, grad_qkv = lax.optimization_barrier((home, grad_qkv))
    grad_w_out, grad_bias = call(
        last_kernel, "last", [((6, DW), f32), ((12, 15), f32)], place, home, *offs, smem=1
    )
    return grad_qkv, grad_bias, grad_w_out


def solution(mesh):
    grid = Mesh(mesh.devices.reshape(Z, Y, X, C), ("z", "y", "x", "core"))
    dp, every = ("z", "y"), ("z", "y", "x", "core")
    return jax.shard_map(
        per_device,
        mesh=grid,
        in_specs=(
            P(None, dp, SEQ, None, None),
            P(dp, None),
            P(),
            P(every, None),
            P(dp, SEQ, None, None, None),
        ),
        out_specs=(P(None, dp, SEQ, None, None), P(), P(every, None)),
        check_vma=False,
    )
```

```python
import math

import jax
import jax.numpy as jnp
import numpy as np
from jax import lax
from jax.experimental import pallas as pl
from jax.experimental.pallas import tpu as pltpu
from jax.sharding import Mesh, PartitionSpec as P

Z, Y, X, C = 8, 4, 4, 2
SEQ = ("x", "core")
F = 8
POS = 128
HALF = 64
NB = 4
HL = 3
HD = 128
COLS = HL * HD
DW = 1536
CAP = 32
FACTOR = 1.0 / math.sqrt(HD)
NN = (((1,), (0,)), ((), ()))
NT = (((1,), (1,)), ((), ()))
TN = (((0,), (0,)), ((), ()))
bf, f32 = jnp.bfloat16, jnp.float32
CORE, YI, ZI, XI, RANK = range(5)

ROW = np.arange(COLS)
ROWS_OF = np.zeros((8, COLS), np.int32)
ROWS_OF[0] = ROW // 6 % 2
ROWS_OF[1] = ROW // 48 % 4
ROWS_OF[2] = ROW // 192 * 4 + ROW // 12 % 4
ROWS_OF[3] = ROW % 6
LEAVE = np.zeros((8, COLS), np.int32)
LEAVE[0] = ROW // 192
SUB = ROW % 192 // 6
LEAVE[1] = ((SUB // 16 * 4 + SUB % 4) * 8 + SUB // 4 % 4 * 2) * 6 + ROW % 6


def dot(a, b, dims, **kw):
    return lax.dot_general(a, b, dims, preferred_element_type=f32, **kw)


def iota(shape, dim):
    return lax.broadcasted_iota(jnp.int32, shape, dim)


def call(body, name, outs, *ins, smem=0, scratch=(), flops=0, space=pltpu.VMEM, vmem=16):
    total = sum(math.prod(s) * jnp.dtype(d).itemsize for s, d in outs)
    total += sum(a.size * a.dtype.itemsize for a in ins)
    specs = [pl.BlockSpec(memory_space=pltpu.SMEM)] * smem
    specs += [pl.BlockSpec(memory_space=space)] * (len(ins) - smem)
    return pl.pallas_call(
        body,
        out_shape=tuple(jax.ShapeDtypeStruct(s, d) for s, d in outs),
        in_specs=specs,
        out_specs=tuple(pl.BlockSpec(memory_space=space) for _ in outs),
        scratch_shapes=list(scratch),
        compiler_params=pltpu.CompilerParams(vmem_limit_bytes=vmem << 20),
        cost_estimate=pl.CostEstimate(flops=flops, bytes_accessed=total, transcendentals=0),
        name=name,
    )(*ins)


def stack_kernel(*refs):
    out_ref, row = refs[-1], 0
    for ref in refs[:-1]:
        rows = ref.shape[0]
        out_ref[row : row + rows] = ref[...]
        row += rows


def stack(parts):
    rows = sum(p.shape[0] for p in parts)
    return call(stack_kernel, "stack", [((rows, DW), bf)], *parts)[0]


def pack_kernel(qkv_ref, out_ref):
    for d in range(F):
        r, c = d % C * HALF, d // C * COLS
        out_ref[d] = qkv_ref[:, r : r + HALF, c : c + COLS]


def compact_kernel(place, sizes, cot_ref, same_ref, other_ref):
    shape = (POS, F * CAP)
    row, col = iota(shape, 0), iota(shape, 1)
    pos = row ^ (place[CORE] * HALF)
    start = jnp.int32(0)
    picked = jnp.full(shape, -1, jnp.int32)
    for j in range(F):
        slot = col - j * CAP
        inside = (slot >= 0) & (slot < sizes[0, j])
        picked = jnp.where(inside, slot + start, picked)
        start = start + sizes[0, j]
    hot = (picked == pos).astype(f32).astype(bf)
    up = dot(hot, cot_ref[...].reshape(F * CAP, DW), NN).astype(bf)
    same_ref[...] = up[:HALF]
    other_ref[...] = up[HALF:]


def block(ref, i, b, h):
    return ref[:, i, b * 16 : (b + 1) * 16, h * HD : (h + 1) * HD].reshape(POS, HD)


def fwd_kernel(place, bias, leave_ref, qkv_ref, probs_ref, mixed_ref, raw_ref):
    row, col = iota((POS, POS), 0), iota((POS, POS), 1)
    alike = (row & 15) == (col & 15)
    offset = (col >> 4) - (row >> 4) + 7
    for h in range(HL):
        pair = jnp.full((POS, POS), -1e30, f32)
        for o in range(15):
            pair = jnp.where(alike & (offset == o), bias[place[XI] * HL + h, o], pair)
        for b in range(NB):
            q, k, v = (block(qkv_ref, i, b, h) for i in range(3))
            s = dot(q, k, NT) * FACTOR + pair
            e = jnp.exp(s - jnp.max(s, axis=-1, keepdims=True))
            p = e / jnp.sum(e, axis=-1, keepdims=True)
            probs_ref[h, b] = p
            m = dot(p.astype(bf), v, NN).astype(bf).reshape(F, 16, HD)
            raw_ref[:, b * 16 : (b + 1) * 16, h * HD : (h + 1) * HD] = m
    source = leave_ref[1:2] + (leave_ref[0:1] ^ place[CORE]) * 6
    order = (iota((COLS, COLS), 0) == source).astype(f32).astype(bf)
    mixed_ref[...] = dot(raw_ref[...].reshape(F * HALF, COLS), order, NN).astype(bf)


def gw_kernel(place, mixed_ref, u0, u1, u2, u3, mine_ref, other_ref, up_ref):
    for k, ref in enumerate((u0, u1, u2, u3)):
        chip = (place[XI] ^ k) * C
        up_ref[chip + place[CORE]] = ref[:HALF]
        up_ref[chip + 1 - place[CORE]] = ref[HALF:]
    gw = dot(mixed_ref[...], up_ref[...].reshape(F * HALF, DW), TN)
    mine_ref[...] = gw[: COLS // 2]
    other_ref[...] = gw[COLS // 2 :].astype(bf)


def score_kernel(place, rows_ref, recv_ref, probs_ref, up_ref, w0_ref, w1_ref, dm_ref, ds_ref, sums_ref):
    up = up_ref[...].reshape(F * HALF, DW)
    dm = jnp.concatenate([dot(up, w[...], NT).astype(bf) for w in (w0_ref, w1_ref)], axis=1)
    c, y, j = (rows_ref[n : n + 1] ^ place[n] for n in (CORE, YI, ZI))
    spot = ((c * Y + y) * Z + j) * 8 + rows_ref[3:4]
    spot = (iota((512, COLS), 0) == spot).astype(f32).astype(bf)
    dm = dot(dm, spot, NN)
    dm_ref[...] = dm.astype(bf).reshape(F, HALF, COLS)
    for h in range(HL):
        cols = slice(h * HD, (h + 1) * HD)
        total = jnp.zeros((F, POS), f32)
        for b in range(NB):
            d = dm_ref[:, b * 16 : (b + 1) * 16, cols].reshape(POS, HD)
            p = probs_ref[h, b]
            g = dot(d, block(recv_ref, 2, b, h), NT)
            ds = p * (g - jnp.sum(p * g, axis=-1, keepdims=True))
            total = total + jnp.sum(ds.reshape(F, 16, POS), axis=1)
            ds_ref[h, b] = ds.astype(bf)
        sums_ref[:, cols] = total


def grad_kernel(place, qkv_ref, probs_ref, dm_ref, ds_ref, *refs):
    pieces, nat_ref = refs[:F], refs[F]
    for h in range(HL):
        cols = slice(h * HD, (h + 1) * HD)
        for b in range(NB):
            rows = slice(b * 16, (b + 1) * 16)
            d = dm_ref[:, rows, cols].reshape(POS, HD)
            low = ds_ref[h, b]
            gq = dot(low, block(qkv_ref, 1, b, h), NN) * FACTOR
            gk = dot(low, block(qkv_ref, 0, b, h), TN) * FACTOR
            gv = dot(probs_ref[h, b].astype(bf), d, TN)
            for i, val in enumerate((gq, gk, gv)):
                nat_ref[:, i, rows, cols] = val.astype(bf).reshape(F, 16, HD)
    for k in range(F):
        pieces[k][...] = nat_ref[place[RANK] ^ k]


def unpack_kernel(place, *refs):
    pieces, out_ref, nat_ref = refs[:F], refs[F], refs[F + 1]
    for k in range(F):
        nat_ref[place[RANK] ^ k] = pieces[k][...]
    for d in range(F):
        r, c = d % C * HALF, d // C * COLS
        out_ref[:, r : r + HALF, c : c + COLS] = nat_ref[d]


def split(b):
    high = b.astype(bf).astype(f32)
    low = (b - high).astype(bf).astype(f32)
    return high, low


def join_kernel(mine_ref, other_ref, s0, s1, out_ref):
    gw = mine_ref[...] + other_ref[...].astype(f32)
    hot = ((iota((COLS, 128), 0) >> 4) == iota((COLS, 128), 1)).astype(f32)
    b = dot(s0[...] + s1[...], hot, NN, precision=lax.Precision.HIGHEST)
    ride = jnp.concatenate([x[:, :64] for x in split(b)], axis=1)
    for d in range(Z * Y):
        part = gw[6 * d : 6 * d + 6]
        ends = [
            jnp.concatenate([part[r + i : r + i + 1, 1152:] for i in range(3)], axis=1) for r in (0, 3)
        ]
        part = jnp.concatenate([part[:, :1152]] + ends, axis=0)
        out_ref[d] = jnp.concatenate([part, ride], axis=1).astype(bf)


def total_kernel(in_ref, sum_ref, off_ref):
    total = jnp.sum(in_ref[...].astype(f32), axis=0)
    sum_ref[:, :1152] = total[:, :1152]
    for r in range(6):
        sum_ref[r : r + 1, 1152:] = total[6 + r // 3 : 7 + r // 3, r % 3 * 384 : (r % 3 + 1) * 384]
    sum_ref[6:, 1152:] = jnp.zeros((2, 384), f32)
    sums = total[:, 1152:1216] + total[:, 1216:]
    head, lane = iota((16, 64), 0) % HL, iota((16, 64), 1)
    g, o = iota((64, 128), 0) & 7, iota((64, 128), 1)
    out = jnp.zeros((16, 128), f32)
    for f in range(F):
        row = jnp.where((lane >> 3) == head, sums[f : f + 1], 0.0)
        out = out + dot(row, (g - f + 7 == o).astype(f32), NN, precision=lax.Precision.HIGHEST)
    off_ref[...] = out


def last_kernel(place, home_ref, o0, o1, o2, o3, gw_ref, bias_ref):
    gw_ref[...] = home_ref[:6]
    row = iota((16, 128), 0) // HL
    out = jnp.zeros((16, 128), f32)
    for k, o in enumerate((o0, o1, o2, o3)):
        out = out + jnp.where(row == (place[XI] ^ k), o[...], 0.0)
    bias_ref[...] = out[:12, :15]


def hop(x, axis, k, n):
    return lax.ppermute(x, axis, [(i, i ^ k) for i in range(n)])


def per_device(qkv_time, shard_sizes, bias_time, w_out, cot_out):
    xi, yi, zi, core = (lax.axis_index(a) for a in ("x", "y", "z", "core"))
    place = jnp.stack([core, yi, zi, xi, xi * C + core]).astype(jnp.int32)

    there = [
        ((2 * c + z0) * X + x, (z0 * X + x) * X + c)
        for c in range(X)
        for z0 in range(2)
        for x in range(X)
    ]
    near = [(a, b ^ X) for a, b in there]
    cot = lax.all_to_all(cot_out[0, 0], SEQ, 0, 0, tiled=True)
    (packed,) = call(pack_kernel, "pack", [((F, 3, HALF, COLS), bf)], qkv_time[:, 0, 0])
    rows8, packed = lax.optimization_barrier((jnp.pad(w_out, ((0, 2), (0, 0))), packed))
    held = [lax.ppermute(rows8, ("z", "x"), p) for p in (there, near)]
    packed, held = lax.optimization_barrier((packed, held))
    recv = lax.all_to_all(packed, SEQ, 0, 0, tiled=True)
    held = jnp.concatenate(held)
    held = jnp.concatenate([held, hop(held, "z", 2, Z)])

    same, other = call(
        compact_kernel,
        "compact",
        [((HALF, DW), bf)] * 2,
        place,
        shard_sizes,
        cot,
        smem=2,
        flops=100_000_000,
    )
    held, same = lax.optimization_barrier((held, same))
    held = jnp.concatenate([held, hop(held, "z", 4, Z)])
    u0 = stack([same, hop(other, "core", 1, C)])
    held, _ = lax.optimization_barrier((held, u0))
    ups = [u0] + [hop(u0, "x", k, X) for k in range(1, X)]
    w1, w2 = hop(held, "y", 1, Y), hop(held, "y", 2, Y)
    far, ups[1] = lax.optimization_barrier((w1, ups[1]))
    held = stack([held, w1, w2, hop(far, "y", 2, Y)])
    held2 = hop(held, "core", 1, C)

    probs, mixed = call(
        fwd_kernel,
        "attn_fwd",
        [((HL, NB, POS, POS), f32), ((F * HALF, COLS), bf)],
        place,
        bias_time,
        LEAVE,
        recv,
        smem=2,
        scratch=[pltpu.VMEM((F, HALF, COLS), bf)],
        flops=20_000_000_000,
    )

    mine, theirs, up = call(
        gw_kernel,
        "grad_w",
        [((COLS // 2, DW), f32), ((COLS // 2, DW), bf), ((F, HALF, DW), bf)],
        place,
        mixed,
        *ups,
        smem=1,
        flops=20_000_000_000,
    )
    dm, ds, sums = call(
        score_kernel,
        "scores_bwd",
        [((F, HALF, COLS), bf), ((HL, NB, POS, POS), bf), ((F, COLS), f32)],
        place,
        ROWS_OF,
        recv,
        probs,
        up,
        held,
        held2,
        smem=1,
        flops=900_000_000,
    )
    theirs = hop(theirs, "core", 1, C)
    sums2 = hop(sums, "core", 1, C)

    pieces = call(
        grad_kernel,
        "grads",
        [((3, HALF, COLS), bf)] * F,
        place,
        recv,
        probs,
        dm,
        ds,
        smem=1,
        scratch=[pltpu.VMEM((F, 3, HALF, COLS), bf)],
        flops=150_000_000,
    )

    (msgs,) = call(join_kernel, "join", [((Z * Y, 8, 1280), bf)], mine, theirs, sums, sums2)
    msgs, *pieces = lax.optimization_barrier((msgs, *pieces))
    msgs = lax.all_to_all(msgs, ("z", "y"), 0, 0, tiled=True)
    pieces = pieces[:1] + [hop(p, SEQ, k, F) for k, p in enumerate(pieces[1:], 1)]
    msgs, *pieces[1:6] = lax.optimization_barrier((msgs, *pieces[1:6]))
    total, off = call(total_kernel, "total", [((8, DW), f32), ((16, 128), f32)], msgs)
    home = lax.ppermute(total, ("z", "x"), [(b, a) for a, b in there])
    offs = [off] + [hop(off, "x", k, X) for k in range(1, X)]
    (grad_qkv,) = call(
        unpack_kernel,
        "unpack",
        [((3, POS, DW), bf)],
        place,
        *pieces,
        smem=1,
        scratch=[pltpu.VMEM((F, 3, HALF, COLS), bf)],
    )
    grad_qkv = grad_qkv.reshape(3, 1, 1, POS, DW)
    home, grad_qkv = lax.optimization_barrier((home, grad_qkv))
    grad_w_out, grad_bias = call(
        last_kernel, "last", [((6, DW), f32), ((12, 15), f32)], place, home, *offs, smem=1
    )
    return grad_qkv, grad_bias, grad_w_out


def solution(mesh):
    grid = Mesh(mesh.devices.reshape(Z, Y, X, C), ("z", "y", "x", "core"))
    dp, every = ("z", "y"), ("z", "y", "x", "core")
    return jax.shard_map(
        per_device,
        mesh=grid,
        in_specs=(
            P(None, dp, SEQ, None, None),
            P(dp, None),
            P(),
            P(every, None),
            P(dp, SEQ, None, None, None),
        ),
        out_specs=(P(None, dp, SEQ, None, None), P(), P(every, None)),
        check_vma=False,
    )
```

```python
import math

import jax
import jax.numpy as jnp
import numpy as np
from jax import lax
from jax.experimental import pallas as pl
from jax.experimental.pallas import tpu as pltpu
from jax.sharding import Mesh, PartitionSpec as P

Z, Y, X, C = 8, 4, 4, 2
SEQ = ("x", "core")
F = 8
POS = 128
HALF = 64
NB = 4
HL = 3
HD = 128
COLS = HL * HD
DW = 1536
CAP = 32
FACTOR = 1.0 / math.sqrt(HD)
NN = (((1,), (0,)), ((), ()))
NT = (((1,), (1,)), ((), ()))
TN = (((0,), (0,)), ((), ()))
bf, f32 = jnp.bfloat16, jnp.float32
CORE, YI, ZI, XI, RANK = range(5)

ROW = np.arange(COLS)
ROWS_OF = np.zeros((8, COLS), np.int32)
ROWS_OF[0] = ROW // 6 % 2
ROWS_OF[1] = ROW // 48 % 4
ROWS_OF[2] = ROW // 192 * 4 + ROW // 12 % 4
ROWS_OF[3] = ROW % 6
LEAVE = np.zeros((8, COLS), np.int32)
LEAVE[0] = ROW // 192
SUB = ROW % 192 // 6
LEAVE[1] = ((SUB // 16 * 4 + SUB % 4) * 8 + SUB // 4 % 4 * 2) * 6 + ROW % 6


def dot(a, b, dims, **kw):
    return lax.dot_general(a, b, dims, preferred_element_type=f32, **kw)


def iota(shape, dim):
    return lax.broadcasted_iota(jnp.int32, shape, dim)


def call(body, name, outs, *ins, smem=0, scratch=(), flops=0, space=pltpu.VMEM, vmem=16):
    total = sum(math.prod(s) * jnp.dtype(d).itemsize for s, d in outs)
    total += sum(a.size * a.dtype.itemsize for a in ins)
    specs = [pl.BlockSpec(memory_space=pltpu.SMEM)] * smem
    specs += [pl.BlockSpec(memory_space=space)] * (len(ins) - smem)
    return pl.pallas_call(
        body,
        out_shape=tuple(jax.ShapeDtypeStruct(s, d) for s, d in outs),
        in_specs=specs,
        out_specs=tuple(pl.BlockSpec(memory_space=space) for _ in outs),
        scratch_shapes=list(scratch),
        compiler_params=pltpu.CompilerParams(vmem_limit_bytes=vmem << 20),
        cost_estimate=pl.CostEstimate(flops=flops, bytes_accessed=total, transcendentals=0),
        name=name,
    )(*ins)


def stack_kernel(*refs):
    out_ref, row = refs[-1], 0
    for ref in refs[:-1]:
        rows = ref.shape[0]
        out_ref[row : row + rows] = ref[...]
        row += rows


def stack(parts):
    rows = sum(p.shape[0] for p in parts)
    return call(stack_kernel, "stack", [((rows, DW), bf)], *parts)[0]


def pack_kernel(qkv_ref, out_ref):
    for d in range(F):
        r, c = d % C * HALF, d // C * COLS
        out_ref[d] = qkv_ref[:, r : r + HALF, c : c + COLS]


def compact_kernel(place, sizes, cot_ref, same_ref, other_ref):
    shape = (POS, F * CAP)
    row, col = iota(shape, 0), iota(shape, 1)
    pos = row ^ (place[CORE] * HALF)
    start = jnp.int32(0)
    picked = jnp.full(shape, -1, jnp.int32)
    for j in range(F):
        slot = col - j * CAP
        inside = (slot >= 0) & (slot < sizes[0, j])
        picked = jnp.where(inside, slot + start, picked)
        start = start + sizes[0, j]
    hot = (picked == pos).astype(f32).astype(bf)
    up = dot(hot, cot_ref[...].reshape(F * CAP, DW), NN).astype(bf)
    same_ref[...] = up[:HALF]
    other_ref[...] = up[HALF:]


def block(ref, i, b, h):
    return ref[:, i, b * 16 : (b + 1) * 16, h * HD : (h + 1) * HD].reshape(POS, HD)


def fwd_kernel(place, bias, leave_ref, qkv_ref, probs_ref, mixed_ref, raw_ref):
    row, col = iota((POS, POS), 0), iota((POS, POS), 1)
    alike = (row & 15) == (col & 15)
    offset = (col >> 4) - (row >> 4) + 7
    for h in range(HL):
        pair = jnp.full((POS, POS), -1e30, f32)
        for o in range(15):
            pair = jnp.where(alike & (offset == o), bias[place[XI] * HL + h, o], pair)
        for b in range(NB):
            q, k, v = (block(qkv_ref, i, b, h) for i in range(3))
            s = dot(q, k, NT) * FACTOR + pair
            e = jnp.exp(s - jnp.max(s, axis=-1, keepdims=True))
            p = e / jnp.sum(e, axis=-1, keepdims=True)
            probs_ref[h, b] = p
            m = dot(p.astype(bf), v, NN).astype(bf).reshape(F, 16, HD)
            raw_ref[:, b * 16 : (b + 1) * 16, h * HD : (h + 1) * HD] = m
    source = leave_ref[1:2] + (leave_ref[0:1] ^ place[CORE]) * 6
    order = (iota((COLS, COLS), 0) == source).astype(f32).astype(bf)
    mixed_ref[...] = dot(raw_ref[...].reshape(F * HALF, COLS), order, NN).astype(bf)


def gw_kernel(place, mixed_ref, u0, u1, u2, u3, mine_ref, other_ref, up_ref):
    for k, ref in enumerate((u0, u1, u2, u3)):
        chip = (place[XI] ^ k) * C
        up_ref[chip + place[CORE]] = ref[:HALF]
        up_ref[chip + 1 - place[CORE]] = ref[HALF:]
    gw = dot(mixed_ref[...], up_ref[...].reshape(F * HALF, DW), TN)
    mine_ref[...] = gw[: COLS // 2]
    other_ref[...] = gw[COLS // 2 :].astype(bf)


def score_kernel(place, rows_ref, recv_ref, probs_ref, up_ref, w0_ref, w1_ref, dm_ref, ds_ref, sums_ref):
    up = up_ref[...].reshape(F * HALF, DW)
    dm = jnp.concatenate([dot(up, w[...], NT).astype(bf) for w in (w0_ref, w1_ref)], axis=1)
    c, y, j = (rows_ref[n : n + 1] ^ place[n] for n in (CORE, YI, ZI))
    spot = ((c * Y + y) * Z + j) * 8 + rows_ref[3:4]
    spot = (iota((512, COLS), 0) == spot).astype(f32).astype(bf)
    dm = dot(dm, spot, NN)
    dm_ref[...] = dm.astype(bf).reshape(F, HALF, COLS)
    for h in range(HL):
        cols = slice(h * HD, (h + 1) * HD)
        total = jnp.zeros((F, POS), f32)
        for b in range(NB):
            d = dm_ref[:, b * 16 : (b + 1) * 16, cols].reshape(POS, HD)
            p = probs_ref[h, b]
            g = dot(d, block(recv_ref, 2, b, h), NT)
            ds = p * (g - jnp.sum(p * g, axis=-1, keepdims=True))
            total = total + jnp.sum(ds.reshape(F, 16, POS), axis=1)
            ds_ref[h, b] = ds.astype(bf)
        sums_ref[:, cols] = total


def grad_kernel(place, qkv_ref, probs_ref, dm_ref, ds_ref, *refs):
    pieces, nat_ref = refs[:F], refs[F]
    for h in range(HL):
        cols = slice(h * HD, (h + 1) * HD)
        for b in range(NB):
            rows = slice(b * 16, (b + 1) * 16)
            d = dm_ref[:, rows, cols].reshape(POS, HD)
            low = ds_ref[h, b]
            gq = dot(low, block(qkv_ref, 1, b, h), NN) * FACTOR
            gk = dot(low, block(qkv_ref, 0, b, h), TN) * FACTOR
            gv = dot(probs_ref[h, b].astype(bf), d, TN)
            for i, val in enumerate((gq, gk, gv)):
                nat_ref[:, i, rows, cols] = val.astype(bf).reshape(F, 16, HD)
    for k in range(F):
        pieces[k][...] = nat_ref[place[RANK] ^ k]


def unpack_kernel(place, *refs):
    pieces, out_ref, nat_ref = refs[:F], refs[F], refs[F + 1]
    for k in range(F):
        nat_ref[place[RANK] ^ k] = pieces[k][...]
    for d in range(F):
        r, c = d % C * HALF, d // C * COLS
        out_ref[:, r : r + HALF, c : c + COLS] = nat_ref[d]


def split(b):
    high = b.astype(bf).astype(f32)
    low = (b - high).astype(bf).astype(f32)
    return high, low


def join_kernel(mine_ref, other_ref, s0, s1, out_ref):
    gw = mine_ref[...] + other_ref[...].astype(f32)
    hot = ((iota((COLS, 128), 0) >> 4) == iota((COLS, 128), 1)).astype(f32)
    b = dot(s0[...] + s1[...], hot, NN, precision=lax.Precision.HIGHEST)
    ride = jnp.concatenate([x[:, :64] for x in split(b)], axis=1)
    for d in range(Z * Y):
        part = gw[6 * d : 6 * d + 6]
        ends = [
            jnp.concatenate([part[r + i : r + i + 1, 1152:] for i in range(3)], axis=1) for r in (0, 3)
        ]
        part = jnp.concatenate([part[:, :1152]] + ends, axis=0)
        out_ref[d] = jnp.concatenate([part, ride], axis=1).astype(bf)


def total_kernel(in_ref, sum_ref, off_ref):
    total = jnp.sum(in_ref[...].astype(f32), axis=0)
    sum_ref[:, :1152] = total[:, :1152]
    for r in range(6):
        sum_ref[r : r + 1, 1152:] = total[6 + r // 3 : 7 + r // 3, r % 3 * 384 : (r % 3 + 1) * 384]
    sum_ref[6:, 1152:] = jnp.zeros((2, 384), f32)
    sums = total[:, 1152:1216] + total[:, 1216:]
    head, lane = iota((16, 64), 0) % HL, iota((16, 64), 1)
    g, o = iota((64, 128), 0) & 7, iota((64, 128), 1)
    out = jnp.zeros((16, 128), f32)
    for f in range(F):
        row = jnp.where((lane >> 3) == head, sums[f : f + 1], 0.0)
        out = out + dot(row, (g - f + 7 == o).astype(f32), NN, precision=lax.Precision.HIGHEST)
    off_ref[...] = out


def last_kernel(place, home_ref, o0, o1, o2, o3, gw_ref, bias_ref):
    gw_ref[...] = home_ref[:6]
    row = iota((16, 128), 0) // HL
    out = jnp.zeros((16, 128), f32)
    for k, o in enumerate((o0, o1, o2, o3)):
        out = out + jnp.where(row == (place[XI] ^ k), o[...], 0.0)
    bias_ref[...] = out[:12, :15]


def hop(x, axis, k, n):
    return lax.ppermute(x, axis, [(i, i ^ k) for i in range(n)])


def per_device(qkv_time, shard_sizes, bias_time, w_out, cot_out):
    xi, yi, zi, core = (lax.axis_index(a) for a in ("x", "y", "z", "core"))
    place = jnp.stack([core, yi, zi, xi, xi * C + core]).astype(jnp.int32)

    there = [
        ((2 * c + z0) * X + x, (z0 * X + x) * X + c)
        for c in range(X)
        for z0 in range(2)
        for x in range(X)
    ]
    near = [(a, b ^ X) for a, b in there]
    cot = lax.all_to_all(cot_out[0, 0], SEQ, 0, 0, tiled=True)
    (packed,) = call(pack_kernel, "pack", [((F, 3, HALF, COLS), bf)], qkv_time[:, 0, 0])
    rows8, packed = lax.optimization_barrier((jnp.pad(w_out, ((0, 2), (0, 0))), packed))
    held = [lax.ppermute(rows8, ("z", "x"), p) for p in (there, near)]
    recv = lax.all_to_all(packed, SEQ, 0, 0, tiled=True)
    held = jnp.concatenate(held)
    held = jnp.concatenate([held, hop(held, "z", 2, Z)])

    same, other = call(
        compact_kernel,
        "compact",
        [((HALF, DW), bf)] * 2,
        place,
        shard_sizes,
        cot,
        smem=2,
        flops=100_000_000,
    )
    held, same = lax.optimization_barrier((held, same))
    held = jnp.concatenate([held, hop(held, "z", 4, Z)])
    u0 = stack([same, hop(other, "core", 1, C)])
    held, _ = lax.optimization_barrier((held, u0))
    ups = [u0] + [hop(u0, "x", k, X) for k in range(1, X)]
    w1, w2 = hop(held, "y", 1, Y), hop(held, "y", 2, Y)
    far, ups[1] = lax.optimization_barrier((w1, ups[1]))
    held = stack([held, w1, w2, hop(far, "y", 2, Y)])
    held2 = hop(held, "core", 1, C)

    probs, mixed = call(
        fwd_kernel,
        "attn_fwd",
        [((HL, NB, POS, POS), f32), ((F * HALF, COLS), bf)],
        place,
        bias_time,
        LEAVE,
        recv,
        smem=2,
        scratch=[pltpu.VMEM((F, HALF, COLS), bf)],
        flops=20_000_000_000,
    )

    mine, theirs, up = call(
        gw_kernel,
        "grad_w",
        [((COLS // 2, DW), f32), ((COLS // 2, DW), bf), ((F, HALF, DW), bf)],
        place,
        mixed,
        *ups,
        smem=1,
        flops=20_000_000_000,
    )
    dm, ds, sums = call(
        score_kernel,
        "scores_bwd",
        [((F, HALF, COLS), bf), ((HL, NB, POS, POS), bf), ((F, COLS), f32)],
        place,
        ROWS_OF,
        recv,
        probs,
        up,
        held,
        held2,
        smem=1,
        flops=900_000_000,
    )
    theirs = hop(theirs, "core", 1, C)
    sums2 = hop(sums, "core", 1, C)

    pieces = call(
        grad_kernel,
        "grads",
        [((3, HALF, COLS), bf)] * F,
        place,
        recv,
        probs,
        dm,
        ds,
        smem=1,
        scratch=[pltpu.VMEM((F, 3, HALF, COLS), bf)],
        flops=150_000_000,
    )

    (msgs,) = call(join_kernel, "join", [((Z * Y, 8, 1280), bf)], mine, theirs, sums, sums2)
    msgs, *pieces = lax.optimization_barrier((msgs, *pieces))
    msgs = lax.all_to_all(msgs, ("z", "y"), 0, 0, tiled=True)
    pieces = pieces[:1] + [hop(p, SEQ, k, F) for k, p in enumerate(pieces[1:], 1)]
    msgs, *pieces[1:6] = lax.optimization_barrier((msgs, *pieces[1:6]))
    total, off = call(total_kernel, "total", [((8, DW), f32), ((16, 128), f32)], msgs)
    home = lax.ppermute(total, ("z", "x"), [(b, a) for a, b in there])
    offs = [off] + [hop(off, "x", k, X) for k in range(1, X)]
    (grad_qkv,) = call(
        unpack_kernel,
        "unpack",
        [((3, POS, DW), bf)],
        place,
        *pieces,
        smem=1,
        scratch=[pltpu.VMEM((F, 3, HALF, COLS), bf)],
    )
    grad_qkv = grad_qkv.reshape(3, 1, 1, POS, DW)
    home, grad_qkv = lax.optimization_barrier((home, grad_qkv))
    grad_w_out, grad_bias = call(
        last_kernel, "last", [((6, DW), f32), ((12, 15), f32)], place, home, *offs, smem=1
    )
    return grad_qkv, grad_bias, grad_w_out


def solution(mesh):
    grid = Mesh(mesh.devices.reshape(Z, Y, X, C), ("z", "y", "x", "core"))
    dp, every = ("z", "y"), ("z", "y", "x", "core")
    return jax.shard_map(
        per_device,
        mesh=grid,
        in_specs=(
            P(None, dp, SEQ, None, None),
            P(dp, None),
            P(),
            P(every, None),
            P(dp, SEQ, None, None, None),
        ),
        out_specs=(P(None, dp, SEQ, None, None), P(), P(every, None)),
        check_vma=False,
    )
```

```python
import math

import jax
import jax.numpy as jnp
import numpy as np
from jax import lax
from jax.experimental import pallas as pl
from jax.experimental.pallas import tpu as pltpu
from jax.sharding import Mesh, PartitionSpec as P

Z, Y, X, C = 8, 4, 4, 2
SEQ = ("x", "core")
F = 8
POS = 128
HALF = 64
NB = 4
HL = 3
HD = 128
COLS = HL * HD
DW = 1536
CAP = 32
FACTOR = 1.0 / math.sqrt(HD)
NN = (((1,), (0,)), ((), ()))
NT = (((1,), (1,)), ((), ()))
TN = (((0,), (0,)), ((), ()))
bf, f32 = jnp.bfloat16, jnp.float32
CORE, YI, ZI, XI, RANK = range(5)

ROW = np.arange(COLS)
ROWS_OF = np.zeros((8, COLS), np.int32)
ROWS_OF[0] = ROW // 6 % 2
ROWS_OF[1] = ROW // 48 % 4
ROWS_OF[2] = ROW // 192 * 4 + ROW // 12 % 4
ROWS_OF[3] = ROW % 6
LEAVE = np.zeros((8, COLS), np.int32)
LEAVE[0] = ROW // 192
SUB = ROW % 192 // 6
LEAVE[1] = ((SUB // 16 * 4 + SUB % 4) * 8 + SUB // 4 % 4 * 2) * 6 + ROW % 6


def dot(a, b, dims, **kw):
    return lax.dot_general(a, b, dims, preferred_element_type=f32, **kw)


def iota(shape, dim):
    return lax.broadcasted_iota(jnp.int32, shape, dim)


def call(body, name, outs, *ins, smem=0, scratch=(), flops=0, space=pltpu.VMEM, vmem=16):
    total = sum(math.prod(s) * jnp.dtype(d).itemsize for s, d in outs)
    total += sum(a.size * a.dtype.itemsize for a in ins)
    specs = [pl.BlockSpec(memory_space=pltpu.SMEM)] * smem
    specs += [pl.BlockSpec(memory_space=space)] * (len(ins) - smem)
    return pl.pallas_call(
        body,
        out_shape=tuple(jax.ShapeDtypeStruct(s, d) for s, d in outs),
        in_specs=specs,
        out_specs=tuple(pl.BlockSpec(memory_space=space) for _ in outs),
        scratch_shapes=list(scratch),
        compiler_params=pltpu.CompilerParams(vmem_limit_bytes=vmem << 20),
        cost_estimate=pl.CostEstimate(flops=flops, bytes_accessed=total, transcendentals=0),
        name=name,
    )(*ins)


def stack_kernel(*refs):
    out_ref, row = refs[-1], 0
    for ref in refs[:-1]:
        rows = ref.shape[0]
        out_ref[row : row + rows] = ref[...]
        row += rows


def stack(parts):
    rows = sum(p.shape[0] for p in parts)
    return call(stack_kernel, "stack", [((rows, DW), bf)], *parts)[0]


def pack_kernel(qkv_ref, out_ref):
    for d in range(F):
        r, c = d % C * HALF, d // C * COLS
        out_ref[d] = qkv_ref[:, r : r + HALF, c : c + COLS]


def compact_kernel(place, sizes, cot_ref, same_ref, other_ref):
    shape = (POS, F * CAP)
    row, col = iota(shape, 0), iota(shape, 1)
    pos = row ^ (place[CORE] * HALF)
    start = jnp.int32(0)
    picked = jnp.full(shape, -1, jnp.int32)
    for j in range(F):
        slot = col - j * CAP
        inside = (slot >= 0) & (slot < sizes[0, j])
        picked = jnp.where(inside, slot + start, picked)
        start = start + sizes[0, j]
    hot = (picked == pos).astype(f32).astype(bf)
    up = dot(hot, cot_ref[...].reshape(F * CAP, DW), NN).astype(bf)
    same_ref[...] = up[:HALF]
    other_ref[...] = up[HALF:]


def block(ref, i, b, h):
    return ref[:, i, b * 16 : (b + 1) * 16, h * HD : (h + 1) * HD].reshape(POS, HD)


def fwd_kernel(place, bias, leave_ref, qkv_ref, probs_ref, mixed_ref, raw_ref):
    row, col = iota((POS, POS), 0), iota((POS, POS), 1)
    alike = (row & 15) == (col & 15)
    offset = (col >> 4) - (row >> 4) + 7
    for h in range(HL):
        pair = jnp.full((POS, POS), -1e30, f32)
        for o in range(15):
            pair = jnp.where(alike & (offset == o), bias[place[XI] * HL + h, o], pair)
        for b in range(NB):
            q, k, v = (block(qkv_ref, i, b, h) for i in range(3))
            s = dot(q, k, NT) * FACTOR + pair
            e = jnp.exp(s - jnp.max(s, axis=-1, keepdims=True))
            p = e / jnp.sum(e, axis=-1, keepdims=True)
            probs_ref[h, b] = p
            m = dot(p.astype(bf), v, NN).astype(bf).reshape(F, 16, HD)
            raw_ref[:, b * 16 : (b + 1) * 16, h * HD : (h + 1) * HD] = m
    source = leave_ref[1:2] + (leave_ref[0:1] ^ place[CORE]) * 6
    order = (iota((COLS, COLS), 0) == source).astype(f32).astype(bf)
    mixed_ref[...] = dot(raw_ref[...].reshape(F * HALF, COLS), order, NN).astype(bf)


def gw_kernel(place, mixed_ref, u0, u1, u2, u3, mine_ref, other_ref, up_ref):
    for k, ref in enumerate((u0, u1, u2, u3)):
        chip = (place[XI] ^ k) * C
        up_ref[chip + place[CORE]] = ref[:HALF]
        up_ref[chip + 1 - place[CORE]] = ref[HALF:]
    gw = dot(mixed_ref[...], up_ref[...].reshape(F * HALF, DW), TN)
    mine_ref[...] = gw[: COLS // 2]
    other_ref[...] = gw[COLS // 2 :].astype(bf)


def score_kernel(place, rows_ref, recv_ref, probs_ref, up_ref, w0_ref, w1_ref, dm_ref, ds_ref, sums_ref):
    up = up_ref[...].reshape(F * HALF, DW)
    dm = jnp.concatenate([dot(up, w[...], NT).astype(bf) for w in (w0_ref, w1_ref)], axis=1)
    c, y, j = (rows_ref[n : n + 1] ^ place[n] for n in (CORE, YI, ZI))
    spot = ((c * Y + y) * Z + j) * 8 + rows_ref[3:4]
    spot = (iota((512, COLS), 0) == spot).astype(f32).astype(bf)
    dm = dot(dm, spot, NN)
    dm_ref[...] = dm.astype(bf).reshape(F, HALF, COLS)
    for h in range(HL):
        cols = slice(h * HD, (h + 1) * HD)
        total = jnp.zeros((F, POS), f32)
        for b in range(NB):
            d = dm_ref[:, b * 16 : (b + 1) * 16, cols].reshape(POS, HD)
            p = probs_ref[h, b]
            g = dot(d, block(recv_ref, 2, b, h), NT)
            ds = p * (g - jnp.sum(p * g, axis=-1, keepdims=True))
            total = total + jnp.sum(ds.reshape(F, 16, POS), axis=1)
            ds_ref[h, b] = ds.astype(bf)
        sums_ref[:, cols] = total


def grad_kernel(place, qkv_ref, probs_ref, dm_ref, ds_ref, *refs):
    pieces, nat_ref = refs[:F], refs[F]
    for h in range(HL):
        cols = slice(h * HD, (h + 1) * HD)
        for b in range(NB):
            rows = slice(b * 16, (b + 1) * 16)
            d = dm_ref[:, rows, cols].reshape(POS, HD)
            low = ds_ref[h, b]
            gq = dot(low, block(qkv_ref, 1, b, h), NN) * FACTOR
            gk = dot(low, block(qkv_ref, 0, b, h), TN) * FACTOR
            gv = dot(probs_ref[h, b].astype(bf), d, TN)
            for i, val in enumerate((gq, gk, gv)):
                nat_ref[:, i, rows, cols] = val.astype(bf).reshape(F, 16, HD)
    for k in range(F):
        pieces[k][...] = nat_ref[place[RANK] ^ k]


def unpack_kernel(place, *refs):
    pieces, out_ref, nat_ref = refs[:F], refs[F], refs[F + 1]
    for k in range(F):
        nat_ref[place[RANK] ^ k] = pieces[k][...]
    for d in range(F):
        r, c = d % C * HALF, d // C * COLS
        out_ref[:, r : r + HALF, c : c + COLS] = nat_ref[d]


def split(b):
    high = b.astype(bf).astype(f32)
    low = (b - high).astype(bf).astype(f32)
    return high, low


def join_kernel(mine_ref, other_ref, s0, s1, out_ref):
    gw = mine_ref[...] + other_ref[...].astype(f32)
    hot = ((iota((COLS, 128), 0) >> 4) == iota((COLS, 128), 1)).astype(f32)
    b = dot(s0[...] + s1[...], hot, NN, precision=lax.Precision.HIGHEST)
    ride = jnp.concatenate([x[:, :64] for x in split(b)], axis=1)
    for d in range(Z * Y):
        part = gw[6 * d : 6 * d + 6]
        ends = [
            jnp.concatenate([part[r + i : r + i + 1, 1152:] for i in range(3)], axis=1) for r in (0, 3)
        ]
        part = jnp.concatenate([part[:, :1152]] + ends, axis=0)
        out_ref[d] = jnp.concatenate([part, ride], axis=1).astype(bf)


def total_kernel(in_ref, sum_ref, off_ref):
    total = jnp.sum(in_ref[...].astype(f32), axis=0)
    sum_ref[:, :1152] = total[:, :1152]
    for r in range(6):
        sum_ref[r : r + 1, 1152:] = total[6 + r // 3 : 7 + r // 3, r % 3 * 384 : (r % 3 + 1) * 384]
    sum_ref[6:, 1152:] = jnp.zeros((2, 384), f32)
    sums = total[:, 1152:1216] + total[:, 1216:]
    head, lane = iota((16, 64), 0) % HL, iota((16, 64), 1)
    g, o = iota((64, 128), 0) & 7, iota((64, 128), 1)
    out = jnp.zeros((16, 128), f32)
    for f in range(F):
        row = jnp.where((lane >> 3) == head, sums[f : f + 1], 0.0)
        out = out + dot(row, (g - f + 7 == o).astype(f32), NN, precision=lax.Precision.HIGHEST)
    off_ref[...] = out


def last_kernel(place, home_ref, o0, o1, o2, o3, gw_ref, bias_ref):
    gw_ref[...] = home_ref[:6]
    row = iota((16, 128), 0) // HL
    out = jnp.zeros((16, 128), f32)
    for k, o in enumerate((o0, o1, o2, o3)):
        out = out + jnp.where(row == (place[XI] ^ k), o[...], 0.0)
    bias_ref[...] = out[:12, :15]


def hop(x, axis, k, n):
    return lax.ppermute(x, axis, [(i, i ^ k) for i in range(n)])


def per_device(qkv_time, shard_sizes, bias_time, w_out, cot_out):
    xi, yi, zi, core = (lax.axis_index(a) for a in ("x", "y", "z", "core"))
    place = jnp.stack([core, yi, zi, xi, xi * C + core]).astype(jnp.int32)

    there = [
        ((2 * c + z0) * X + x, (z0 * X + x) * X + c)
        for c in range(X)
        for z0 in range(2)
        for x in range(X)
    ]
    near = [(a, b ^ X) for a, b in there]
    cot = lax.all_to_all(cot_out[0, 0], SEQ, 0, 0, tiled=True)
    (packed,) = call(pack_kernel, "pack", [((F, 3, HALF, COLS), bf)], qkv_time[:, 0, 0])
    rows8 = jnp.pad(w_out, ((0, 2), (0, 0)))
    held = [lax.ppermute(rows8, ("z", "x"), p) for p in (there, near)]
    recv = lax.all_to_all(packed, SEQ, 0, 0, tiled=True)
    held = jnp.concatenate(held)
    held = jnp.concatenate([held, hop(held, "z", 2, Z)])

    same, other = call(
        compact_kernel,
        "compact",
        [((HALF, DW), bf)] * 2,
        place,
        shard_sizes,
        cot,
        smem=2,
        flops=100_000_000,
    )
    held, same = lax.optimization_barrier((held, same))
    held = jnp.concatenate([held, hop(held, "z", 4, Z)])
    u0 = stack([same, hop(other, "core", 1, C)])
    held, _ = lax.optimization_barrier((held, u0))
    ups = [u0] + [hop(u0, "x", k, X) for k in range(1, X)]
    w1, w2 = hop(held, "y", 1, Y), hop(held, "y", 2, Y)
    far, ups[1] = lax.optimization_barrier((w1, ups[1]))
    held = stack([held, w1, w2, hop(far, "y", 2, Y)])
    held2 = hop(held, "core", 1, C)

    probs, mixed = call(
        fwd_kernel,
        "attn_fwd",
        [((HL, NB, POS, POS), f32), ((F * HALF, COLS), bf)],
        place,
        bias_time,
        LEAVE,
        recv,
        smem=2,
        scratch=[pltpu.VMEM((F, HALF, COLS), bf)],
        flops=20_000_000_000,
    )

    mine, theirs, up = call(
        gw_kernel,
        "grad_w",
        [((COLS // 2, DW), f32), ((COLS // 2, DW), bf), ((F, HALF, DW), bf)],
        place,
        mixed,
        *ups,
        smem=1,
        flops=20_000_000_000,
    )
    dm, ds, sums = call(
        score_kernel,
        "scores_bwd",
        [((F, HALF, COLS), bf), ((HL, NB, POS, POS), bf), ((F, COLS), f32)],
        place,
        ROWS_OF,
        recv,
        probs,
        up,
        held,
        held2,
        smem=1,
        flops=900_000_000,
    )
    theirs = hop(theirs, "core", 1, C)
    sums2 = hop(sums, "core", 1, C)

    pieces = call(
        grad_kernel,
        "grads",
        [((3, HALF, COLS), bf)] * F,
        place,
        recv,
        probs,
        dm,
        ds,
        smem=1,
        scratch=[pltpu.VMEM((F, 3, HALF, COLS), bf)],
        flops=150_000_000,
    )

    (msgs,) = call(join_kernel, "join", [((Z * Y, 8, 1280), bf)], mine, theirs, sums, sums2)
    msgs, *pieces = lax.optimization_barrier((msgs, *pieces))
    msgs = lax.all_to_all(msgs, ("z", "y"), 0, 0, tiled=True)
    pieces = pieces[:1] + [hop(p, SEQ, k, F) for k, p in enumerate(pieces[1:], 1)]
    msgs, *pieces[1:6] = lax.optimization_barrier((msgs, *pieces[1:6]))
    total, off = call(total_kernel, "total", [((8, DW), f32), ((16, 128), f32)], msgs)
    home = lax.ppermute(total, ("z", "x"), [(b, a) for a, b in there])
    offs = [off] + [hop(off, "x", k, X) for k in range(1, X)]
    (grad_qkv,) = call(
        unpack_kernel,
        "unpack",
        [((3, POS, DW), bf)],
        place,
        *pieces,
        smem=1,
        scratch=[pltpu.VMEM((F, 3, HALF, COLS), bf)],
    )
    grad_qkv = grad_qkv.reshape(3, 1, 1, POS, DW)
    home, grad_qkv = lax.optimization_barrier((home, grad_qkv))
    grad_w_out, grad_bias = call(
        last_kernel, "last", [((6, DW), f32), ((12, 15), f32)], place, home, *offs, smem=1
    )
    return grad_qkv, grad_bias, grad_w_out


def solution(mesh):
    grid = Mesh(mesh.devices.reshape(Z, Y, X, C), ("z", "y", "x", "core"))
    dp, every = ("z", "y"), ("z", "y", "x", "core")
    return jax.shard_map(
        per_device,
        mesh=grid,
        in_specs=(
            P(None, dp, SEQ, None, None),
            P(dp, None),
            P(),
            P(every, None),
            P(dp, SEQ, None, None, None),
        ),
        out_specs=(P(None, dp, SEQ, None, None), P(), P(every, None)),
        check_vma=False,
    )
```

```python
import math

import jax
import jax.numpy as jnp
import numpy as np
from jax import lax
from jax.experimental import pallas as pl
from jax.experimental.pallas import tpu as pltpu
from jax.sharding import Mesh, PartitionSpec as P

Z, Y, X, C = 8, 4, 4, 2
SEQ = ("x", "core")
F = 8
POS = 128
HALF = 64
NB = 4
HL = 3
HD = 128
COLS = HL * HD
DW = 1536
CAP = 32
FACTOR = 1.0 / math.sqrt(HD)
NN = (((1,), (0,)), ((), ()))
NT = (((1,), (1,)), ((), ()))
TN = (((0,), (0,)), ((), ()))
bf, f32 = jnp.bfloat16, jnp.float32
CORE, YI, ZI, XI, RANK = range(5)

ROW = np.arange(COLS)
ROWS_OF = np.zeros((8, COLS), np.int32)
ROWS_OF[0] = ROW // 6 % 2
ROWS_OF[1] = ROW // 48 % 4
ROWS_OF[2] = ROW // 192 * 4 + ROW // 12 % 4
ROWS_OF[3] = ROW % 6
LEAVE = np.zeros((8, COLS), np.int32)
LEAVE[0] = ROW // 192
SUB = ROW % 192 // 6
LEAVE[1] = ((SUB // 16 * 4 + SUB % 4) * 8 + SUB // 4 % 4 * 2) * 6 + ROW % 6


def dot(a, b, dims, **kw):
    return lax.dot_general(a, b, dims, preferred_element_type=f32, **kw)


def iota(shape, dim):
    return lax.broadcasted_iota(jnp.int32, shape, dim)


def call(body, name, outs, *ins, smem=0, scratch=(), flops=0, space=pltpu.VMEM, vmem=16):
    total = sum(math.prod(s) * jnp.dtype(d).itemsize for s, d in outs)
    total += sum(a.size * a.dtype.itemsize for a in ins)
    specs = [pl.BlockSpec(memory_space=pltpu.SMEM)] * smem
    specs += [pl.BlockSpec(memory_space=space)] * (len(ins) - smem)
    return pl.pallas_call(
        body,
        out_shape=tuple(jax.ShapeDtypeStruct(s, d) for s, d in outs),
        in_specs=specs,
        out_specs=tuple(pl.BlockSpec(memory_space=space) for _ in outs),
        scratch_shapes=list(scratch),
        compiler_params=pltpu.CompilerParams(vmem_limit_bytes=vmem << 20),
        cost_estimate=pl.CostEstimate(flops=flops, bytes_accessed=total, transcendentals=0),
        name=name,
    )(*ins)


def stack_kernel(*refs):
    out_ref, row = refs[-1], 0
    for ref in refs[:-1]:
        rows = ref.shape[0]
        out_ref[row : row + rows] = ref[...]
        row += rows


def stack(parts):
    rows = sum(p.shape[0] for p in parts)
    return call(stack_kernel, "stack", [((rows, DW), bf)], *parts)[0]


def pack_kernel(qkv_ref, out_ref):
    for d in range(F):
        r, c = d % C * HALF, d // C * COLS
        out_ref[d] = qkv_ref[:, r : r + HALF, c : c + COLS]


def compact_kernel(place, sizes, cot_ref, same_ref, other_ref):
    shape = (POS, F * CAP)
    row, col = iota(shape, 0), iota(shape, 1)
    pos = row ^ (place[CORE] * HALF)
    start = jnp.int32(0)
    picked = jnp.full(shape, -1, jnp.int32)
    for j in range(F):
        slot = col - j * CAP
        inside = (slot >= 0) & (slot < sizes[0, j])
        picked = jnp.where(inside, slot + start, picked)
        start = start + sizes[0, j]
    hot = (picked == pos).astype(f32).astype(bf)
    up = dot(hot, cot_ref[...].reshape(F * CAP, DW), NN).astype(bf)
    same_ref[...] = up[:HALF]
    other_ref[...] = up[HALF:]


def block(ref, i, b, h):
    return ref[:, i, b * 16 : (b + 1) * 16, h * HD : (h + 1) * HD].reshape(POS, HD)


def fwd_kernel(place, bias, leave_ref, qkv_ref, probs_ref, mixed_ref, raw_ref):
    row, col = iota((POS, POS), 0), iota((POS, POS), 1)
    alike = (row & 15) == (col & 15)
    offset = (col >> 4) - (row >> 4) + 7
    for h in range(HL):
        pair = jnp.full((POS, POS), -1e30, f32)
        for o in range(15):
            pair = jnp.where(alike & (offset == o), bias[place[XI] * HL + h, o], pair)
        for b in range(NB):
            q, k, v = (block(qkv_ref, i, b, h) for i in range(3))
            s = dot(q, k, NT) * FACTOR + pair
            e = jnp.exp(s - jnp.max(s, axis=-1, keepdims=True))
            p = e / jnp.sum(e, axis=-1, keepdims=True)
            probs_ref[h, b] = p
            m = dot(p.astype(bf), v, NN).astype(bf).reshape(F, 16, HD)
            raw_ref[:, b * 16 : (b + 1) * 16, h * HD : (h + 1) * HD] = m
    source = leave_ref[1:2] + (leave_ref[0:1] ^ place[CORE]) * 6
    order = (iota((COLS, COLS), 0) == source).astype(f32).astype(bf)
    mixed_ref[...] = dot(raw_ref[...].reshape(F * HALF, COLS), order, NN).astype(bf)


def gw_kernel(place, mixed_ref, u0, u1, u2, u3, mine_ref, other_ref, up_ref):
    for k, ref in enumerate((u0, u1, u2, u3)):
        chip = (place[XI] ^ k) * C
        up_ref[chip + place[CORE]] = ref[:HALF]
        up_ref[chip + 1 - place[CORE]] = ref[HALF:]
    gw = dot(mixed_ref[...], up_ref[...].reshape(F * HALF, DW), TN)
    mine_ref[...] = gw[: COLS // 2]
    other_ref[...] = gw[COLS // 2 :].astype(bf)


def score_kernel(place, rows_ref, recv_ref, probs_ref, up_ref, w0_ref, w1_ref, dm_ref, ds_ref, sums_ref):
    up = up_ref[...].reshape(F * HALF, DW)
    dm = jnp.concatenate([dot(up, w[...], NT).astype(bf) for w in (w0_ref, w1_ref)], axis=1)
    c, y, j = (rows_ref[n : n + 1] ^ place[n] for n in (CORE, YI, ZI))
    spot = ((c * Y + y) * Z + j) * 8 + rows_ref[3:4]
    spot = (iota((512, COLS), 0) == spot).astype(f32).astype(bf)
    dm = dot(dm, spot, NN)
    dm_ref[...] = dm.astype(bf).reshape(F, HALF, COLS)
    for h in range(HL):
        cols = slice(h * HD, (h + 1) * HD)
        total = jnp.zeros((F, POS), f32)
        for b in range(NB):
            d = dm_ref[:, b * 16 : (b + 1) * 16, cols].reshape(POS, HD)
            p = probs_ref[h, b]
            g = dot(d, block(recv_ref, 2, b, h), NT)
            ds = p * (g - jnp.sum(p * g, axis=-1, keepdims=True))
            total = total + jnp.sum(ds.reshape(F, 16, POS), axis=1)
            ds_ref[h, b] = ds.astype(bf)
        sums_ref[:, cols] = total


def grad_kernel(place, qkv_ref, probs_ref, dm_ref, ds_ref, *refs):
    pieces, nat_ref = refs[:F], refs[F]
    for h in range(HL):
        cols = slice(h * HD, (h + 1) * HD)
        for b in range(NB):
            rows = slice(b * 16, (b + 1) * 16)
            d = dm_ref[:, rows, cols].reshape(POS, HD)
            low = ds_ref[h, b]
            gq = dot(low, block(qkv_ref, 1, b, h), NN) * FACTOR
            gk = dot(low, block(qkv_ref, 0, b, h), TN) * FACTOR
            gv = dot(probs_ref[h, b].astype(bf), d, TN)
            for i, val in enumerate((gq, gk, gv)):
                nat_ref[:, i, rows, cols] = val.astype(bf).reshape(F, 16, HD)
    for k in range(F):
        pieces[k][...] = nat_ref[place[RANK] ^ k]


def unpack_kernel(place, *refs):
    pieces, out_ref, nat_ref = refs[:F], refs[F], refs[F + 1]
    for k in range(F):
        nat_ref[place[RANK] ^ k] = pieces[k][...]
    for d in range(F):
        r, c = d % C * HALF, d // C * COLS
        out_ref[:, r : r + HALF, c : c + COLS] = nat_ref[d]


def split(b):
    high = b.astype(bf).astype(f32)
    low = (b - high).astype(bf).astype(f32)
    return high, low


def join_kernel(mine_ref, other_ref, s0, s1, out_ref):
    gw = mine_ref[...] + other_ref[...].astype(f32)
    hot = ((iota((COLS, 128), 0) >> 4) == iota((COLS, 128), 1)).astype(f32)
    b = dot(s0[...] + s1[...], hot, NN, precision=lax.Precision.HIGHEST)
    ride = jnp.concatenate([x[:, :64] for x in split(b)], axis=1)
    for d in range(Z * Y):
        part = gw[6 * d : 6 * d + 6]
        ends = [
            jnp.concatenate([part[r + i : r + i + 1, 1152:] for i in range(3)], axis=1) for r in (0, 3)
        ]
        part = jnp.concatenate([part[:, :1152]] + ends, axis=0)
        out_ref[d] = jnp.concatenate([part, ride], axis=1).astype(bf)


def total_kernel(in_ref, sum_ref, off_ref):
    total = jnp.sum(in_ref[...].astype(f32), axis=0)
    sum_ref[:, :1152] = total[:, :1152]
    for r in range(6):
        sum_ref[r : r + 1, 1152:] = total[6 + r // 3 : 7 + r // 3, r % 3 * 384 : (r % 3 + 1) * 384]
    sum_ref[6:, 1152:] = jnp.zeros((2, 384), f32)
    sums = total[:, 1152:1216] + total[:, 1216:]
    head, lane = iota((16, 64), 0) % HL, iota((16, 64), 1)
    g, o = iota((64, 128), 0) & 7, iota((64, 128), 1)
    out = jnp.zeros((16, 128), f32)
    for f in range(F):
        row = jnp.where((lane >> 3) == head, sums[f : f + 1], 0.0)
        out = out + dot(row, (g - f + 7 == o).astype(f32), NN, precision=lax.Precision.HIGHEST)
    off_ref[...] = out


def last_kernel(place, home_ref, o0, o1, o2, o3, gw_ref, bias_ref):
    gw_ref[...] = home_ref[:6]
    row = iota((16, 128), 0) // HL
    out = jnp.zeros((16, 128), f32)
    for k, o in enumerate((o0, o1, o2, o3)):
        out = out + jnp.where(row == (place[XI] ^ k), o[...], 0.0)
    bias_ref[...] = out[:12, :15]


def hop(x, axis, k, n):
    return lax.ppermute(x, axis, [(i, i ^ k) for i in range(n)])


def per_device(qkv_time, shard_sizes, bias_time, w_out, cot_out):
    xi, yi, zi, core = (lax.axis_index(a) for a in ("x", "y", "z", "core"))
    place = jnp.stack([core, yi, zi, xi, xi * C + core]).astype(jnp.int32)

    there = [
        ((2 * c + z0) * X + x, (z0 * X + x) * X + c)
        for c in range(X)
        for z0 in range(2)
        for x in range(X)
    ]
    near = [(a, b ^ X) for a, b in there]
    cot = lax.all_to_all(cot_out[0, 0], SEQ, 0, 0, tiled=True)
    (packed,) = call(pack_kernel, "pack", [((F, 3, HALF, COLS), bf)], qkv_time[:, 0, 0])
    rows8 = jnp.pad(w_out, ((0, 2), (0, 0)))
    held = [lax.ppermute(rows8, ("z", "x"), p) for p in (there, near)]
    recv = lax.all_to_all(packed, SEQ, 0, 0, tiled=True)
    held = jnp.concatenate(held)
    held = jnp.concatenate([held, hop(held, "z", 2, Z)])

    same, other = call(
        compact_kernel,
        "compact",
        [((HALF, DW), bf)] * 2,
        place,
        shard_sizes,
        cot,
        smem=2,
        flops=100_000_000,
    )
    held, same = lax.optimization_barrier((held, same))
    held = jnp.concatenate([held, hop(held, "z", 4, Z)])
    u0 = stack([same, hop(other, "core", 1, C)])
    held, _ = lax.optimization_barrier((held, u0))
    ups = [u0] + [hop(u0, "x", k, X) for k in range(1, X)]
    w1, w2 = hop(held, "y", 1, Y), hop(held, "y", 2, Y)
    far, ups[1] = lax.optimization_barrier((w1, ups[1]))
    held = stack([held, w1, w2, hop(far, "y", 2, Y)])
    held2 = hop(held, "core", 1, C)

    probs, mixed = call(
        fwd_kernel,
        "attn_fwd",
        [((HL, NB, POS, POS), f32), ((F * HALF, COLS), bf)],
        place,
        bias_time,
        LEAVE,
        recv,
        smem=2,
        scratch=[pltpu.VMEM((F, HALF, COLS), bf)],
        flops=20_000_000_000,
    )

    mine, theirs, up = call(
        gw_kernel,
        "grad_w",
        [((COLS // 2, DW), f32), ((COLS // 2, DW), bf), ((F, HALF, DW), bf)],
        place,
        mixed,
        *ups,
        smem=1,
        flops=20_000_000_000,
    )
    dm, ds, sums = call(
        score_kernel,
        "scores_bwd",
        [((F, HALF, COLS), bf), ((HL, NB, POS, POS), bf), ((F, COLS), f32)],
        place,
        ROWS_OF,
        recv,
        probs,
        up,
        held,
        held2,
        smem=1,
        flops=900_000_000,
    )
    theirs = hop(theirs, "core", 1, C)
    sums2 = hop(sums, "core", 1, C)

    pieces = call(
        grad_kernel,
        "grads",
        [((3, HALF, COLS), bf)] * F,
        place,
        recv,
        probs,
        dm,
        ds,
        smem=1,
        scratch=[pltpu.VMEM((F, 3, HALF, COLS), bf)],
        flops=150_000_000,
    )

    (msgs,) = call(join_kernel, "join", [((Z * Y, 8, 1280), bf)], mine, theirs, sums, sums2)
    msgs, *pieces = lax.optimization_barrier((msgs, *pieces))
    msgs = lax.all_to_all(msgs, ("z", "y"), 0, 0, tiled=True)
    pieces = pieces[:1] + [hop(p, SEQ, k, F) for k, p in enumerate(pieces[1:], 1)]
    msgs, *pieces[1:5] = lax.optimization_barrier((msgs, *pieces[1:5]))
    total, off = call(total_kernel, "total", [((8, DW), f32), ((16, 128), f32)], msgs)
    home = lax.ppermute(total, ("z", "x"), [(b, a) for a, b in there])
    offs = [off] + [hop(off, "x", k, X) for k in range(1, X)]
    (grad_qkv,) = call(
        unpack_kernel,
        "unpack",
        [((3, POS, DW), bf)],
        place,
        *pieces,
        smem=1,
        scratch=[pltpu.VMEM((F, 3, HALF, COLS), bf)],
    )
    grad_qkv = grad_qkv.reshape(3, 1, 1, POS, DW)
    home, grad_qkv = lax.optimization_barrier((home, grad_qkv))
    grad_w_out, grad_bias = call(
        last_kernel, "last", [((6, DW), f32), ((12, 15), f32)], place, home, *offs, smem=1
    )
    return grad_qkv, grad_bias, grad_w_out


def solution(mesh):
    grid = Mesh(mesh.devices.reshape(Z, Y, X, C), ("z", "y", "x", "core"))
    dp, every = ("z", "y"), ("z", "y", "x", "core")
    return jax.shard_map(
        per_device,
        mesh=grid,
        in_specs=(
            P(None, dp, SEQ, None, None),
            P(dp, None),
            P(),
            P(every, None),
            P(dp, SEQ, None, None, None),
        ),
        out_specs=(P(None, dp, SEQ, None, None), P(), P(every, None)),
        check_vma=False,
    )
```
